1024 devices in a mesh: gx: 64 (over y, x, core), gy: 16 (over z).
Axes of the slice: x: 4, y: 8, z: 16, core: 2. Of those that a mesh axis runs over, the one named last changes fastest.
Arguments:
- trial: bfloat16 [256, 64, 8, 4, 256], P('gx', 'gy'), may hold values from -6 to 6
- positions: float32 [3, 256, 64, 8], P(None, 'gx', 'gy'), as said below
- pair_atoms: int32 [64, 16, 2, 512], P('gx', 'gy'), may hold values from 0 to 127, as said below
- pair_owner: int32 [64, 16, 512], P('gx', 'gy'), may hold values from 0 to 1023, as said below
- pair_image: int32 [64, 16, 3, 512], P('gx', 'gy'), may hold values from -1 to 1, as said below
- pair_count: int32 [64, 16], P('gx', 'gy'), may hold values from 128 to 512, as said below
Outputs:
- product: float32 [256, 64, 8, 4, 256], P('gx', 'gy')
The draws below stay inside these ranges and needn't reach their ends.
Inputs may be any that keep to these rules, and one draw needn't show every extreme that they name: `pair_atoms`: row 0 holds atom i and row 1 atom j, each as index (x * 4 + y) * 8 + z of its lattice place inside its owner's block of 4 x 4 x 8 sites; atom i belongs to the device holding the list. The lattice sites of i and j differ by at most one step along each direction, counted periodically over the 256 x 64 x 8 sites, and not by zero along all three. Padding slots hold pairs of the same form. `pair_owner`: the owner of atom j is the listing device or one of its eight neighbours in the periodic grid of devices. `pair_image`: the number of whole box periods added to atom j's coordinates so that it lies beside atom i. `pair_count`: slots at or beyond a device's count are padding; some device's list is full. `positions`: each coordinate is 1.6 times the lattice index plus a displacement of at most 0.24.
All inputs are finite; a program needn't handle non-finite values.
Results may differ from the reference program's by a relative error of at most 0.0027.
Values may be sent and summed in bfloat16 or wider, within the bound.
No kernel may reach another device: no remote copies, remote signals or barrier semaphores. Data moves between devices by JAX's collectives and lax.ppermute only.
A program may use at most 32 MiB of HBM per device.

```python
import jax
import jax.numpy as jnp
from jax import lax

NV = 256
LX = 4
LY = 4
LZ = 8
SLOTS = 4
PAIRS = 512
NX = 256
NY = 64
N_GX = 64
N_GY = 16


LATTICE_STEP = 1.6


def pair_tables(key):
    key_atoms, key_codes, key_counts, key_full = jax.random.split(key, 4)
    per_device = LX * LY * LZ
    slot_total = SLOTS * per_device
    shape = (N_GX, N_GY, slot_total)
    first_atom = jax.random.randint(key_atoms, shape, 0, per_device)
    codes = jax.random.randint(key_codes, shape, 0, 26)
    codes = codes + (codes >= 13).astype(codes.dtype)
    step_x = codes // 9 - 1
    step_y = codes // 3 % 3 - 1
    step_z = codes % 3 - 1
    first_x = first_atom // (LY * LZ)
    first_y = first_atom // LZ % LY
    first_z = first_atom % LZ
    device_x = jnp.arange(N_GX)[:, None, None]
    device_y = jnp.arange(N_GY)[None, :, None]
    reach_x = device_x * LX + first_x + step_x
    reach_y = device_y * LY + first_y + step_y
    reach_z = first_z + step_z
    image_x = reach_x // (LX * N_GX)
    image_y = reach_y // (LY * N_GY)
    image_z = reach_z // LZ
    place_x = reach_x - image_x * (LX * N_GX)
    place_y = reach_y - image_y * (LY * N_GY)
    place_z = reach_z - image_z * LZ
    owner_ids = place_x // LX * N_GY + place_y // LY
    second_atom = (place_x % LX * LY + place_y % LY) * LZ + place_z
    atoms = jnp.stack([first_atom, second_atom], axis=2).astype(jnp.int32)
    images = jnp.stack([image_x, image_y, image_z], axis=2).astype(jnp.int32)
    totals = jax.random.randint(key_counts, (N_GX * N_GY,), slot_total // 4, slot_total + 1)
    fullest = jax.random.randint(key_full, (), 0, N_GX * N_GY)
    totals = jnp.where(jnp.arange(N_GX * N_GY) == fullest, slot_total, totals)
    return (atoms, owner_ids.astype(jnp.int32), images, totals.reshape(N_GX, N_GY).astype(jnp.int32))


def draw_pair_atoms(key, part):
    tables = pair_tables(key)
    key = jax.random.fold_in(key, 1)
    return tables[0]


def draw_pair_owner(key, part):
    tables = pair_tables(key)
    key = jax.random.fold_in(key, 2)
    return tables[1]


def draw_pair_image(key, part):
    tables = pair_tables(key)
    key = jax.random.fold_in(key, 3)
    return tables[2]


def draw_pair_count(key, part):
    tables = pair_tables(key)
    key = jax.random.fold_in(key, 4)
    return tables[3]


def draw_positions(key, part):
    key = jax.random.fold_in(key, 5)
    shape = (3, NX, NY, LZ)
    jitter = 0.15 * jnp.clip(0.6 * jax.random.normal(key, shape, jnp.float32), -1.0, 1.0)
    index_x = jnp.broadcast_to(jnp.arange(NX, dtype=jnp.float32)[:, None, None], (NX, NY, LZ))
    index_y = jnp.broadcast_to(jnp.arange(NY, dtype=jnp.float32)[None, :, None], (NX, NY, LZ))
    index_z = jnp.broadcast_to(jnp.arange(LZ, dtype=jnp.float32)[None, None, :], (NX, NY, LZ))
    lattice = jnp.stack([index_x, index_y, index_z])
    return ((lattice + jitter) * LATTICE_STEP).astype(jnp.float32)


def level_of(rng, shape, shards, smallest, largest):
    def one(axis_at, shards_of):
        steps = jax.random.uniform(jax.random.fold_in(jax.random.fold_in(rng, 6), axis_at), (shards_of,), jnp.float32, smallest / len(shards), largest / len(shards))
        return jnp.repeat(jnp.exp(steps), shape[axis_at] // shards_of).reshape((-1,) + (1,) * (len(shape) - axis_at - 1))

    loudness = one(*shards[0])
    for cut in shards[1:]:
        loudness = loudness * one(*cut)
    return loudness


def centred(key, shape, width, limit, shards=(), kind=jnp.bfloat16):
    values = width * jax.random.normal(key, shape, jnp.float32)
    if shards:
        values = values * level_of(key, shape, shards, -0.22, 0.18)
    return jnp.clip(values, -limit, limit).astype(kind)


def setup_inputs(seed: int = 0) -> dict:
    streams_of = jax.random.split(jax.random.key(seed), 7)
    trial = centred(streams_of[0], (NX, NY, LZ, 4, NV), 1.0, 6.0, ((0, 64), (1, 16)))
    positions = draw_positions(jax.random.fold_in(streams_of[6], 71), 0)
    pair_atoms = draw_pair_atoms(jax.random.fold_in(streams_of[6], 71), 0)
    pair_owner = draw_pair_owner(jax.random.fold_in(streams_of[6], 71), 0)
    pair_image = draw_pair_image(jax.random.fold_in(streams_of[6], 71), 0)
    pair_count = draw_pair_count(jax.random.fold_in(streams_of[6], 71), 0)
    return {"trial": trial, "positions": positions, "pair_atoms": pair_atoms, "pair_owner": pair_owner, "pair_image": pair_image, "pair_count": pair_count}


ONSITE_S = -0.22
ONSITE_P = 0.27
HOP_SS = -0.37
HOP_SP = 0.35
HOP_PPS = 0.4
HOP_PPP = -0.114
BOND_LENGTH = 1.536
LATTICE_STEP = 1.6

def hopping(displacement):
    distance = jnp.sqrt(lax.optimization_barrier(jnp.sum(displacement * displacement, axis=0)))
    cosines = displacement / distance
    radial = (BOND_LENGTH / distance) ** 2 * jnp.exp(1.0 - distance / BOND_LENGTH)
    upper_row = [HOP_SS * radial] + [HOP_SP * radial * cosines[a] for a in range(3)]
    block_rows = [jnp.stack(upper_row)]
    for a in range(3):
        entries = [-HOP_SP * radial * cosines[a]]
        for b in range(3):
            diagonal_part = HOP_PPP if a == b else 0.0
            entries.append(((HOP_PPS - HOP_PPP) * cosines[a] * cosines[b] + diagonal_part) * radial)
        block_rows.append(jnp.stack(entries))
    return jnp.stack(block_rows)

def reference(trial, positions, pair_atoms, pair_owner, pair_image, pair_count):
    site_count = NX * NY * LZ
    ghost_total = (LX + 2) * (LY + 2) * LZ
    flat_trial = trial.reshape(site_count, 4, NV)
    flat_pos = positions.reshape(3, site_count)
    period = jnp.array([LATTICE_STEP * NX, LATTICE_STEP * NY, LATTICE_STEP * LZ], jnp.float32)
    onsite = jnp.array([ONSITE_S, ONSITE_P, ONSITE_P, ONSITE_P], jnp.float32)
    column_ids = jnp.arange(N_GY, dtype=jnp.int32)[:, None]
    slot_index = jnp.arange(PAIRS, dtype=jnp.int32)[None, :]
    cell_x = jnp.arange(LX + 2, dtype=jnp.int32) - 1
    cell_y = jnp.arange(LY + 2, dtype=jnp.int32) - 1
    cell_z = jnp.arange(LZ, dtype=jnp.int32)

    def site_index(device_x, device_y, local_index):
        place_x = device_x * LX + local_index // (LY * LZ)
        place_y = device_y * LY + local_index // LZ % LY
        return ((place_x * NY + place_y) * LZ + local_index % LZ).astype(jnp.int32)

    def one_row(accum, inputs):
        row_x, atom_ids, owner_ids, image_shift, pair_total = inputs
        first_atom = site_index(row_x, column_ids, atom_ids[:, 0])
        second_atom = site_index(owner_ids // N_GY, owner_ids % N_GY, atom_ids[:, 1])
        shifts = jnp.transpose(image_shift, (1, 0, 2)).astype(jnp.float32)
        displacement = flat_pos[:, second_atom] + shifts * period[:, None, None] - flat_pos[:, first_atom]
        live_mask = (slot_index < pair_total[:, None]).astype(jnp.float32)
        blocks = (hopping(displacement) * live_mask).astype(jnp.bfloat16)
        blocks = lax.optimization_barrier(blocks).astype(jnp.float32)
        blocks = blocks.reshape(4, 4, N_GY * PAIRS)
        step_x = (owner_ids // N_GY - row_x + 1) % N_GX - 1
        step_y = (owner_ids % N_GY - column_ids + 1) % N_GY - 1
        local_j = atom_ids[:, 1]
        ghost_j = ((local_j // (LY * LZ) + step_x * LX + 1) * (LY + 2) + local_j // LZ % LY + step_y * LY + 1) * LZ + local_j % LZ
        ghost_flat = (column_ids * ghost_total + ghost_j).astype(jnp.int32).reshape(-1)
        remote = (owner_ids != row_x * N_GY + column_ids).astype(jnp.float32).reshape(-1)[:, None, None]
        first_atom = first_atom.reshape(-1)
        second_atom = second_atom.reshape(-1)
        upper_terms = jnp.einsum('abp,pbv->pav', blocks, flat_trial[second_atom].astype(jnp.float32), precision=lax.Precision.HIGHEST)
        lower_terms = jnp.einsum('bap,pbv->pav', blocks, flat_trial[first_atom].astype(jnp.float32), precision=lax.Precision.HIGHEST)
        accum = accum.at[first_atom].add(upper_terms).at[second_atom].add(lower_terms * (1.0 - remote))
        buffer = jnp.zeros((N_GY * ghost_total, 4, NV), jnp.float32).at[ghost_flat].add(lower_terms * remote)
        buffer = lax.optimization_barrier(buffer.astype(jnp.bfloat16)).astype(jnp.float32)
        global_x = (row_x * LX + cell_x) % NX
        global_y = (jnp.arange(N_GY, dtype=jnp.int32)[:, None] * LY + cell_y[None, :]) % NY
        sites = ((global_x[None, :, None, None] * NY + global_y[:, None, :, None]) * LZ + cell_z[None, None, None, :]).astype(jnp.int32).reshape(-1)
        accum = accum.at[sites].add(buffer)
        return (accum, None)
    begin = onsite[None, :, None] * flat_trial.astype(jnp.float32)
    rows_in = (jnp.arange(N_GX, dtype=jnp.int32), pair_atoms, pair_owner, pair_image, pair_count)
    accum = lax.scan(one_row, begin, rows_in)[0]
    return accum.reshape(NX, NY, LZ, 4, NV)
```

```python
import jax
import jax.numpy as jnp
from jax import lax
from jax.experimental import pallas as pl
from jax.experimental.pallas import tpu as pltpu
from jax.sharding import PartitionSpec as P

ONSITE_S = -0.22
ONSITE_P = 0.27
HOP_SS = -0.37
HOP_SP = 0.35
HOP_PPS = 0.4
HOP_PPP = -0.114
BOND_LENGTH = 1.536
LATTICE_STEP = 1.6

SIDE = 4
DEPTH = 8
ATOMS = SIDE * SIDE * DEPTH
FACE = SIDE * DEPTH
WIDE = FACE + 2 * DEPTH
NV = 256
POS_ROWS = 9
LIST_ROWS = 6
Y_AUX = 4
X_AUX = 7
F32 = jnp.float32
BF16 = jnp.bfloat16


def iota(shape, axis):
    return lax.broadcasted_iota(jnp.int32, shape, axis)


def onehot(values, expected):
    wide = [jnp.where(row == expected, 1.0, 0.0).astype(BF16) for row in values]
    return wide[0] if len(wide) == 1 else jnp.concatenate(wide, axis=1)


def dot_nt(a, b):
    return lax.dot_general(a, b, (((1,), (1,)), ((), ())), preferred_element_type=F32)


def dot(a, b):
    return jnp.dot(a, b, preferred_element_type=F32)


def list_of(rows):
    first = [rows[k : k + 1] for k in range(2)]
    key = [rows[4 + k : 5 + k] * float(ATOMS) + rows[2 + k : 3 + k] for k in range(2)]
    return first, key


def code(step_x, step_y):
    return (step_x + 1) * 3 + step_y + 1


def hopping(dx, dy, dz, count):
    square = jnp.maximum(dx * dx + dy * dy + dz * dz, 0.5)
    inverse = lax.rsqrt(square)
    cosines = [d * inverse for d in (dx, dy, dz)]
    ratio = BOND_LENGTH * inverse
    radial = ratio * ratio * jnp.exp(1.0 - square * inverse * (1.0 / BOND_LENGTH))

    def final(value):
        return (value.astype(BF16).astype(F32) * count).astype(BF16)

    grid = [[None] * 4 for _ in range(4)]
    grid[0][0] = final(HOP_SS * radial)
    for a in range(3):
        across = final(HOP_SP * radial * cosines[a])
        grid[0][1 + a] = across
        grid[1 + a][0] = -across
        for b in range(a, 3):
            entry = (HOP_PPS - HOP_PPP) * cosines[a] * cosines[b]
            if a == b:
                entry = entry + HOP_PPP
            grid[1 + a][1 + b] = grid[1 + b][1 + a] = final(entry * radial)
    return grid


def interleave(grid, rows, columns):
    total = None
    for b in range(4):
        stacked = jnp.concatenate([grid[a][b] for a in range(4)], axis=0)
        at = (iota((columns, 4 * columns), 1) == 4 * iota((columns, 4 * columns), 0) + b)
        part = dot(stacked, jnp.where(at, 1.0, 0.0).astype(BF16))
        total = part if total is None else total + part
    target = iota((4 * rows, 4 * rows), 0)
    source = (target & 3) * rows + (target >> 2)
    turn = jnp.where(iota((4 * rows, 4 * rows), 1) == source, 1.0, 0.0).astype(BF16)
    return dot(turn, total.astype(BF16)).astype(BF16)


def joined(block):
    n = block.shape[0]
    wide = block.astype(F32).reshape(n // 2, 2, 4, NV)
    return jnp.concatenate([wide[:, 0], wide[:, 1]], axis=1).reshape(4 * n, NV)


def z_shift(zi, zj, period):
    step = zj - zi
    return jnp.where(step > 1.5, -period, jnp.where(step < -1.5, period, 0.0))


def pack_y(trial, pos, lists, low, high, aux):
    for face, out in ((0, low), (SIDE - 1, high)):
        for x in range(SIDE):
            begin = (x * SIDE + face) * DEPTH
            out[x * DEPTH : (x + 1) * DEPTH] = trial[begin : begin + DEPTH]
        aux[...] = jnp.zeros_like(aux)
        points = jnp.concatenate(
            [
                pos[:, (x * SIDE + face) * DEPTH : (x * SIDE + face + 1) * DEPTH]
                for x in range(SIDE)
            ],
            axis=1,
        )
        for part in range(3):
            piece = points.astype(BF16).astype(F32)
            aux[3 * part : 3 * part + 3, :FACE] = piece
            points = points - piece
        aux[POS_ROWS : POS_ROWS + LIST_ROWS] = lists[...]
        for k in range(Y_AUX):
            out[FACE + k] = aux[4 * k : 4 * k + 4].astype(BF16)


def pack_x(trial, pos, lists, from_low, from_high, low, high, aux):
    sides = [
        jnp.concatenate([m[FACE + k].astype(F32) for k in range(Y_AUX)], axis=0)
        for m in (from_low, from_high)
    ]
    for face, out in ((0, low), (SIDE - 1, high)):
        out[:FACE] = trial[face * FACE : (face + 1) * FACE]
        column = slice(face * DEPTH, (face + 1) * DEPTH)
        out[FACE : FACE + DEPTH] = from_low[column]
        out[FACE + DEPTH : WIDE] = from_high[column]
        aux[...] = jnp.zeros_like(aux)
        points = pos[:, face * FACE : (face + 1) * FACE]
        for part in range(3):
            piece = points.astype(BF16).astype(F32)
            rows = slice(3 * part, 3 * part + 3)
            aux[rows, :WIDE] = jnp.concatenate(
                [piece] + [side[rows, column] for side in sides], axis=1
            )
            points = points - piece
        aux[POS_ROWS : POS_ROWS + LIST_ROWS] = lists[...]
        for n, side in enumerate(sides):
            begin = POS_ROWS + (n + 1) * LIST_ROWS
            aux[begin : begin + LIST_ROWS] = side[POS_ROWS : POS_ROWS + LIST_ROWS]
        for k in range(X_AUX):
            out[WIDE + k] = aux[4 * k : 4 * k + 4].astype(BF16)


def aux_rows(message, first, count):
    return jnp.concatenate([message[first + k].astype(F32) for k in range(count)], axis=0)


def ghost_points(rows, columns):
    return rows[0:3, :columns] + rows[3:6, :columns] + rows[6:9, :columns]


def assemble(periods, places, trial, pos, pos_t, lists, y_low, y_high, x_low, x_high, out, acc):
    own_first, own_key = list_of(lists[...])
    at_x, at_y = places[0], places[1]
    wrap_low_x = jnp.where(at_x == 0, -periods[0], 0.0)
    wrap_high_x = jnp.where(at_x == places[2] - 1, periods[0], 0.0)
    wrap_low_y = jnp.where(at_y == 0, -periods[1], 0.0)
    wrap_high_y = jnp.where(at_y == places[3] - 1, periods[1], 0.0)
    col = lambda n: iota((n, 1), 0)

    wave = joined(trial[...])
    here = float(code(0, 0) * ATOMS)
    atom = col(ATOMS).astype(F32)
    is_first = onehot(own_first, atom)
    is_second = onehot(own_key, atom + here)
    count = dot_nt(is_first, is_second) + dot_nt(is_second, is_first)
    dx, dy, dz = (pos[a : a + 1, :] - pos_t[:, a : a + 1] for a in range(3))
    zi = (col(ATOMS) & (DEPTH - 1)).astype(F32)
    zj = (iota((1, ATOMS), 1) & (DEPTH - 1)).astype(F32)
    dz = (pos[2:3, :] + z_shift(zi, zj, periods[2])) - pos_t[:, 2:3]
    matrix = interleave(hopping(dx, dy, dz, count), ATOMS, ATOMS)
    orbital = iota((4 * ATOMS, 1), 0) & 3
    onsite = jnp.where(orbital == 0, ONSITE_S, ONSITE_P)
    acc[...] = onsite * wave + dot(matrix, wave.astype(BF16))

    zi = (col(FACE) & (DEPTH - 1)).astype(F32)

    for side, message in ((-1, y_low), (1, y_high)):
        mine = 0 if side < 0 else SIDE - 1
        theirs = SIDE - 1 - mine
        rows = aux_rows(message, FACE, Y_AUX)
        first, key = list_of(rows[POS_ROWS : POS_ROWS + LIST_ROWS])
        k = col(FACE)
        line = (k >> 3) * (SIDE * DEPTH) + (k & (DEPTH - 1))
        my_atom = (line + mine * DEPTH).astype(F32)
        their_atom = (line + theirs * DEPTH).astype(F32)
        left = onehot(own_first + key, my_atom)
        left = jnp.concatenate(
            [
                onehot(own_first, my_atom),
                onehot(key, my_atom + float(code(0, -side) * ATOMS)),
            ],
            axis=1,
        )
        right = jnp.concatenate(
            [
                onehot(own_key, their_atom + float(code(0, side) * ATOMS)),
                onehot(first, their_atom),
            ],
            axis=1,
        )
        count = dot_nt(left, right)
        points = ghost_points(rows, FACE)
        mine_t = jnp.concatenate(
            [
                pos_t[(x * SIDE + mine) * DEPTH : (x * SIDE + mine + 1) * DEPTH, :]
                for x in range(SIDE)
            ],
            axis=0,
        )
        zj = (iota((1, FACE), 1) & (DEPTH - 1)).astype(F32)
        dx = points[0:1] - mine_t[:, 0:1]
        dy = (points[1:2] + (wrap_low_y if side < 0 else wrap_high_y)) - mine_t[:, 1:2]
        dz = (points[2:3] + z_shift(zi, zj, periods[2])) - mine_t[:, 2:3]
        matrix = interleave(hopping(dx, dy, dz, count), FACE, FACE)
        part = dot(matrix, joined(message[:FACE]).astype(BF16))
        for x in range(SIDE):
            begin = (x * SIDE + mine) * DEPTH * 4
            acc[begin : begin + 4 * DEPTH] += part[x * 4 * DEPTH : (x + 1) * 4 * DEPTH]

    for side, message in ((-1, x_low), (1, x_high)):
        mine = 0 if side < 0 else SIDE - 1
        theirs = SIDE - 1 - mine
        rows = aux_rows(message, WIDE, X_AUX)
        k = col(WIDE)
        corner = (SIDE - 1) * DEPTH
        their_atom = theirs * FACE + jnp.where(
            k < FACE, k, jnp.where(k < FACE + DEPTH, k - FACE + corner, k - FACE - DEPTH)
        )
        belongs = jnp.where(k < FACE, 0, jnp.where(k < FACE + DEPTH, -1, 1))
        my_atom = (col(FACE) + mine * FACE).astype(F32)
        target = (their_atom + code(side, belongs) * ATOMS).astype(F32)
        left = [onehot(own_first, my_atom)]
        right = [onehot(own_key, target)]
        for n, step in enumerate((0, -1, 1)):
            begin = POS_ROWS + n * LIST_ROWS
            first, key = list_of(rows[begin : begin + LIST_ROWS])
            left.append(onehot(key, my_atom + float(code(-side, -step) * ATOMS)))
            right.append(onehot(first, jnp.where(belongs == step, their_atom, -2).astype(F32)))
        count = dot_nt(jnp.concatenate(left, axis=1), jnp.concatenate(right, axis=1))
        points = ghost_points(rows, WIDE)
        lane = iota((1, WIDE), 1)
        zj = (lane & (DEPTH - 1)).astype(F32)
        shift_y = jnp.where(
            lane < FACE, 0.0, jnp.where(lane < FACE + DEPTH, wrap_low_y, wrap_high_y)
        )
        mine_t = pos_t[mine * FACE : (mine + 1) * FACE, :]
        dx = (points[0:1] + (wrap_low_x if side < 0 else wrap_high_x)) - mine_t[:, 0:1]
        dy = (points[1:2] + shift_y) - mine_t[:, 1:2]
        dz = (points[2:3] + z_shift(zi, zj, periods[2])) - mine_t[:, 2:3]
        matrix = interleave(hopping(dx, dy, dz, count), FACE, WIDE)
        part = dot(matrix, joined(message[:WIDE]).astype(BF16))
        acc[mine * 4 * FACE : (mine + 1) * 4 * FACE] += part

    total = acc[...].reshape(ATOMS // 2, 8, NV)
    out[...] = jnp.stack([total[:, :4], total[:, 4:]], axis=1).reshape(ATOMS, 4, NV)


def ring(count, step):
    return [(i, (i + step) % count) for i in range(count)]


def exchange(low, high, axis):
    count = lax.axis_size(axis)
    from_low = lax.ppermute(high, axis, ring(count, 1))
    from_high = lax.ppermute(low, axis, ring(count, -1))
    return from_low, from_high


def shards(trial, positions, pair_atoms, pair_owner, pair_image, pair_count):
    across_x = lax.axis_size("gx")
    across_y = lax.axis_size("gy")
    place_x = lax.axis_index("gx")
    place_y = lax.axis_index("gy")
    periods = (
        LATTICE_STEP * (SIDE * across_x),
        LATTICE_STEP * (SIDE * across_y),
        LATTICE_STEP * DEPTH,
    )
    vmem = pl.BlockSpec(memory_space=pltpu.VMEM)
    smem = pl.BlockSpec(memory_space=pltpu.SMEM)
    mine = trial.reshape(ATOMS, 4, NV)
    pos = positions.reshape(3, ATOMS)
    owner = pair_owner[0, 0]
    step_x = (owner // across_y - place_x + 1) % across_x - 1
    step_y = (owner % across_y - place_y + 1) % across_y - 1
    slot = jnp.arange(owner.shape[0], dtype=jnp.int32)
    first = jnp.where(slot < pair_count[0, 0], pair_atoms[0, 0, 0], -1)
    lists = jnp.stack([first, pair_atoms[0, 0, 1], code(step_x, step_y)])
    lists = lists.astype(F32).reshape(LIST_ROWS, NV)
    places = jnp.stack(
        [place_x, place_y, jnp.int32(across_x), jnp.int32(across_y)]
    ).astype(jnp.int32)

    def message(sites):
        return jax.ShapeDtypeStruct((sites, 4, NV), BF16)

    low, high = pl.pallas_call(
        pack_y,
        out_shape=[message(FACE + Y_AUX)] * 2,
        in_specs=[vmem] * 3,
        out_specs=[vmem] * 2,
        scratch_shapes=[pltpu.VMEM((4 * Y_AUX, NV), F32)],
    )(mine, pos, lists)
    y_low, y_high = exchange(low, high, "gy")
    low, high = pl.pallas_call(
        pack_x,
        out_shape=[message(WIDE + X_AUX)] * 2,
        in_specs=[vmem] * 5,
        out_specs=[vmem] * 2,
        scratch_shapes=[pltpu.VMEM((4 * X_AUX, NV), F32)],
    )(mine, pos, lists, y_low, y_high)
    x_low, x_high = exchange(low, high, "gx")
    product = pl.pallas_call(
        lambda *refs: assemble(periods, *refs),
        out_shape=jax.ShapeDtypeStruct((ATOMS, 4, NV), F32),
        in_specs=[smem] + [vmem] * 8,
        out_specs=vmem,
        scratch_shapes=[pltpu.VMEM((4 * ATOMS, NV), F32)],
        compiler_params=pltpu.CompilerParams(vmem_limit_bytes=32 * 1024 * 1024),
    )(places, mine, pos, pos.T, lists, y_low, y_high, x_low, x_high)
    return product.reshape(trial.shape)


def solution(mesh):
    in_specs = (
        P("gx", "gy", None, None, None),
        P(None, "gx", "gy", None),
        P("gx", "gy", None, None),
        P("gx", "gy", None),
        P("gx", "gy", None, None),
        P("gx", "gy"),
    )
    out_specs = P("gx", "gy", None, None, None)
    return jax.shard_map(shards, mesh=mesh, in_specs=in_specs, out_specs=out_specs, check_vma=False)
```

```python
import jax
import jax.numpy as jnp
from jax import lax
from jax.experimental import pallas as pl
from jax.experimental.pallas import tpu as pltpu
from jax.sharding import PartitionSpec as P

ONSITE_S = -0.22
ONSITE_P = 0.27
HOP_SS = -0.37
HOP_SP = 0.35
HOP_PPS = 0.4
HOP_PPP = -0.114
BOND_LENGTH = 1.536
LATTICE_STEP = 1.6

SIDE = 4
DEPTH = 8
ATOMS = SIDE * SIDE * DEPTH
FACE = SIDE * DEPTH
WIDE = FACE + 2 * DEPTH
NV = 256
POS_ROWS = 9
LIST_ROWS = 6
AUX = 4
Y_SITES = FACE + AUX
X_SITES = WIDE + 3 * AUX
STEPS = [(x, y) for x in (-1, 0, 1) for y in (-1, 0, 1)]
F32 = jnp.float32
BF16 = jnp.bfloat16


def iota(shape, axis):
    return lax.broadcasted_iota(jnp.int32, shape, axis)


def onehot(values, expected):
    wide = [jnp.where(row == expected, 1.0, 0.0).astype(BF16) for row in values]
    return wide[0] if len(wide) == 1 else jnp.concatenate(wide, axis=1)


def dot_nt(a, b):
    return lax.dot_general(a, b, (((1,), (1,)), ((), ())), preferred_element_type=F32)


def dot(a, b):
    return jnp.dot(a, b, preferred_element_type=F32)


def list_of(rows):
    first = [rows[k : k + 1] for k in range(2)]
    key = [rows[4 + k : 5 + k] * float(ATOMS) + rows[2 + k : 3 + k] for k in range(2)]
    return first, key


def code(step_x, step_y):
    return (step_x + 1) * 3 + step_y + 1


def hopping(dx, dy, dz, count):
    square = jnp.maximum(dx * dx + dy * dy + dz * dz, 0.5)
    inverse = lax.rsqrt(square)
    cosines = [d * inverse for d in (dx, dy, dz)]
    ratio = BOND_LENGTH * inverse
    radial = ratio * ratio * jnp.exp(1.0 - square * inverse * (1.0 / BOND_LENGTH))

    def final(value):
        return (value.astype(BF16).astype(F32) * count).astype(BF16)

    grid = [[None] * 4 for _ in range(4)]
    grid[0][0] = final(HOP_SS * radial)
    for a in range(3):
        across = final(HOP_SP * radial * cosines[a])
        grid[0][1 + a] = across
        grid[1 + a][0] = -across
        for b in range(a, 3):
            entry = (HOP_PPS - HOP_PPP) * cosines[a] * cosines[b]
            if a == b:
                entry = entry + HOP_PPP
            grid[1 + a][1 + b] = grid[1 + b][1 + a] = final(entry * radial)
    return grid


def interleave(grid, rows, columns):
    total = None
    for b in range(4):
        stacked = jnp.concatenate([grid[a][b] for a in range(4)], axis=0)
        at = (iota((columns, 4 * columns), 1) == 4 * iota((columns, 4 * columns), 0) + b)
        part = dot(stacked, jnp.where(at, 1.0, 0.0).astype(BF16))
        total = part if total is None else total + part
    target = iota((4 * rows, 4 * rows), 0)
    source = (target & 3) * rows + (target >> 2)
    turn = jnp.where(iota((4 * rows, 4 * rows), 1) == source, 1.0, 0.0).astype(BF16)
    return dot(turn, total.astype(BF16)).astype(BF16)


def joined(block):
    n = block.shape[0]
    wide = block.astype(F32).reshape(n // 2, 2, 4, NV)
    return jnp.concatenate([wide[:, 0], wide[:, 1]], axis=1).reshape(4 * n, NV)


def turned(points):
    n = points.shape[1]
    return jnp.concatenate([points, jnp.zeros((5, n), F32)], axis=0).T


def picked_rows(pick, points):
    total = None
    for _ in range(3):
        piece = points.astype(BF16)
        part = dot(pick, piece)
        total = part if total is None else total + part
        points = points - piece.astype(F32)
    return total


def z_shift(zi, zj):
    step = zj - zi
    period = LATTICE_STEP * DEPTH
    return jnp.where(step > 1.5, -period, jnp.where(step < -1.5, period, 0.0))


def wrap(place, across, side, period):
    high = jnp.where((side > 0) & (place == across - 1), period, 0.0)
    return jnp.where((side < 0) & (place == 0), -period, high)


def side_of(place):
    first = 1 - 2 * (place & 1)
    return first, -first


def faces_of(side):
    mine = jnp.where(side > 0, SIDE - 1, 0)
    return mine, SIDE - 1 - mine


def aux_of(message, first):
    return jnp.concatenate([message[first + k].astype(F32) for k in range(AUX)], axis=0)


def points_of(rows):
    return rows[0:3] + rows[3:6] + rows[6:9]


def pack_y(places, count, trial, positions, atoms, owner, one, two, aux):
    at_x, at_y, across_x, across_y = (places[k] for k in range(4))
    rest = positions[...]
    parts = []
    for _ in range(3):
        piece = rest.astype(BF16)
        parts.append(piece)
        rest = rest - piece.astype(F32)
    rows = 3 * SIDE * SIDE
    tile = (iota((DEPTH, ATOMS), 1) & (DEPTH - 1)) == iota((DEPTH, ATOMS), 0)
    spread = dot(jnp.concatenate(parts, axis=0), jnp.where(tile, 1.0, 0.0).astype(BF16))
    row = iota((3 * rows, ATOMS), 0)
    keep = (row & (SIDE * SIDE - 1)) == (iota((3 * rows, ATOMS), 1) >> 3)
    spread = jnp.where(keep, spread, 0.0).astype(BF16)
    gather = (iota((16, 3 * rows), 1) >> 4) == iota((16, 3 * rows), 0)
    aux[:, :ATOMS] = dot(jnp.where(gather, 1.0, 0.0).astype(BF16), spread)
    aux[:, ATOMS:] = jnp.zeros((4 * AUX, NV - ATOMS), F32)
    owners = owner[...]
    step = jnp.zeros(owners.shape, F32)
    for x, y in STEPS:
        whose = lax.rem(at_x + x + across_x, across_x) * across_y
        whose = whose + lax.rem(at_y + y + across_y, across_y)
        step = jnp.where(owners == whose, float(code(x, y)), step)
    live = iota(owners.shape, 1) < count[0, 0]
    first = jnp.where(live, atoms[0:1], -1).astype(F32)
    second = atoms[1:2].astype(F32)
    for k, values in enumerate((first, second, step)):
        for h in range(2):
            at = POS_ROWS + 2 * k + h
            aux[at : at + 1] = values[:, h * NV : (h + 1) * NV]
    sites = [aux[4 * k : 4 * k + 4].astype(BF16) for k in range(AUX)]
    for side, out in zip(side_of(at_y), (one, two)):
        face, _ = faces_of(side)
        for x in range(SIDE):
            begin = (x * SIDE + face) * DEPTH
            out[x * DEPTH : (x + 1) * DEPTH] = trial[pl.ds(begin, DEPTH)]
        for k in range(AUX):
            out[FACE + k] = sites[k]


def own(places, trial, message, acc, one, two):
    rows = aux_of(message, FACE)
    first, key = list_of(rows[POS_ROWS : POS_ROWS + LIST_ROWS])
    wave = joined(trial[...])
    atom = iota((ATOMS, 1), 0)
    is_first = onehot(first, atom.astype(F32))
    is_second = onehot(key, (atom + code(0, 0) * ATOMS).astype(F32))
    count = dot_nt(is_first, is_second) + dot_nt(is_second, is_first)
    pos = points_of(rows)[:, :ATOMS]
    pos_t = turned(pos)
    zi = (atom & (DEPTH - 1)).astype(F32)
    zj = (iota((1, ATOMS), 1) & (DEPTH - 1)).astype(F32)
    dx, dy = (pos[a : a + 1] - pos_t[:, a : a + 1] for a in range(2))
    dz = (pos[2:3] + z_shift(zi, zj)) - pos_t[:, 2:3]
    matrix = interleave(hopping(dx, dy, dz, count), ATOMS, ATOMS)
    orbital = iota((4 * ATOMS, 1), 0) & 3
    onsite = jnp.where(orbital == 0, ONSITE_S, ONSITE_P)
    acc[...] = onsite * wave + dot(matrix, wave.astype(BF16))
    for side, out in zip(side_of(places[0]), (one, two)):
        face, _ = faces_of(side)
        out[:FACE] = trial[pl.ds(face * FACE, FACE)]
        out[FACE:WIDE] = jnp.zeros((2 * DEPTH, 4, NV), BF16)
        for k in range(AUX):
            out[WIDE + k] = message[FACE + k]
        out[WIDE + AUX :] = jnp.zeros((2 * AUX, 4, NV), BF16)


def corners(places, y_one, y_two, one_in, two_in, one, two):
    for side, before, out in zip(side_of(places[0]), (one_in, two_in), (one, two)):
        face, _ = faces_of(side)
        out[:FACE] = before[:FACE]
        out[WIDE : WIDE + AUX] = before[WIDE : WIDE + AUX]
        for n, message in enumerate((y_one, y_two)):
            at = FACE + n * DEPTH
            out[at : at + DEPTH] = message[pl.ds(face * DEPTH, DEPTH)]
            at = WIDE + (n + 1) * AUX
            out[at : at + AUX] = message[FACE:]


def y_faces(periods, places, message, y_one, y_two, acc_in, acc):
    acc[...] = acc_in[...]
    rows = aux_of(message, FACE)
    own_first, own_key = list_of(rows[POS_ROWS : POS_ROWS + LIST_ROWS])
    pos_t = turned(points_of(rows)[:, :ATOMS])
    k = iota((FACE, 1), 0)
    line = (k >> 3) * (SIDE * DEPTH) + (k & (DEPTH - 1))
    zi = (k & (DEPTH - 1)).astype(F32)
    zj = (iota((1, FACE), 1) & (DEPTH - 1)).astype(F32)
    for side, other in zip(side_of(places[1]), (y_one, y_two)):
        mine, theirs = faces_of(side)
        rows = aux_of(other, FACE)
        first, key = list_of(rows[POS_ROWS : POS_ROWS + LIST_ROWS])
        my_atom = line + mine * DEPTH
        their_atom = line + theirs * DEPTH
        left = [
            onehot(own_first, my_atom.astype(F32)),
            onehot(key, (my_atom + (4 - side) * ATOMS).astype(F32)),
        ]
        right = [
            onehot(own_key, (their_atom + (4 + side) * ATOMS).astype(F32)),
            onehot(first, their_atom.astype(F32)),
        ]
        count = dot_nt(jnp.concatenate(left, axis=1), jnp.concatenate(right, axis=1))
        lane = iota((ATOMS, FACE), 1)
        lane = (lane >> 3) * (SIDE * DEPTH) + (lane & (DEPTH - 1)) + theirs * DEPTH
        pick = jnp.where(iota((ATOMS, FACE), 0) == lane, 1.0, 0.0).astype(BF16)
        points = points_of(dot(rows[:, :ATOMS].astype(BF16), pick))
        pick = jnp.where(iota((FACE, ATOMS), 1) == my_atom, 1.0, 0.0).astype(BF16)
        mine_t = picked_rows(pick, pos_t)
        dx = points[0:1] - mine_t[:, 0:1]
        dy = (points[1:2] + wrap(places[1], places[3], side, periods[1])) - mine_t[:, 1:2]
        dz = (points[2:3] + z_shift(zi, zj)) - mine_t[:, 2:3]
        matrix = interleave(hopping(dx, dy, dz, count), FACE, FACE)
        part = dot(matrix, joined(other[:FACE]).astype(BF16))
        for x in range(SIDE):
            at = pl.ds(pl.multiple_of((x * SIDE + mine) * DEPTH * 4, DEPTH * 4), 4 * DEPTH)
            acc[at] += part[x * 4 * DEPTH : (x + 1) * 4 * DEPTH]


def x_faces(periods, places, message, x_one, x_two, acc, out, total):
    total[...] = acc[...]
    rows = aux_of(message, FACE)
    own_first, own_key = list_of(rows[POS_ROWS : POS_ROWS + LIST_ROWS])
    pos_t = turned(points_of(rows)[:, :ATOMS])
    k = iota((FACE, 1), 0)
    zi = (k & (DEPTH - 1)).astype(F32)
    y_sides = side_of(places[1])
    for side, other in zip(side_of(places[0]), (x_one, x_two)):
        mine, theirs = faces_of(side)
        my_atom = k + mine * FACE

        def ghost(shape, axis):
            at = iota(shape, axis)
            part = jnp.where(at < FACE, 0, jnp.where(at < FACE + DEPTH, 1, 2))
            step = jnp.where(part == 0, 0, jnp.where(part == 1, y_sides[0], y_sides[1]))
            row = jnp.where(step > 0, 0, (SIDE - 1) * DEPTH)
            atom = theirs * FACE + jnp.where(part == 0, at, row + (at & (DEPTH - 1)))
            return atom, step, part

        their_atom, step, part = ghost((WIDE, 1), 0)
        target = their_atom + ((side + 1) * 3 + step + 1) * ATOMS
        left = [onehot(own_first, my_atom.astype(F32))]
        right = [onehot(own_key, target.astype(F32))]
        points = None
        lane_atom, _, lane_part = ghost((ATOMS, WIDE), 1)
        for n, y in enumerate((0, *y_sides)):
            rows = aux_of(other, WIDE + n * AUX)
            first, key = list_of(rows[POS_ROWS : POS_ROWS + LIST_ROWS])
            wanted = my_atom + ((1 - side) * 3 + 1 - y) * ATOMS
            left.append(onehot(key, wanted.astype(F32)))
            right.append(onehot(first, jnp.where(part == n, their_atom, -2).astype(F32)))
            pick = jnp.where(
                (iota((ATOMS, WIDE), 0) == lane_atom) & (lane_part == n), 1.0, 0.0
            ).astype(BF16)
            placed = dot(rows[:, :ATOMS].astype(BF16), pick)
            points = placed if points is None else points + placed
        count = dot_nt(jnp.concatenate(left, axis=1), jnp.concatenate(right, axis=1))
        points = points_of(points)
        lane = iota((1, WIDE), 1)
        zj = (lane & (DEPTH - 1)).astype(F32)
        shifts = [wrap(places[1], places[3], y, periods[1]) for y in y_sides]
        shift_y = jnp.where(lane < FACE, 0.0, jnp.where(lane < FACE + DEPTH, *shifts))
        mine_t = picked_rows(
            jnp.where(iota((FACE, ATOMS), 1) == my_atom, 1.0, 0.0).astype(BF16), pos_t
        )
        dx = (points[0:1] + wrap(places[0], places[2], side, periods[0])) - mine_t[:, 0:1]
        dy = (points[1:2] + shift_y) - mine_t[:, 1:2]
        dz = (points[2:3] + z_shift(zi, zj)) - mine_t[:, 2:3]
        matrix = interleave(hopping(dx, dy, dz, count), FACE, WIDE)
        added = dot(matrix, joined(other[:WIDE]).astype(BF16))
        at = pl.ds(pl.multiple_of(mine * 4 * FACE, 4 * FACE), 4 * FACE)
        total[at] += added
    wide = total[...].reshape(ATOMS // 2, 8, NV)
    out[...] = jnp.stack([wide[:, :4], wide[:, 4:]], axis=1).reshape(ATOMS, 4, NV)


def swap(count, begin):
    pairs = []
    for i in range(begin, count + begin, 2):
        a, b = i % count, (i + 1) % count
        pairs += [(a, b), (b, a)]
    return pairs


def exchange(one, two, axis):
    count = lax.axis_size(axis)
    one = lax.ppermute(one, axis, swap(count, 0))
    two = lax.ppermute(two, axis, swap(count, 1))
    return one, two


def call(kernel, inputs, outputs, specs, **options):
    vmem = pl.BlockSpec(memory_space=pltpu.VMEM)
    return pl.pallas_call(
        kernel,
        out_shape=outputs,
        in_specs=specs + [vmem] * (len(inputs) - len(specs)),
        out_specs=[vmem] * len(outputs),
        compiler_params=pltpu.CompilerParams(vmem_limit_bytes=16 * 1024 * 1024),
        **options,
    )(*inputs)


def shards(trial, positions, pair_atoms, pair_owner, pair_image, pair_count):
    across_x = lax.axis_size("gx")
    across_y = lax.axis_size("gy")
    periods = (LATTICE_STEP * (SIDE * across_x), LATTICE_STEP * (SIDE * across_y))
    smem = pl.BlockSpec(memory_space=pltpu.SMEM)
    mine = trial.reshape(ATOMS, 4, NV)
    places = jnp.stack(
        [lax.axis_index("gx"), lax.axis_index("gy"), jnp.int32(across_x), jnp.int32(across_y)]
    ).astype(jnp.int32)

    def message(sites):
        return jax.ShapeDtypeStruct((sites, 4, NV), BF16)

    y_out = call(
        pack_y,
        (
            places,
            pair_count,
            mine,
            positions.reshape(3 * SIDE * SIDE, DEPTH),
            pair_atoms.reshape(2, -1),
            pair_owner.reshape(1, -1),
        ),
        [message(Y_SITES)] * 2,
        [smem] * 2,
        scratch_shapes=[pltpu.VMEM((4 * AUX, NV), F32)],
    )
    y_in = exchange(*y_out, "gy")
    rows = jax.ShapeDtypeStruct((4 * ATOMS, NV), F32)
    acc, *x_out = call(own, (places, mine, y_out[0]), [rows] + [message(X_SITES)] * 2, [smem])
    x_out = call(
        corners,
        (places, *y_in, *x_out),
        [message(X_SITES)] * 2,
        [smem],
        input_output_aliases={3: 0, 4: 1},
    )
    x_in = exchange(*x_out, "gx")
    (acc,) = call(
        lambda *refs: y_faces(periods, *refs),
        (places, y_out[0], *y_in, acc),
        [rows],
        [smem],
        input_output_aliases={4: 0},
    )
    (product,) = call(
        lambda *refs: x_faces(periods, *refs),
        (places, y_out[0], *x_in, acc),
        [jax.ShapeDtypeStruct((ATOMS, 4, NV), F32)],
        [smem],
        scratch_shapes=[pltpu.VMEM((4 * ATOMS, NV), F32)],
    )
    return product.reshape(trial.shape)


def solution(mesh):
    in_specs = (
        P("gx", "gy", None, None, None),
        P(None, "gx", "gy", None),
        P("gx", "gy", None, None),
        P("gx", "gy", None),
        P("gx", "gy", None, None),
        P("gx", "gy"),
    )
    out_specs = P("gx", "gy", None, None, None)
    return jax.shard_map(shards, mesh=mesh, in_specs=in_specs, out_specs=out_specs, check_vma=False)
```

```python
import functools

import jax
import jax.numpy as jnp
from jax import lax
from jax.experimental import pallas as pl
from jax.experimental.pallas import tpu as pltpu
from jax.sharding import PartitionSpec as P

ONSITE_S = -0.22
ONSITE_P = 0.27
HOP_SS = -0.37
HOP_SP = 0.35
HOP_PPS = 0.4
HOP_PPP = -0.114
BOND_LENGTH = 1.536
LATTICE_STEP = 1.6

SIDE = 4
DEPTH = 8
ATOMS = SIDE * SIDE * DEPTH
FACE = SIDE * DEPTH
WIDE = FACE + 2 * DEPTH
NV = 256
LANES = NV // 2
POS_ROWS = 9
LIST_ROWS = 6
AUX = 4
Y_PLACE = (DEPTH, 0, 3 * DEPTH + AUX, 2 * DEPTH + AUX)
Y_AUX = 2 * DEPTH
Y_SITES = FACE + AUX
X_BLOCK = (FACE + AUX, FACE + AUX + DEPTH + AUX)
X_SITES = WIDE + 3 * AUX
STEPS = [(x, y) for x in (-1, 0, 1) for y in (-1, 0, 1)]
F32 = jnp.float32
BF16 = jnp.bfloat16


def iota(shape, axis):
    return lax.broadcasted_iota(jnp.int32, shape, axis)


def onehot(values, expected):
    wide = [jnp.where(row == expected, 1.0, 0.0).astype(BF16) for row in values]
    return wide[0] if len(wide) == 1 else jnp.concatenate(wide, axis=1)


def dot_nt(a, b):
    return lax.dot_general(a, b, (((1,), (1,)), ((), ())), preferred_element_type=F32)


def dot(a, b):
    return jnp.dot(a, b, preferred_element_type=F32)


def list_of(rows):
    first = [rows[k : k + 1] for k in range(2)]
    key = [rows[4 + k : 5 + k] * float(ATOMS) + rows[2 + k : 3 + k] for k in range(2)]
    return first, key


def code(step_x, step_y):
    return (step_x + 1) * 3 + step_y + 1


def hopping(dx, dy, dz, count):
    square = jnp.maximum(dx * dx + dy * dy + dz * dz, 0.5)
    inverse = lax.rsqrt(square)
    cosines = [d * inverse for d in (dx, dy, dz)]
    ratio = BOND_LENGTH * inverse
    radial = ratio * ratio * jnp.exp(1.0 - square * inverse * (1.0 / BOND_LENGTH))

    def final(value):
        return (value.astype(BF16).astype(F32) * count).astype(BF16)

    grid = [[None] * 4 for _ in range(4)]
    grid[0][0] = final(HOP_SS * radial)
    for a in range(3):
        across = final(HOP_SP * radial * cosines[a])
        grid[0][1 + a] = across
        grid[1 + a][0] = -across
        for b in range(a, 3):
            entry = (HOP_PPS - HOP_PPP) * cosines[a] * cosines[b]
            if a == b:
                entry = entry + HOP_PPP
            grid[1 + a][1 + b] = grid[1 + b][1 + a] = final(entry * radial)
    return grid


def planes_of(wave, block):
    n = block.shape[0]
    wide = block.astype(F32).reshape(n // 2, 2, 4, NV)
    wide = jnp.concatenate([wide[:, 0], wide[:, 1]], axis=1).reshape(4 * n, NV)
    for h in range(2):
        wave[h, : 4 * n] = wide[:, h * LANES : (h + 1) * LANES]
    halves = [[wave[h, pl.ds(b, n, stride=4), :] for h in range(2)] for b in range(4)]
    return [jnp.concatenate(pair, axis=1) for pair in halves]


def applied(grid, planes):
    total = None
    for b in range(4):
        stacked = jnp.concatenate([grid[a][b] for a in range(4)], axis=0)
        part = dot(stacked, planes[b].astype(BF16))
        total = part if total is None else total + part
    return total


def atoms_of(planes, wave):
    n = planes[0].shape[0]
    for a in range(4):
        for h in range(2):
            wave[h, pl.ds(a, n, stride=4), :] = planes[a][:, h * LANES : (h + 1) * LANES]
    wide = jnp.concatenate([wave[h, : 4 * n] for h in range(2)], axis=1)
    wide = wide.reshape(n // 2, 8, NV)
    return jnp.stack([wide[:, :4], wide[:, 4:]], axis=1).reshape(n, 4, NV)


def turned(points):
    n = points.shape[1]
    return jnp.concatenate([points, jnp.zeros((5, n), F32)], axis=0).T


def picked_rows(pick, points):
    total = None
    for _ in range(3):
        piece = points.astype(BF16)
        part = dot(pick, piece)
        total = part if total is None else total + part
        points = points - piece.astype(F32)
    return total


def z_shift(zi, zj):
    step = zj - zi
    period = LATTICE_STEP * DEPTH
    return jnp.where(step > 1.5, -period, jnp.where(step < -1.5, period, 0.0))


def wrap(place, across, side, period):
    high = jnp.where((side > 0) & (place == across - 1), period, 0.0)
    return jnp.where((side < 0) & (place == 0), -period, high)


def place_of(sizes):
    return lax.axis_index("gx"), lax.axis_index("gy"), *sizes


def side_of(place):
    first = 1 - 2 * (place & 1)
    return first, -first


def faces_of(side):
    mine = jnp.where(side > 0, SIDE - 1, 0)
    return mine, SIDE - 1 - mine


def aux_of(message, first):
    return jnp.concatenate([message[first + k].astype(F32) for k in range(AUX)], axis=0)


def points_of(rows):
    return rows[0:3] + rows[3:6] + rows[6:9]


def pack_y(sizes, trial, positions, atoms, owner, count, one, two, aux, pos, pairs, owners, total, sem):
    at_x, at_y, across_x, across_y = place_of(sizes)
    copies = [
        pltpu.make_async_copy(a, b, sem.at[k])
        for k, (a, b) in enumerate(
            ((positions, pos), (atoms, pairs), (owner, owners), (count, total))
        )
    ]
    for side, out in zip(side_of(at_y), (one, two)):
        face, _ = faces_of(side)
        for x in range(SIDE):
            begin = (x * SIDE + face) * DEPTH
            part = out.at[pl.ds(Y_PLACE[x], DEPTH)]
            copies.append(
                pltpu.make_async_copy(trial.at[pl.ds(begin, DEPTH)], part, sem.at[len(copies)])
            )
    for copy in copies:
        copy.start()
    rows = 3 * SIDE * SIDE
    tile = (iota((DEPTH, ATOMS), 1) & (DEPTH - 1)) == iota((DEPTH, ATOMS), 0)
    tile = jnp.where(tile, 1.0, 0.0).astype(BF16)
    row = iota((3 * rows, ATOMS), 0)
    keep = (row & (SIDE * SIDE - 1)) == (iota((3 * rows, ATOMS), 1) >> 3)
    gather = (iota((16, 3 * rows), 1) >> 4) == iota((16, 3 * rows), 0)
    gather = jnp.where(gather, 1.0, 0.0).astype(BF16)
    aux[:, ATOMS:] = jnp.zeros((4 * AUX, NV - ATOMS), F32)
    for copy in copies[:4]:
        copy.wait()
    rest = pos[...]
    parts = []
    for _ in range(3):
        piece = rest.astype(BF16)
        parts.append(piece)
        rest = rest - piece.astype(F32)
    spread = dot(jnp.concatenate(parts, axis=0), tile)
    aux[:, :ATOMS] = dot(gather, jnp.where(keep, spread, 0.0).astype(BF16))
    whose = owners[...]
    step = jnp.zeros(whose.shape, F32)
    for x, y in STEPS:
        name = lax.rem(at_x + x + across_x, across_x) * across_y
        name = name + lax.rem(at_y + y + across_y, across_y)
        step = jnp.where(whose == name, float(code(x, y)), step)
    live = iota(whose.shape, 1) < total[0, 0]
    first = jnp.where(live, pairs[0:1], -1).astype(F32)
    second = pairs[1:2].astype(F32)
    for k, values in enumerate((first, second, step)):
        for h in range(2):
            at = POS_ROWS + 2 * k + h
            aux[at : at + 1] = values[:, h * NV : (h + 1) * NV]
    for k in range(AUX):
        site = aux[4 * k : 4 * k + 4].astype(BF16)
        one[Y_AUX + k] = site
        two[Y_AUX + k] = site
    for copy in copies[4:]:
        copy.wait()


def own(sizes, trial, message, acc, one, two, wave):
    for side, out in zip(side_of(place_of(sizes)[0]), (one, two)):
        face, _ = faces_of(side)
        out[:FACE] = trial[pl.ds(face * FACE, FACE)]
        out[FACE : FACE + AUX] = message[Y_AUX : Y_AUX + AUX]
    rows = aux_of(message, Y_AUX)
    first, key = list_of(rows[POS_ROWS : POS_ROWS + LIST_ROWS])
    atom = iota((ATOMS, 1), 0)
    is_first = onehot(first, atom.astype(F32))
    is_second = onehot(key, (atom + code(0, 0) * ATOMS).astype(F32))
    count = dot_nt(is_first, is_second) + dot_nt(is_second, is_first)
    pos = points_of(rows)[:, :ATOMS]
    pos_t = turned(pos)
    zi = (atom & (DEPTH - 1)).astype(F32)
    zj = (iota((1, ATOMS), 1) & (DEPTH - 1)).astype(F32)
    dx, dy = (pos[a : a + 1] - pos_t[:, a : a + 1] for a in range(2))
    dz = (pos[2:3] + z_shift(zi, zj)) - pos_t[:, 2:3]
    grid = hopping(dx, dy, dz, count)
    planes = planes_of(wave, trial[...])
    matrix = jnp.concatenate([jnp.concatenate(line, axis=1) for line in grid], axis=0)
    part = dot(matrix, jnp.concatenate(planes, axis=0).astype(BF16))
    for a in range(4):
        onsite = ONSITE_P if a else ONSITE_S
        rows = slice(a * ATOMS, (a + 1) * ATOMS)
        acc[rows] = onsite * planes[a] + part[rows]


def corners(sizes, y_one, y_two, one_in, two_in, one, two, sem):
    del one_in, two_in
    copies = []
    for side, out in zip(side_of(place_of(sizes)[0]), (one, two)):
        face, _ = faces_of(side)
        begin = jnp.where(face == 0, Y_PLACE[0], Y_AUX)
        for n, message in enumerate((y_one, y_two)):
            part = out.at[pl.ds(X_BLOCK[n], DEPTH + AUX)]
            copy = pltpu.make_async_copy(
                message.at[pl.ds(begin, DEPTH + AUX)], part, sem.at[len(copies)]
            )
            copy.start()
            copies.append(copy)
    for copy in copies:
        copy.wait()


def y_faces(periods, sizes, message, y_one, y_two, acc_in, acc, middle, wave):
    acc[...] = acc_in[...]
    at_x, at_y, _, across_y = place_of(sizes)
    rows = aux_of(message, Y_AUX)
    own_first, own_key = list_of(rows[POS_ROWS : POS_ROWS + LIST_ROWS])
    pos_t = turned(points_of(rows)[:, :ATOMS])
    k = iota((FACE, 1), 0)
    line = (k >> 3) * (SIDE * DEPTH) + (k & (DEPTH - 1))
    crossed = ((k >> 3) ^ 1) * (SIDE * DEPTH) + (k & (DEPTH - 1))
    zi = (k & (DEPTH - 1)).astype(F32)
    zj = (iota((1, FACE), 1) & (DEPTH - 1)).astype(F32)
    half = 2 * DEPTH
    for side, other in zip(side_of(at_y), (y_one, y_two)):
        mine, theirs = faces_of(side)
        rows = aux_of(other, Y_AUX)
        first, key = list_of(rows[POS_ROWS : POS_ROWS + LIST_ROWS])
        my_atom = line + mine * DEPTH
        their_atom = crossed + theirs * DEPTH
        left = [
            onehot(own_first, my_atom.astype(F32)),
            onehot(key, (my_atom + (4 - side) * ATOMS).astype(F32)),
        ]
        right = [
            onehot(own_key, (their_atom + (4 + side) * ATOMS).astype(F32)),
            onehot(first, their_atom.astype(F32)),
        ]
        count = dot_nt(jnp.concatenate(left, axis=1), jnp.concatenate(right, axis=1))
        lane = iota((ATOMS, FACE), 1)
        lane = ((lane >> 3) ^ 1) * (SIDE * DEPTH) + (lane & (DEPTH - 1)) + theirs * DEPTH
        pick = jnp.where(iota((ATOMS, FACE), 0) == lane, 1.0, 0.0).astype(BF16)
        points = points_of(dot(rows[:, :ATOMS].astype(BF16), pick))
        pick = jnp.where(iota((FACE, ATOMS), 1) == my_atom, 1.0, 0.0).astype(BF16)
        mine_t = picked_rows(pick, pos_t)
        dx = points[0:1] - mine_t[:, 0:1]
        dy = (points[1:2] + wrap(at_y, across_y, side, periods[1])) - mine_t[:, 1:2]
        dz = (points[2:3] + z_shift(zi, zj)) - mine_t[:, 2:3]
        grid = hopping(dx, dy, dz, count)
        block = jnp.concatenate([other[:half], other[half + AUX :]], axis=0)
        part = applied(grid, planes_of(wave, block))
        for a in range(4):
            for x in range(SIDE):
                at = pl.multiple_of(a * ATOMS + (x * SIDE + mine) * DEPTH, DEPTH)
                begin = a * FACE + x * DEPTH
                acc[pl.ds(at, DEPTH)] += part[begin : begin + DEPTH]
    planes = [acc[a * ATOMS + FACE : a * ATOMS + 3 * FACE] for a in range(4)]
    middle[...] = atoms_of(planes, wave)


def x_faces(periods, sizes, message, x_two, x_one, acc, middle, out, wave, other_wave, faces, sem):
    copies = [pltpu.make_async_copy(middle, out.at[pl.ds(FACE, 2 * FACE)], sem.at[2])]
    copies[0].start()
    at_x, at_y, across_x, across_y = place_of(sizes)
    rows = aux_of(message, Y_AUX)
    own_first, own_key = list_of(rows[POS_ROWS : POS_ROWS + LIST_ROWS])
    pos_t = turned(points_of(rows)[:, :ATOMS])
    k = iota((FACE, 1), 0)
    zi = (k & (DEPTH - 1)).astype(F32)
    lane = iota((1, WIDE), 1)
    zj = (lane & (DEPTH - 1)).astype(F32)
    y_sides = side_of(at_y)
    shifts = [wrap(at_y, across_y, y, periods[1]) for y in y_sides]
    shift_y = jnp.where(lane < FACE, 0.0, jnp.where(lane < FACE + DEPTH, *shifts))
    parts = []
    for n, (side, other) in enumerate(zip(side_of(at_x), (x_one, x_two))):
        mine, theirs = faces_of(side)
        corner_at = jnp.where(theirs == 0, 0, AUX)
        aux_at = jnp.where(theirs == 0, DEPTH, 0)
        my_atom = k + mine * FACE

        def ghost(shape, axis):
            at = iota(shape, axis)
            part = jnp.where(at < FACE, 0, jnp.where(at < FACE + DEPTH, 1, 2))
            step = jnp.where(part == 0, 0, jnp.where(part == 1, y_sides[0], y_sides[1]))
            row = jnp.where(step > 0, 0, (SIDE - 1) * DEPTH)
            atom = theirs * FACE + jnp.where(part == 0, at, row + (at & (DEPTH - 1)))
            return atom, step, part

        their_atom, step, part = ghost((WIDE, 1), 0)
        target = their_atom + ((side + 1) * 3 + step + 1) * ATOMS
        left = [onehot(own_first, my_atom.astype(F32))]
        right = [onehot(own_key, target.astype(F32))]
        points = None
        lane_atom, _, lane_part = ghost((ATOMS, WIDE), 1)
        for m, y in enumerate((0, *y_sides)):
            rows = aux_of(other, X_BLOCK[m - 1] + aux_at if m else FACE)
            first, key = list_of(rows[POS_ROWS : POS_ROWS + LIST_ROWS])
            wanted = my_atom + ((1 - side) * 3 + 1 - y) * ATOMS
            left.append(onehot(key, wanted.astype(F32)))
            right.append(onehot(first, jnp.where(part == m, their_atom, -2).astype(F32)))
            pick = (iota((ATOMS, WIDE), 0) == lane_atom) & (lane_part == m)
            placed = dot(rows[:, :ATOMS].astype(BF16), jnp.where(pick, 1.0, 0.0).astype(BF16))
            points = placed if points is None else points + placed
        count = dot_nt(jnp.concatenate(left, axis=1), jnp.concatenate(right, axis=1))
        points = points_of(points)
        mine_t = picked_rows(
            jnp.where(iota((FACE, ATOMS), 1) == my_atom, 1.0, 0.0).astype(BF16), pos_t
        )
        dx = (points[0:1] + wrap(at_x, across_x, side, periods[0])) - mine_t[:, 0:1]
        dy = (points[1:2] + shift_y) - mine_t[:, 1:2]
        dz = (points[2:3] + z_shift(zi, zj)) - mine_t[:, 2:3]
        grid = hopping(dx, dy, dz, count)
        block = [other[:FACE]] + [other[pl.ds(X_BLOCK[m] + corner_at, DEPTH)] for m in range(2)]
        planes = planes_of((wave, other_wave)[n], jnp.concatenate(block, axis=0))
        part = applied(grid, planes)
        before = [acc[pl.ds(pl.multiple_of(a * ATOMS + mine * FACE, FACE), FACE)] for a in range(4)]
        parts.append([before[a] + part[a * FACE : (a + 1) * FACE] for a in range(4)])
    for n, side in enumerate(side_of(at_x)):
        mine, _ = faces_of(side)
        faces[n] = atoms_of(parts[n], (wave, other_wave)[n])
        copy = pltpu.make_async_copy(faces.at[n], out.at[pl.ds(mine * FACE, FACE)], sem.at[n])
        copy.start()
        copies.append(copy)
    for copy in copies:
        copy.wait()


def swap(count, begin):
    pairs = []
    for i in range(begin, count + begin, 2):
        a, b = i % count, (i + 1) % count
        pairs += [(a, b), (b, a)]
    return pairs


def exchange(one, two, axis):
    count = lax.axis_size(axis)
    two = lax.ppermute(two, axis, swap(count, 1))
    one = lax.ppermute(one, axis, swap(count, 0))
    return one, two


VMEM = pl.BlockSpec(memory_space=pltpu.VMEM)
HBM = pl.BlockSpec(memory_space=pltpu.HBM)
ANY = pl.BlockSpec(memory_space=pl.ANY)


def call(kernel, inputs, outputs, in_space=VMEM, out_space=VMEM, limit=16, **options):
    limit = limit and limit * 1024 * 1024
    return pl.pallas_call(
        kernel,
        out_shape=outputs,
        in_specs=[in_space] * len(inputs),
        out_specs=[out_space] * len(outputs),
        compiler_params=pltpu.CompilerParams(vmem_limit_bytes=limit),
        **options,
    )(*inputs)


def shards(trial, positions, pair_atoms, pair_owner, pair_image, pair_count):
    sizes = lax.axis_size("gx"), lax.axis_size("gy")
    periods = tuple(LATTICE_STEP * (SIDE * count) for count in sizes)
    mine = trial.reshape(ATOMS, 4, NV)
    slots = pair_owner.shape[2]

    def message(sites):
        return jax.ShapeDtypeStruct((sites, 4, NV), BF16)

    def wave(rows):
        return pltpu.VMEM((2, rows, LANES), F32)

    y_out = call(
        functools.partial(pack_y, sizes),
        (
            mine,
            positions.reshape(3 * SIDE * SIDE, DEPTH),
            pair_atoms.reshape(2, slots),
            pair_owner.reshape(1, slots),
            pair_count,
        ),
        [message(Y_SITES)] * 2,
        in_space=HBM,
        limit=None,
        scratch_shapes=[
            pltpu.VMEM((4 * AUX, NV), F32),
            pltpu.VMEM((3 * SIDE * SIDE, DEPTH), F32),
            pltpu.VMEM((2, slots), jnp.int32),
            pltpu.VMEM((1, slots), jnp.int32),
            pltpu.SMEM((1, 1), jnp.int32),
            pltpu.SemaphoreType.DMA((4 + 2 * SIDE,)),
        ],
    )
    y_one, y_two = exchange(*y_out, "gy")
    rows = jax.ShapeDtypeStruct((4 * ATOMS, NV), F32)
    acc, *x_out = call(
        functools.partial(own, sizes),
        (mine, y_out[0]),
        [rows] + [message(X_SITES)] * 2,
        scratch_shapes=[wave(4 * ATOMS)],
    )
    x_out = call(
        functools.partial(corners, sizes),
        (y_one, y_two, *x_out),
        [message(X_SITES)] * 2,
        in_space=ANY,
        out_space=ANY,
        input_output_aliases={2: 0, 3: 1},
        scratch_shapes=[pltpu.SemaphoreType.DMA((4,))],
    )
    x_one, x_two = exchange(*x_out, "gx")
    acc, middle = call(
        functools.partial(y_faces, periods, sizes),
        (y_out[0], y_one, y_two, acc),
        [rows, jax.ShapeDtypeStruct((ATOMS // 2, 4, NV), F32)],
        scratch_shapes=[wave(2 * ATOMS)],
    )
    (product,) = call(
        functools.partial(x_faces, periods, sizes),
        (y_out[0], x_two, x_one, acc, middle),
        [jax.ShapeDtypeStruct((ATOMS, 4, NV), F32)],
        out_space=HBM,
        scratch_shapes=[
            wave(4 * WIDE),
            wave(4 * WIDE),
            pltpu.VMEM((2, FACE, 4, NV), F32),
            pltpu.SemaphoreType.DMA((3,)),
        ],
    )
    return product.reshape(trial.shape)


def solution(mesh):
    in_specs = (
        P("gx", "gy", None, None, None),
        P(None, "gx", "gy", None),
        P("gx", "gy", None, None),
        P("gx", "gy", None),
        P("gx", "gy", None, None),
        P("gx", "gy"),
    )
    out_specs = P("gx", "gy", None, None, None)
    return jax.shard_map(shards, mesh=mesh, in_specs=in_specs, out_specs=out_specs, check_vma=False)
```

```python
import functools

import jax
import jax.numpy as jnp
from jax import lax
from jax.experimental import pallas as pl
from jax.experimental.pallas import tpu as pltpu
from jax.sharding import PartitionSpec as P

ONSITE_S = -0.22
ONSITE_P = 0.27
HOP_SS = -0.37
HOP_SP = 0.35
HOP_PPS = 0.4
HOP_PPP = -0.114
BOND_LENGTH = 1.536
LATTICE_STEP = 1.6

SIDE = 4
DEPTH = 8
ATOMS = SIDE * SIDE * DEPTH
FACE = SIDE * DEPTH
WIDE = FACE + 2 * DEPTH
NV = 256
LANES = NV // 2
POS_ROWS = 9
LIST_ROWS = 6
AUX = 4
Y_PLACE = (DEPTH, 0, 3 * DEPTH + AUX, 2 * DEPTH + AUX)
Y_AUX = 2 * DEPTH
Y_SITES = FACE + AUX
X_BLOCK = (FACE + AUX, FACE + AUX + DEPTH + AUX)
X_SITES = WIDE + 3 * AUX
STEPS = [(x, y) for x in (-1, 0, 1) for y in (-1, 0, 1)]
F32 = jnp.float32
BF16 = jnp.bfloat16


def iota(shape, axis):
    return lax.broadcasted_iota(jnp.int32, shape, axis)


def onehot(values, expected):
    wide = [jnp.where(row == expected, 1.0, 0.0).astype(BF16) for row in values]
    return wide[0] if len(wide) == 1 else jnp.concatenate(wide, axis=1)


def dot_nt(a, b):
    return lax.dot_general(a, b, (((1,), (1,)), ((), ())), preferred_element_type=F32)


def dot(a, b):
    return jnp.dot(a, b, preferred_element_type=F32)


def list_of(rows):
    first = [rows[k : k + 1] for k in range(2)]
    key = [rows[4 + k : 5 + k] * float(ATOMS) + rows[2 + k : 3 + k] for k in range(2)]
    return first, key


def code(step_x, step_y):
    return (step_x + 1) * 3 + step_y + 1


def hopping(dx, dy, dz, count):
    square = jnp.maximum(dx * dx + dy * dy + dz * dz, 0.5)
    inverse = lax.rsqrt(square)
    cosines = [d * inverse for d in (dx, dy, dz)]
    ratio = BOND_LENGTH * inverse
    radial = ratio * ratio * jnp.exp(1.0 - square * inverse * (1.0 / BOND_LENGTH))

    def final(value):
        return (value.astype(BF16).astype(F32) * count).astype(BF16)

    grid = [[None] * 4 for _ in range(4)]
    grid[0][0] = final(HOP_SS * radial)
    for a in range(3):
        across = final(HOP_SP * radial * cosines[a])
        grid[0][1 + a] = across
        grid[1 + a][0] = -across
        for b in range(a, 3):
            entry = (HOP_PPS - HOP_PPP) * cosines[a] * cosines[b]
            if a == b:
                entry = entry + HOP_PPP
            grid[1 + a][1 + b] = grid[1 + b][1 + a] = final(entry * radial)
    return grid


def planes_of(wave, block):
    n = block.shape[0]
    wide = block.astype(F32).reshape(n // 2, 2, 4, NV)
    wide = jnp.concatenate([wide[:, 0], wide[:, 1]], axis=1).reshape(4 * n, NV)
    for h in range(2):
        wave[h, : 4 * n] = wide[:, h * LANES : (h + 1) * LANES]
    halves = [[wave[h, pl.ds(b, n, stride=4), :] for h in range(2)] for b in range(4)]
    return [jnp.concatenate(pair, axis=1) for pair in halves]


def applied(grid, planes):
    total = None
    for b in range(4):
        stacked = jnp.concatenate([grid[a][b] for a in range(4)], axis=0)
        part = dot(stacked, planes[b].astype(BF16))
        total = part if total is None else total + part
    return total


def atoms_of(planes, wave):
    n = planes[0].shape[0]
    for a in range(4):
        for h in range(2):
            wave[h, pl.ds(a, n, stride=4), :] = planes[a][:, h * LANES : (h + 1) * LANES]
    wide = jnp.concatenate([wave[h, : 4 * n] for h in range(2)], axis=1)
    wide = wide.reshape(n // 2, 8, NV)
    return jnp.stack([wide[:, :4], wide[:, 4:]], axis=1).reshape(n, 4, NV)


def turned(points):
    n = points.shape[1]
    return jnp.concatenate([points, jnp.zeros((5, n), F32)], axis=0).T


def picked_rows(pick, points):
    total = None
    for _ in range(3):
        piece = points.astype(BF16)
        part = dot(pick, piece)
        total = part if total is None else total + part
        points = points - piece.astype(F32)
    return total


def z_shift(zi, zj):
    step = zj - zi
    period = LATTICE_STEP * DEPTH
    return jnp.where(step > 1.5, -period, jnp.where(step < -1.5, period, 0.0))


def wrap(place, across, side, period):
    high = jnp.where((side > 0) & (place == across - 1), period, 0.0)
    return jnp.where((side < 0) & (place == 0), -period, high)


def place_of(sizes):
    return lax.axis_index("gx"), lax.axis_index("gy"), *sizes


def side_of(place):
    first = 1 - 2 * (place & 1)
    return first, -first


def faces_of(side):
    mine = jnp.where(side > 0, SIDE - 1, 0)
    return mine, SIDE - 1 - mine


def aux_of(message, first):
    return jnp.concatenate([message[first + k].astype(F32) for k in range(AUX)], axis=0)


def either(lower, low, top):
    return lambda at: jnp.where(lower, low[at].astype(F32), top[at].astype(F32))


def points_of(rows):
    return rows[0:3] + rows[3:6] + rows[6:9]


def pack_y(sizes, trial, positions, atoms, owner, count, low, two, top, aux, pos, pairs, owners, sem):
    at_x, at_y, across_x, across_y = place_of(sizes)
    copies = [
        pltpu.make_async_copy(a, b, sem.at[k])
        for k, (a, b) in enumerate(((positions, pos), (atoms, pairs), (owner, owners)))
    ]
    first, second = side_of(at_y)
    for side, out in ((first, low), (second, two), (first, top)):
        face, _ = faces_of(side)
        for x in range(SIDE):
            begin = (x * SIDE + face) * DEPTH
            part = out.at[pl.ds(Y_PLACE[x], DEPTH)]
            copies.append(
                pltpu.make_async_copy(trial.at[pl.ds(begin, DEPTH)], part, sem.at[len(copies)])
            )
    for copy in copies:
        copy.start()
    rows = 3 * SIDE * SIDE
    tile = (iota((DEPTH, ATOMS), 1) & (DEPTH - 1)) == iota((DEPTH, ATOMS), 0)
    tile = jnp.where(tile, 1.0, 0.0).astype(BF16)
    row = iota((3 * rows, ATOMS), 0)
    keep = (row & (SIDE * SIDE - 1)) == (iota((3 * rows, ATOMS), 1) >> 3)
    gather = (iota((16, 3 * rows), 1) >> 4) == iota((16, 3 * rows), 0)
    gather = jnp.where(gather, 1.0, 0.0).astype(BF16)
    aux[:, ATOMS:] = jnp.zeros((4 * AUX, NV - ATOMS), F32)
    for copy in copies[:3]:
        copy.wait()
    rest = pos[...]
    parts = []
    for _ in range(3):
        piece = rest.astype(BF16)
        parts.append(piece)
        rest = rest - piece.astype(F32)
    spread = dot(jnp.concatenate(parts, axis=0), tile)
    aux[:, :ATOMS] = dot(gather, jnp.where(keep, spread, 0.0).astype(BF16))
    whose = owners[...]
    step = jnp.zeros(whose.shape, F32)
    for x, y in STEPS:
        name = lax.rem(at_x + x + across_x, across_x) * across_y
        name = name + lax.rem(at_y + y + across_y, across_y)
        step = jnp.where(whose == name, float(code(x, y)), step)
    live = iota(whose.shape, 1) < count[0, 0]
    first = jnp.where(live, pairs[0:1], -1).astype(F32)
    second = pairs[1:2].astype(F32)
    for k, values in enumerate((first, second, step)):
        for h in range(2):
            at = POS_ROWS + 2 * k + h
            aux[at : at + 1] = values[:, h * NV : (h + 1) * NV]
    for k in range(AUX):
        site = aux[4 * k : 4 * k + 4].astype(BF16)
        for out in (low, two, top):
            out[Y_AUX + k] = site
    for copy in copies[3:]:
        copy.wait()


def own(sizes, trial, aux, acc, one, two, wave):
    for side, out in zip(side_of(place_of(sizes)[0]), (one, two)):
        face, _ = faces_of(side)
        out[:FACE] = trial[pl.ds(face * FACE, FACE)]
        for k in range(AUX):
            out[FACE + k] = aux[4 * k : 4 * k + 4].astype(BF16)
    rows = aux[...]
    first, key = list_of(rows[POS_ROWS : POS_ROWS + LIST_ROWS])
    atom = iota((ATOMS, 1), 0)
    is_first = onehot(first, atom.astype(F32))
    is_second = onehot(key, (atom + code(0, 0) * ATOMS).astype(F32))
    count = dot_nt(is_first, is_second) + dot_nt(is_second, is_first)
    pos = points_of(rows)[:, :ATOMS]
    pos_t = turned(pos)
    zi = (atom & (DEPTH - 1)).astype(F32)
    zj = (iota((1, ATOMS), 1) & (DEPTH - 1)).astype(F32)
    dx, dy = (pos[a : a + 1] - pos_t[:, a : a + 1] for a in range(2))
    dz = (pos[2:3] + z_shift(zi, zj)) - pos_t[:, 2:3]
    grid = hopping(dx, dy, dz, count)
    planes = planes_of(wave, trial[...])
    matrix = jnp.concatenate([jnp.concatenate(line, axis=1) for line in grid], axis=0)
    part = dot(matrix, jnp.concatenate(planes, axis=0).astype(BF16))
    for a in range(4):
        onsite = ONSITE_P if a else ONSITE_S
        rows = slice(a * ATOMS, (a + 1) * ATOMS)
        acc[rows] = onsite * planes[a] + part[rows]


def in_lower(sizes):
    _, at_y, _, across_y = place_of(sizes)
    return at_y < across_y // 4 * 2


def corners(sizes, y_low, y_two, y_top, one_in, two_in, one, two, sem):
    del one_in, two_in
    lower = in_lower(sizes)
    copies = []
    for side, out in zip(side_of(place_of(sizes)[0]), (one, two)):
        face, _ = faces_of(side)
        begin = jnp.where(face == 0, Y_PLACE[0], Y_AUX)

        def copy_of(message, n):
            part = out.at[pl.ds(X_BLOCK[n], DEPTH + AUX)]
            return pltpu.make_async_copy(
                message.at[pl.ds(begin, DEPTH + AUX)], part, sem.at[len(copies)]
            )

        @pl.when(lower)
        def _():
            copy_of(y_low, 0).start()

        @pl.when(jnp.logical_not(lower))
        def _():
            copy_of(y_top, 0).start()

        copies.append(copy_of(y_low, 0))
        copies.append(copy_of(y_two, 1))
        copies[-1].start()
    for copy in copies:
        copy.wait()


def y_faces(periods, sizes, aux, y_low, y_two, y_top, acc_in, acc, middle, wave):
    acc[...] = acc_in[...]
    at_x, at_y, _, across_y = place_of(sizes)
    rows = aux[...]
    own_first, own_key = list_of(rows[POS_ROWS : POS_ROWS + LIST_ROWS])
    pos_t = turned(points_of(rows)[:, :ATOMS])
    k = iota((FACE, 1), 0)
    line = (k >> 3) * (SIDE * DEPTH) + (k & (DEPTH - 1))
    crossed = ((k >> 3) ^ 1) * (SIDE * DEPTH) + (k & (DEPTH - 1))
    zi = (k & (DEPTH - 1)).astype(F32)
    zj = (iota((1, FACE), 1) & (DEPTH - 1)).astype(F32)
    half = 2 * DEPTH
    readers = either(in_lower(sizes), y_low, y_top), lambda at: y_two[at].astype(F32)
    for side, read in zip(side_of(at_y), readers):
        mine, theirs = faces_of(side)
        rows = jnp.concatenate([read(Y_AUX + k) for k in range(AUX)], axis=0)
        first, key = list_of(rows[POS_ROWS : POS_ROWS + LIST_ROWS])
        my_atom = line + mine * DEPTH
        their_atom = crossed + theirs * DEPTH
        left = [
            onehot(own_first, my_atom.astype(F32)),
            onehot(key, (my_atom + (4 - side) * ATOMS).astype(F32)),
        ]
        right = [
            onehot(own_key, (their_atom + (4 + side) * ATOMS).astype(F32)),
            onehot(first, their_atom.astype(F32)),
        ]
        count = dot_nt(jnp.concatenate(left, axis=1), jnp.concatenate(right, axis=1))
        lane = iota((ATOMS, FACE), 1)
        lane = ((lane >> 3) ^ 1) * (SIDE * DEPTH) + (lane & (DEPTH - 1)) + theirs * DEPTH
        pick = jnp.where(iota((ATOMS, FACE), 0) == lane, 1.0, 0.0).astype(BF16)
        points = points_of(dot(rows[:, :ATOMS].astype(BF16), pick))
        pick = jnp.where(iota((FACE, ATOMS), 1) == my_atom, 1.0, 0.0).astype(BF16)
        mine_t = picked_rows(pick, pos_t)
        dx = points[0:1] - mine_t[:, 0:1]
        dy = (points[1:2] + wrap(at_y, across_y, side, periods[1])) - mine_t[:, 1:2]
        dz = (points[2:3] + z_shift(zi, zj)) - mine_t[:, 2:3]
        grid = hopping(dx, dy, dz, count)
        block = jnp.concatenate([read(slice(0, half)), read(slice(half + AUX, Y_SITES))], axis=0)
        part = applied(grid, planes_of(wave, block))
        for a in range(4):
            for x in range(SIDE):
                at = pl.multiple_of(a * ATOMS + (x * SIDE + mine) * DEPTH, DEPTH)
                begin = a * FACE + x * DEPTH
                acc[pl.ds(at, DEPTH)] += part[begin : begin + DEPTH]
    planes = [acc[a * ATOMS + FACE : a * ATOMS + 3 * FACE] for a in range(4)]
    middle[...] = atoms_of(planes, wave)


def x_faces(periods, sizes, aux, x_two, x_one, acc, middle, out, wave, other_wave, faces, sem):
    copies = [pltpu.make_async_copy(middle, out.at[pl.ds(FACE, 2 * FACE)], sem.at[2])]
    copies[0].start()
    at_x, at_y, across_x, across_y = place_of(sizes)
    rows = aux[...]
    own_first, own_key = list_of(rows[POS_ROWS : POS_ROWS + LIST_ROWS])
    pos_t = turned(points_of(rows)[:, :ATOMS])
    k = iota((FACE, 1), 0)
    zi = (k & (DEPTH - 1)).astype(F32)
    lane = iota((1, WIDE), 1)
    zj = (lane & (DEPTH - 1)).astype(F32)
    y_sides = side_of(at_y)
    shifts = [wrap(at_y, across_y, y, periods[1]) for y in y_sides]
    shift_y = jnp.where(lane < FACE, 0.0, jnp.where(lane < FACE + DEPTH, *shifts))
    parts = []
    for n, (side, other) in enumerate(zip(side_of(at_x), (x_one, x_two))):
        mine, theirs = faces_of(side)
        corner_at = jnp.where(theirs == 0, 0, AUX)
        aux_at = jnp.where(theirs == 0, DEPTH, 0)
        my_atom = k + mine * FACE

        def ghost(shape, axis):
            at = iota(shape, axis)
            part = jnp.where(at < FACE, 0, jnp.where(at < FACE + DEPTH, 1, 2))
            step = jnp.where(part == 0, 0, jnp.where(part == 1, y_sides[0], y_sides[1]))
            row = jnp.where(step > 0, 0, (SIDE - 1) * DEPTH)
            atom = theirs * FACE + jnp.where(part == 0, at, row + (at & (DEPTH - 1)))
            return atom, step, part

        their_atom, step, part = ghost((WIDE, 1), 0)
        target = their_atom + ((side + 1) * 3 + step + 1) * ATOMS
        left = [onehot(own_first, my_atom.astype(F32))]
        right = [onehot(own_key, target.astype(F32))]
        points = None
        lane_atom, _, lane_part = ghost((ATOMS, WIDE), 1)
        for m, y in enumerate((0, *y_sides)):
            rows = aux_of(other, X_BLOCK[m - 1] + aux_at if m else FACE)
            first, key = list_of(rows[POS_ROWS : POS_ROWS + LIST_ROWS])
            wanted = my_atom + ((1 - side) * 3 + 1 - y) * ATOMS
            left.append(onehot(key, wanted.astype(F32)))
            right.append(onehot(first, jnp.where(part == m, their_atom, -2).astype(F32)))
            pick = (iota((ATOMS, WIDE), 0) == lane_atom) & (lane_part == m)
            placed = dot(rows[:, :ATOMS].astype(BF16), jnp.where(pick, 1.0, 0.0).astype(BF16))
            points = placed if points is None else points + placed
        count = dot_nt(jnp.concatenate(left, axis=1), jnp.concatenate(right, axis=1))
        points = points_of(points)
        mine_t = picked_rows(
            jnp.where(iota((FACE, ATOMS), 1) == my_atom, 1.0, 0.0).astype(BF16), pos_t
        )
        dx = (points[0:1] + wrap(at_x, across_x, side, periods[0])) - mine_t[:, 0:1]
        dy = (points[1:2] + shift_y) - mine_t[:, 1:2]
        dz = (points[2:3] + z_shift(zi, zj)) - mine_t[:, 2:3]
        grid = hopping(dx, dy, dz, count)
        block = [other[:FACE]] + [other[pl.ds(X_BLOCK[m] + corner_at, DEPTH)] for m in range(2)]
        planes = planes_of((wave, other_wave)[n], jnp.concatenate(block, axis=0))
        part = applied(grid, planes)
        before = [acc[pl.ds(pl.multiple_of(a * ATOMS + mine * FACE, FACE), FACE)] for a in range(4)]
        parts.append([before[a] + part[a * FACE : (a + 1) * FACE] for a in range(4)])
    for n, side in enumerate(side_of(at_x)):
        mine, _ = faces_of(side)
        faces[n] = atoms_of(parts[n], (wave, other_wave)[n])
        copy = pltpu.make_async_copy(faces.at[n], out.at[pl.ds(mine * FACE, FACE)], sem.at[n])
        copy.start()
        copies.append(copy)
    for copy in copies:
        copy.wait()


def swap(count, begin):
    pairs = []
    for i in range(begin, count + begin, 2):
        a, b = i % count, (i + 1) % count
        pairs += [(a, b), (b, a)]
    return pairs


def exchange(one, two, axis):
    count = lax.axis_size(axis)
    two = lax.ppermute(two, axis, swap(count, 1))
    one = lax.ppermute(one, axis, swap(count, 0))
    return one, two


def exchange_y(low, two, top):
    count = lax.axis_size("gy")
    pairs = swap(count, 0)
    begin = count // 4 * 2
    low = lax.ppermute(low, "gy", pairs[:begin])
    two = lax.ppermute(two, "gy", swap(count, 1))
    top = lax.ppermute(top, "gy", pairs[begin:])
    return low, two, top


VMEM = pl.BlockSpec(memory_space=pltpu.VMEM)
HBM = pl.BlockSpec(memory_space=pltpu.HBM)
ANY = pl.BlockSpec(memory_space=pl.ANY)
SMEM = pl.BlockSpec(memory_space=pltpu.SMEM)


def call(kernel, inputs, outputs, in_space=VMEM, out_space=VMEM, limit=16, **options):
    limit = limit and limit * 1024 * 1024
    return pl.pallas_call(
        kernel,
        out_shape=outputs,
        in_specs=in_space if isinstance(in_space, list) else [in_space] * len(inputs),
        out_specs=[out_space] * len(outputs),
        compiler_params=pltpu.CompilerParams(vmem_limit_bytes=limit),
        **options,
    )(*inputs)


def shards(trial, positions, pair_atoms, pair_owner, pair_image, pair_count):
    sizes = lax.axis_size("gx"), lax.axis_size("gy")
    periods = tuple(LATTICE_STEP * (SIDE * count) for count in sizes)
    mine = trial.reshape(ATOMS, 4, NV)
    slots = pair_owner.shape[2]

    def message(sites):
        return jax.ShapeDtypeStruct((sites, 4, NV), BF16)

    def wave(rows):
        return pltpu.VMEM((2, rows, LANES), F32)

    *y_out, aux = call(
        functools.partial(pack_y, sizes),
        tuple(
            pltpu.with_memory_space_constraint(array, pltpu.HBM)
            for array in (
                mine,
                positions.reshape(3 * SIDE * SIDE, DEPTH),
                pair_atoms.reshape(2, slots),
                pair_owner.reshape(1, slots),
            )
        )
        + (pair_count,),
        [message(Y_SITES)] * 3 + [jax.ShapeDtypeStruct((4 * AUX, NV), F32)],
        in_space=[HBM] * 4 + [SMEM],
        scratch_shapes=[
            pltpu.VMEM((3 * SIDE * SIDE, DEPTH), F32),
            pltpu.VMEM((2, slots), jnp.int32),
            pltpu.VMEM((1, slots), jnp.int32),
            pltpu.SemaphoreType.DMA((3 + 3 * SIDE,)),
        ],
    )
    y_low, y_two, y_top = exchange_y(*y_out)
    rows = jax.ShapeDtypeStruct((4 * ATOMS, NV), F32)
    acc, *x_out = call(
        functools.partial(own, sizes),
        (mine, aux),
        [rows] + [message(X_SITES)] * 2,
        scratch_shapes=[wave(4 * ATOMS)],
    )
    x_out = call(
        functools.partial(corners, sizes),
        (y_low, y_two, y_top, *x_out),
        [message(X_SITES)] * 2,
        in_space=ANY,
        out_space=ANY,
        input_output_aliases={3: 0, 4: 1},
        scratch_shapes=[pltpu.SemaphoreType.DMA((4,))],
    )
    x_one, x_two = exchange(*x_out, "gx")
    acc, middle = call(
        functools.partial(y_faces, periods, sizes),
        (aux, y_low, y_two, y_top, acc),
        [rows, jax.ShapeDtypeStruct((ATOMS // 2, 4, NV), F32)],
        scratch_shapes=[wave(2 * ATOMS)],
    )
    (product,) = call(
        functools.partial(x_faces, periods, sizes),
        (aux, x_two, x_one, acc, middle),
        [jax.ShapeDtypeStruct((ATOMS, 4, NV), F32)],
        out_space=HBM,
        scratch_shapes=[
            wave(4 * WIDE),
            wave(4 * WIDE),
            pltpu.VMEM((2, FACE, 4, NV), F32),
            pltpu.SemaphoreType.DMA((3,)),
        ],
    )
    return product.reshape(trial.shape)


def solution(mesh):
    in_specs = (
        P("gx", "gy", None, None, None),
        P(None, "gx", "gy", None),
        P("gx", "gy", None, None),
        P("gx", "gy", None),
        P("gx", "gy", None, None),
        P("gx", "gy"),
    )
    out_specs = P("gx", "gy", None, None, None)
    return jax.shard_map(shards, mesh=mesh, in_specs=in_specs, out_specs=out_specs, check_vma=False)
```

```python
import functools

import jax
import jax.numpy as jnp
from jax import lax
from jax.experimental import pallas as pl
from jax.experimental.pallas import tpu as pltpu
from jax.sharding import PartitionSpec as P

ONSITE_S = -0.22
ONSITE_P = 0.27
HOP_SS = -0.37
HOP_SP = 0.35
HOP_PPS = 0.4
HOP_PPP = -0.114
BOND_LENGTH = 1.536
LATTICE_STEP = 1.6

SIDE = 4
DEPTH = 8
ATOMS = SIDE * SIDE * DEPTH
FACE = SIDE * DEPTH
WIDE = FACE + 2 * DEPTH
NV = 256
LANES = NV // 2
POS_ROWS = 9
LIST_ROWS = 6
AUX = 4
Y_PLACE = (DEPTH, 0, 3 * DEPTH + AUX, 2 * DEPTH + AUX)
Y_AUX = 2 * DEPTH
Y_SITES = FACE + AUX
BLOCK = DEPTH + AUX
X_BLOCK = (FACE + AUX, FACE + AUX + BLOCK)
X_SITES = WIDE + 3 * AUX
STEPS = [(x, y) for x in (-1, 0, 1) for y in (-1, 0, 1)]
F32 = jnp.float32
BF16 = jnp.bfloat16


def iota(shape, axis):
    return lax.broadcasted_iota(jnp.int32, shape, axis)


def onehot(values, expected):
    wide = [jnp.where(row == expected, 1.0, 0.0).astype(BF16) for row in values]
    return wide[0] if len(wide) == 1 else jnp.concatenate(wide, axis=1)


def dot_nt(a, b):
    return lax.dot_general(a, b, (((1,), (1,)), ((), ())), preferred_element_type=F32)


def dot(a, b):
    return jnp.dot(a, b, preferred_element_type=F32)


def list_of(rows):
    first = [rows[k : k + 1] for k in range(2)]
    key = [rows[4 + k : 5 + k] * float(ATOMS) + rows[2 + k : 3 + k] for k in range(2)]
    return first, key


def code(step_x, step_y):
    return (step_x + 1) * 3 + step_y + 1


def hopping(dx, dy, dz, count):
    square = jnp.maximum(dx * dx + dy * dy + dz * dz, 0.5)
    inverse = lax.rsqrt(square)
    cosines = [d * inverse for d in (dx, dy, dz)]
    ratio = BOND_LENGTH * inverse
    radial = ratio * ratio * jnp.exp(1.0 - square * inverse * (1.0 / BOND_LENGTH))

    def final(value):
        return (value.astype(BF16).astype(F32) * count).astype(BF16)

    grid = [[None] * 4 for _ in range(4)]
    grid[0][0] = final(HOP_SS * radial)
    for a in range(3):
        across = final(HOP_SP * radial * cosines[a])
        grid[0][1 + a] = across
        grid[1 + a][0] = -across
        for b in range(a, 3):
            entry = (HOP_PPS - HOP_PPP) * cosines[a] * cosines[b]
            if a == b:
                entry = entry + HOP_PPP
            grid[1 + a][1 + b] = grid[1 + b][1 + a] = final(entry * radial)
    return grid


def planes_of(wave, block):
    n = block.shape[0]
    wide = block.astype(F32).reshape(n // 2, 2, 4, NV)
    wide = jnp.concatenate([wide[:, 0], wide[:, 1]], axis=1).reshape(4 * n, NV)
    for h in range(2):
        wave[h, : 4 * n] = wide[:, h * LANES : (h + 1) * LANES]
    halves = [[wave[h, pl.ds(b, n, stride=4), :] for h in range(2)] for b in range(4)]
    return [jnp.concatenate(pair, axis=1) for pair in halves]


def applied(grid, planes):
    total = None
    for b in range(4):
        stacked = jnp.concatenate([grid[a][b] for a in range(4)], axis=0)
        part = dot(stacked, planes[b].astype(BF16))
        total = part if total is None else total + part
    return total


def atoms_of(planes, wave):
    n = planes[0].shape[0]
    for a in range(4):
        for h in range(2):
            wave[h, pl.ds(a, n, stride=4), :] = planes[a][:, h * LANES : (h + 1) * LANES]
    wide = jnp.concatenate([wave[h, : 4 * n] for h in range(2)], axis=1)
    wide = wide.reshape(n // 2, 8, NV)
    return jnp.stack([wide[:, :4], wide[:, 4:]], axis=1).reshape(n, 4, NV)


def turned(points):
    n = points.shape[1]
    return jnp.concatenate([points, jnp.zeros((5, n), F32)], axis=0).T


def picked_rows(pick, points):
    total = None
    for _ in range(3):
        piece = points.astype(BF16)
        part = dot(pick, piece)
        total = part if total is None else total + part
        points = points - piece.astype(F32)
    return total


def z_shift(zi, zj):
    step = zj - zi
    period = LATTICE_STEP * DEPTH
    return jnp.where(step > 1.5, -period, jnp.where(step < -1.5, period, 0.0))


def wrap(place, across, side, period):
    high = jnp.where((side > 0) & (place == across - 1), period, 0.0)
    return jnp.where((side < 0) & (place == 0), -period, high)


def place_of(sizes):
    return lax.axis_index("gx"), lax.axis_index("gy"), *sizes


def side_of(place):
    first = 1 - 2 * (place & 1)
    return first, -first


def faces_of(side):
    mine = jnp.where(side > 0, SIDE - 1, 0)
    return mine, SIDE - 1 - mine


def sum_of(*readers):
    def read(at):
        total = None
        for reader in readers:
            value = reader(at)
            total = value if total is None else total + value
        return total

    return read


def reader_of(message, first=0):
    return lambda at: message[pl.ds(first + at[0], at[1])].astype(F32)


def aux_of(read, first):
    sites = read((first, AUX))
    return jnp.concatenate([sites[k] for k in range(AUX)], axis=0)


def points_of(rows):
    return rows[0:3] + rows[3:6] + rows[6:9]


def pack_y(sizes, trial, positions, atoms, owner, count, *refs):
    low, two, top, over, over_up, over_down, aux, pos, pairs, owners, sem = refs
    at_x, at_y, across_x, across_y = place_of(sizes)
    copies = [
        pltpu.make_async_copy(a, b, sem.at[k])
        for k, (a, b) in enumerate(((positions, pos), (atoms, pairs), (owner, owners)))
    ]
    faces = [faces_of(side)[0] for side in side_of(at_y)]
    moves = [
        (x, faces[n], out.at[pl.ds(begin + Y_PLACE[x], DEPTH)])
        for n, out, begin in (
            (0, low, 0),
            (1, low, Y_SITES),
            (1, two, 0),
            (0, top, 0),
            (1, over, 0),
        )
        for x in range(SIDE)
    ]
    moves.append((SIDE - 1, faces[1], over_up.at[pl.ds(AUX, DEPTH)]))
    moves.append((0, faces[1], over_down.at[pl.ds(0, DEPTH)]))
    for x, face, out in moves:
        begin = (x * SIDE + face) * DEPTH
        copies.append(
            pltpu.make_async_copy(trial.at[pl.ds(begin, DEPTH)], out, sem.at[len(copies)])
        )
    for copy in copies:
        copy.start()
    rows = 3 * SIDE * SIDE
    tile = (iota((DEPTH, ATOMS), 1) & (DEPTH - 1)) == iota((DEPTH, ATOMS), 0)
    tile = jnp.where(tile, 1.0, 0.0).astype(BF16)
    row = iota((3 * rows, ATOMS), 0)
    keep = (row & (SIDE * SIDE - 1)) == (iota((3 * rows, ATOMS), 1) >> 3)
    gather = (iota((16, 3 * rows), 1) >> 4) == iota((16, 3 * rows), 0)
    gather = jnp.where(gather, 1.0, 0.0).astype(BF16)
    aux[:, ATOMS:] = jnp.zeros((4 * AUX, NV - ATOMS), F32)
    for copy in copies[:3]:
        copy.wait()
    rest = pos[...]
    parts = []
    for _ in range(3):
        piece = rest.astype(BF16)
        parts.append(piece)
        rest = rest - piece.astype(F32)
    spread = dot(jnp.concatenate(parts, axis=0), tile)
    aux[:, :ATOMS] = dot(gather, jnp.where(keep, spread, 0.0).astype(BF16))
    whose = owners[...]
    step = jnp.zeros(whose.shape, F32)
    for x, y in STEPS:
        name = lax.rem(at_x + x + across_x, across_x) * across_y
        name = name + lax.rem(at_y + y + across_y, across_y)
        step = jnp.where(whose == name, float(code(x, y)), step)
    live = iota(whose.shape, 1) < count[0, 0]
    first = jnp.where(live, pairs[0:1], -1).astype(F32)
    second = pairs[1:2].astype(F32)
    for k, values in enumerate((first, second, step)):
        for h in range(2):
            at = POS_ROWS + 2 * k + h
            aux[at : at + 1] = values[:, h * NV : (h + 1) * NV]
    places = [(out, Y_AUX) for out in (low, two, top, over)]
    places += [(low, Y_SITES + Y_AUX), (over_up, 0), (over_down, DEPTH)]
    for k in range(AUX):
        site = aux[4 * k : 4 * k + 4].astype(BF16)
        for out, at in places:
            out[at + k] = site
    for copy in copies[3:]:
        copy.wait()


def own(trial, aux, acc, wave):
    rows = aux[...]
    first, key = list_of(rows[POS_ROWS : POS_ROWS + LIST_ROWS])
    atom = iota((ATOMS, 1), 0)
    is_first = onehot(first, atom.astype(F32))
    is_second = onehot(key, (atom + code(0, 0) * ATOMS).astype(F32))
    count = dot_nt(is_first, is_second) + dot_nt(is_second, is_first)
    pos = points_of(rows)[:, :ATOMS]
    pos_t = turned(pos)
    zi = (atom & (DEPTH - 1)).astype(F32)
    zj = (iota((1, ATOMS), 1) & (DEPTH - 1)).astype(F32)
    dx, dy = (pos[a : a + 1] - pos_t[:, a : a + 1] for a in range(2))
    dz = (pos[2:3] + z_shift(zi, zj)) - pos_t[:, 2:3]
    grid = hopping(dx, dy, dz, count)
    planes = planes_of(wave, trial[...])
    matrix = jnp.concatenate([jnp.concatenate(line, axis=1) for line in grid], axis=0)
    part = dot(matrix, jnp.concatenate(planes, axis=0).astype(BF16))
    for a in range(4):
        onsite = ONSITE_P if a else ONSITE_S
        rows = slice(a * ATOMS, (a + 1) * ATOMS)
        acc[rows] = onsite * planes[a] + part[rows]


def corners(sizes, late, *refs):
    *inputs, one, two, sem = refs
    if late:
        _, relayed, *inputs = inputs
    trial, message, y_one, y_two = inputs
    at_x, at_y, _, across_y = place_of(sizes)
    copies = []

    def copy_of(source, begin, count, out, at):
        return pltpu.make_async_copy(
            source.at[pl.ds(begin, count)], out.at[pl.ds(at, count)], sem.at[len(copies)]
        )

    for side, out in zip(side_of(at_x), (one, two)):
        face, _ = faces_of(side)
        begin = jnp.where(face == 0, Y_PLACE[0], Y_AUX)
        for given in (
            (trial, face * FACE, FACE, out, 0),
            (message, Y_AUX, AUX, out, FACE),
            (y_one, begin, BLOCK, out, X_BLOCK[0]),
        ):
            copies.append(copy_of(*given))
            copies[-1].start()
        plain = copy_of(y_two, begin, BLOCK, out, X_BLOCK[1])
        if late:
            other = copy_of(relayed, begin, BLOCK, out, X_BLOCK[1])

            @pl.when(at_y == across_y - 1)
            def _():
                other.start()

            @pl.when(at_y != across_y - 1)
            def _():
                plain.start()
        else:
            plain.start()
        copies.append(plain)
    for copy in copies:
        copy.wait()


def crossed(sizes, over, up, down, one, two, sem):
    del over
    copies = []
    for n, (side, out) in enumerate(zip(side_of(place_of(sizes)[0]), (one, two))):
        low, high = (pltpu.make_async_copy(source.at[pl.ds(0, BLOCK)], out, sem.at[n]) for source in (up, down))

        @pl.when(side < 0)
        def _():
            low.start()

        @pl.when(side > 0)
        def _():
            high.start()

        copies.append(low)
    for copy in copies:
        copy.wait()


def hand_on(after, y_low, top, relay, out, sem):
    del after
    copies = [
        pltpu.make_async_copy(y_low.at[pl.ds(Y_SITES, Y_SITES)], relay, sem.at[0]),
        pltpu.make_async_copy(top, out, sem.at[1]),
    ]
    for copy in copies:
        copy.start()
    for copy in copies:
        copy.wait()


def own_of(aux):
    rows = aux[...]
    return *list_of(rows[POS_ROWS : POS_ROWS + LIST_ROWS]), turned(points_of(rows)[:, :ATOMS])


def y_atoms(side):
    mine, theirs = faces_of(side)
    k = iota((FACE, 1), 0)
    z = k & (DEPTH - 1)
    line = (k >> 3) * (SIDE * DEPTH) + z
    crossed = ((k >> 3) ^ 1) * (SIDE * DEPTH) + z
    return line + mine * DEPTH, crossed + theirs * DEPTH


def y_ahead(side, own_first, own_key, pos_t):
    my_atom, their_atom = y_atoms(side)
    left = onehot(own_first, my_atom.astype(F32))
    right = onehot(own_key, (their_atom + (4 + side) * ATOMS).astype(F32))
    pick = jnp.where(iota((FACE, ATOMS), 1) == my_atom, 1.0, 0.0).astype(BF16)
    return dot_nt(left, right), picked_rows(pick, pos_t)


def y_part(period, sizes, side, read, forward, mine_t, wave):
    _, at_y, _, across_y = place_of(sizes)
    _, theirs = faces_of(side)
    my_atom, their_atom = y_atoms(side)
    rows = aux_of(read, Y_AUX)
    first, key = list_of(rows[POS_ROWS : POS_ROWS + LIST_ROWS])
    left = onehot(key, (my_atom + (4 - side) * ATOMS).astype(F32))
    count = forward + dot_nt(left, onehot(first, their_atom.astype(F32)))
    lane = iota((ATOMS, FACE), 1)
    lane = ((lane >> 3) ^ 1) * (SIDE * DEPTH) + (lane & (DEPTH - 1)) + theirs * DEPTH
    pick = jnp.where(iota((ATOMS, FACE), 0) == lane, 1.0, 0.0).astype(BF16)
    points = points_of(dot(rows[:, :ATOMS].astype(BF16), pick))
    zi = (iota((FACE, 1), 0) & (DEPTH - 1)).astype(F32)
    zj = (iota((1, FACE), 1) & (DEPTH - 1)).astype(F32)
    dx = points[0:1] - mine_t[:, 0:1]
    dy = (points[1:2] + wrap(at_y, across_y, side, period)) - mine_t[:, 1:2]
    dz = (points[2:3] + z_shift(zi, zj)) - mine_t[:, 2:3]
    grid = hopping(dx, dy, dz, count)
    half = 2 * DEPTH
    block = jnp.concatenate([read((0, half)), read((half + AUX, half))], axis=0)
    return applied(grid, planes_of(wave, block))


def y_add(acc, side, part):
    mine, _ = faces_of(side)
    for a in range(4):
        for x in range(SIDE):
            at = pl.multiple_of(a * ATOMS + (x * SIDE + mine) * DEPTH, DEPTH)
            begin = a * FACE + x * DEPTH
            acc[pl.ds(at, DEPTH)] += part[begin : begin + DEPTH]


def ghost(theirs, y_sides, shape, axis):
    at = iota(shape, axis)
    part = jnp.where(at < FACE, 0, jnp.where(at < FACE + DEPTH, 1, 2))
    step = jnp.where(part == 0, 0, jnp.where(part == 1, y_sides[0], y_sides[1]))
    row = jnp.where(step > 0, 0, (SIDE - 1) * DEPTH)
    atom = theirs * FACE + jnp.where(part == 0, at, row + (at & (DEPTH - 1)))
    return atom, step, part


def first_half(periods, sizes, aux, y_low, y_top, acc_in, *refs):
    acc, forward_y, mine_y, forward_x, mine_x, wave = refs
    acc[...] = acc_in[...]
    at_x, at_y, _, _ = place_of(sizes)
    own_first, own_key, pos_t = own_of(aux)
    y_sides = side_of(at_y)
    forward_y[...], mine_y[...] = y_ahead(y_sides[1], own_first, own_key, pos_t)
    for n, side in enumerate(side_of(at_x)):
        mine, theirs = faces_of(side)
        my_atom = iota((FACE, 1), 0) + mine * FACE
        their_atom, step, _ = ghost(theirs, y_sides, (WIDE, 1), 0)
        target = their_atom + ((side + 1) * 3 + step + 1) * ATOMS
        left = onehot(own_first, my_atom.astype(F32))
        forward_x[n] = dot_nt(left, onehot(own_key, target.astype(F32)))
        pick = jnp.where(iota((FACE, ATOMS), 1) == my_atom, 1.0, 0.0).astype(BF16)
        mine_x[n] = picked_rows(pick, pos_t)
    forward, mine_t = y_ahead(y_sides[0], own_first, own_key, pos_t)
    read = sum_of(reader_of(y_low), reader_of(y_top))
    y_add(acc, y_sides[0], y_part(periods[1], sizes, y_sides[0], read, forward, mine_t, wave))


def second_half(periods, sizes, *refs):
    forward_y, mine_y, forward_x, mine_x, acc_in = refs[:5]
    y_two, over, relayed, *beside = refs[5:10]
    x_messages = refs[10:12]
    out, acc, wave, one_wave, two_wave, result, sem = refs[12:]
    at_x, at_y, across_x, across_y = place_of(sizes)
    acc[...] = acc_in[...]
    y_sides = side_of(at_y)
    x_sides = side_of(at_x)
    read = sum_of(reader_of(y_two), reader_of(over), reader_of(relayed))
    added = y_part(periods[1], sizes, y_sides[1], read, forward_y[...], mine_y[...], wave)
    k = iota((FACE, 1), 0)
    zi = (k & (DEPTH - 1)).astype(F32)
    lane = iota((1, WIDE), 1)
    zj = (lane & (DEPTH - 1)).astype(F32)
    shifts = [wrap(at_y, across_y, y, periods[1]) for y in y_sides]
    shift_y = jnp.where(lane < FACE, 0.0, jnp.where(lane < FACE + DEPTH, *shifts))
    parts = []
    for n, side in enumerate(x_sides):
        mine, theirs = faces_of(side)
        corner_at = jnp.where(theirs == 0, 0, AUX)
        aux_at = jnp.where(theirs == 0, DEPTH, 0)
        plain = reader_of(x_messages[n])

        def second(at, plain=plain, other=reader_of(beside[n])):
            return plain((X_BLOCK[1] + at[0], at[1])) + other(at)

        def first(at, plain=plain):
            return plain((X_BLOCK[0] + at[0], at[1]))

        my_atom = k + mine * FACE
        their_atom, _, part = ghost(theirs, y_sides, (WIDE, 1), 0)
        lane_atom, _, lane_part = ghost(theirs, y_sides, (ATOMS, WIDE), 1)
        left, right, picks, placed = [], [], [], []
        for m, y in enumerate((0, *y_sides)):
            rows = aux_of((plain, first, second)[m], aux_at if m else FACE)
            listed, key = list_of(rows[POS_ROWS : POS_ROWS + LIST_ROWS])
            wanted = my_atom + ((1 - side) * 3 + 1 - y) * ATOMS
            left.append(onehot(key, wanted.astype(F32)))
            right.append(onehot(listed, jnp.where(part == m, their_atom, -2).astype(F32)))
            pick = (iota((ATOMS, WIDE), 0) == lane_atom) & (lane_part == m)
            picks.append(jnp.where(pick, 1.0, 0.0).astype(BF16))
            placed.append(rows[:, :ATOMS].astype(BF16))
        count = forward_x[n] + dot_nt(
            jnp.concatenate(left, axis=1), jnp.concatenate(right, axis=1)
        )
        points = dot(jnp.concatenate(placed, axis=1), jnp.concatenate(picks, axis=0))
        points = points_of(points)
        mine_t = mine_x[n]
        dx = (points[0:1] + wrap(at_x, across_x, side, periods[0])) - mine_t[:, 0:1]
        dy = (points[1:2] + shift_y) - mine_t[:, 1:2]
        dz = (points[2:3] + z_shift(zi, zj)) - mine_t[:, 2:3]
        grid = hopping(dx, dy, dz, count)
        block = [plain((0, FACE)), first((corner_at, DEPTH)), second((corner_at, DEPTH))]
        planes = planes_of((one_wave, two_wave)[n], jnp.concatenate(block, axis=0))
        parts.append(applied(grid, planes))
    y_add(acc, y_sides[1], added)
    planes = [acc[a * ATOMS + FACE : a * ATOMS + 3 * FACE] for a in range(4)]
    result[FACE : 3 * FACE] = atoms_of(planes, wave)
    middle = pl.ds(FACE, 2 * FACE)
    copies = [pltpu.make_async_copy(result.at[middle], out.at[middle], sem.at[2])]
    copies[0].start()
    for n, side in enumerate(x_sides):
        mine, _ = faces_of(side)
        planes = []
        for a in range(4):
            at = pl.multiple_of(a * ATOMS + mine * FACE, FACE)
            planes.append(acc[pl.ds(at, FACE)] + parts[n][a * FACE : (a + 1) * FACE])
        face = pl.ds(mine * FACE, FACE)
        result[face] = atoms_of(planes, (one_wave, two_wave)[n])
        copies.append(pltpu.make_async_copy(result.at[face], out.at[face], sem.at[n]))
        copies[-1].start()
    for copy in copies:
        copy.wait()


def swap(count, begin):
    pairs = []
    for i in range(begin, count + begin, 2):
        a, b = i % count, (i + 1) % count
        pairs += [(a, b), (b, a)]
    return pairs


def exchange_x(one, two, rows):
    count, across_y = lax.axis_size("gx"), lax.axis_size("gy")

    def pairs(begin):
        return [
            (a * across_y + y, b * across_y + y) for y in rows for a, b in swap(count, begin)
        ]

    two = lax.ppermute(two, ("gx", "gy"), pairs(1))
    one = lax.ppermute(one, ("gx", "gy"), pairs(0))
    return one, two


def over_wrap(message, step):
    count, across_y = lax.axis_size("gx"), lax.axis_size("gy")
    pairs = [
        (x * across_y + across_y - 1, (x + step) % count * across_y) for x in range(count)
    ]
    return lax.ppermute(message, ("gx", "gy"), pairs)


VMEM = pl.BlockSpec(memory_space=pltpu.VMEM)
SMEM = pl.BlockSpec(memory_space=pltpu.SMEM)
HBM = pl.BlockSpec(memory_space=pltpu.HBM)
ANY = pl.BlockSpec(memory_space=pl.ANY)


def call(kernel, inputs, outputs, in_space=VMEM, out_space=VMEM, **options):
    return pl.pallas_call(
        kernel,
        out_shape=outputs,
        in_specs=in_space if isinstance(in_space, list) else [in_space] * len(inputs),
        out_specs=[out_space] * len(outputs),
        compiler_params=pltpu.CompilerParams(vmem_limit_bytes=16 * 1024 * 1024),
        **options,
    )(*inputs)


def shards(trial, positions, pair_atoms, pair_owner, pair_image, pair_count):
    sizes = across_x, across_y = lax.axis_size("gx"), lax.axis_size("gy")
    periods = tuple(LATTICE_STEP * (SIDE * count) for count in sizes)
    mine = trial.reshape(ATOMS, 4, NV)
    slots = pair_owner.shape[2]

    def message(sites):
        return jax.ShapeDtypeStruct((sites, 4, NV), BF16)

    def floats(*shape):
        return jax.ShapeDtypeStruct(shape, F32)

    def wave(rows):
        return pltpu.VMEM((2, rows, LANES), F32)

    low, two, top, over, over_up, over_down, aux = call(
        functools.partial(pack_y, sizes),
        tuple(
            pltpu.with_memory_space_constraint(array, pltpu.HBM)
            for array in (
                mine,
                positions.reshape(3 * SIDE * SIDE, DEPTH),
                pair_atoms.reshape(2, slots),
                pair_owner.reshape(1, slots),
            )
        )
        + (pair_count,),
        [message(2 * Y_SITES)]
        + [message(Y_SITES)] * 3
        + [message(Y_SITES)] * 2
        + [floats(4 * AUX, NV)],
        in_space=[HBM] * 4 + [SMEM],
        scratch_shapes=[
            pltpu.VMEM((3 * SIDE * SIDE, DEPTH), F32),
            pltpu.VMEM((2, slots), jnp.int32),
            pltpu.VMEM((1, slots), jnp.int32),
            pltpu.SemaphoreType.DMA((3 + 5 * SIDE + 2,)),
        ],
    )
    half = across_y // 4 * 2
    pairs = swap(across_y, 0)
    early = lax.axis_index("gy") < half
    y_low = lax.ppermute(low, "gy", pairs[:half])
    y_two = lax.ppermute(two, "gy", swap(across_y, 1)[:-2])
    over = over_wrap(over, 0)
    over_up = over_wrap(over_up, 1)
    over_down = over_wrap(over_down, -1)
    (acc,) = call(own, (mine, aux), [floats(4 * ATOMS, NV)], scratch_shapes=[wave(4 * ATOMS)])

    def x_messages(late, *given):
        return call(
            functools.partial(corners, sizes, late),
            given,
            [message(X_SITES)] * 2,
            in_space=ANY,
            out_space=ANY,
            scratch_shapes=[pltpu.SemaphoreType.DMA((8,))],
        )

    x_in = lax.cond(
        early,
        lambda: exchange_x(*x_messages(False, mine, two, y_low, y_two), range(half)),
        lambda: (jnp.zeros((X_SITES, 4, NV), BF16),) * 2,
    )
    relay, top = call(
        hand_on,
        (x_in[0], y_low, top),
        [message(Y_SITES)] * 2,
        in_space=ANY,
        out_space=ANY,
        scratch_shapes=[pltpu.SemaphoreType.DMA((2,))],
    )
    relayed = lax.ppermute(relay, "gy", [(1, across_y - 1)])
    y_top = lax.ppermute(top, "gy", pairs[half:])
    beside = call(
        functools.partial(crossed, sizes),
        (over, over_up, over_down),
        [message(BLOCK)] * 2,
        in_space=ANY,
        out_space=ANY,
        scratch_shapes=[pltpu.SemaphoreType.DMA((2,))],
    )
    x_late = x_messages(True, beside[0], relayed, mine, two, y_top, y_two)
    x_in = lax.cond(
        early,
        lambda: tuple(x_in),
        lambda: exchange_x(*x_late, range(half, across_y)),
    )
    acc, *ahead = call(
        functools.partial(first_half, periods, sizes),
        (aux, y_low, y_top, acc),
        [
            floats(4 * ATOMS, NV),
            floats(FACE, FACE),
            floats(FACE, 8),
            floats(2, FACE, WIDE),
            floats(2, FACE, 8),
        ],
        scratch_shapes=[wave(4 * FACE)],
    )
    (product,) = call(
        functools.partial(second_half, periods, sizes),
        (*ahead, acc, y_two, over, relayed, *beside, *x_in),
        [floats(ATOMS, 4, NV)],
        out_space=HBM,
        scratch_shapes=[
            pltpu.VMEM((4 * ATOMS, NV), F32),
            wave(2 * ATOMS),
            wave(4 * WIDE),
            wave(4 * WIDE),
            pltpu.VMEM((ATOMS, 4, NV), F32),
            pltpu.SemaphoreType.DMA((3,)),
        ],
    )
    return product.reshape(trial.shape)


def solution(mesh):
    in_specs = (
        P("gx", "gy", None, None, None),
        P(None, "gx", "gy", None),
        P("gx", "gy", None, None),
        P("gx", "gy", None),
        P("gx", "gy", None, None),
        P("gx", "gy"),
    )
    out_specs = P("gx", "gy", None, None, None)
    return jax.shard_map(shards, mesh=mesh, in_specs=in_specs, out_specs=out_specs, check_vma=False)
```

```python
import functools

import jax
import jax.numpy as jnp
from jax import lax
from jax.experimental import pallas as pl
from jax.experimental.pallas import tpu as pltpu
from jax.sharding import PartitionSpec as P

ONSITE_S = -0.22
ONSITE_P = 0.27
HOP_SS = -0.37
HOP_SP = 0.35
HOP_PPS = 0.4
HOP_PPP = -0.114
BOND_LENGTH = 1.536
LATTICE_STEP = 1.6

SIDE = 4
DEPTH = 8
ATOMS = SIDE * SIDE * DEPTH
FACE = SIDE * DEPTH
WIDE = FACE + 2 * DEPTH
NV = 256
LANES = NV // 2
POS_ROWS = 9
LIST_ROWS = 6
AUX = 4
BLOCK = DEPTH + AUX
PLACE = (DEPTH, 0, 3 * DEPTH + AUX, 2 * DEPTH + AUX)
X_AUX = 2 * DEPTH
X_SITES = FACE + AUX
Y_BLOCK = (FACE + AUX, FACE + AUX + BLOCK)
Y_SITES = WIDE + 3 * AUX
STEPS = [(x, y) for x in (-1, 0, 1) for y in (-1, 0, 1)]
F32 = jnp.float32
BF16 = jnp.bfloat16


def iota(shape, axis):
    return lax.broadcasted_iota(jnp.int32, shape, axis)


def onehot(values, expected):
    wide = [jnp.where(row == expected, 1.0, 0.0).astype(BF16) for row in values]
    return wide[0] if len(wide) == 1 else jnp.concatenate(wide, axis=1)


def dot_nt(a, b):
    return lax.dot_general(a, b, (((1,), (1,)), ((), ())), preferred_element_type=F32)


def dot(a, b):
    return jnp.dot(a, b, preferred_element_type=F32)


def list_of(rows):
    first = [rows[k : k + 1] for k in range(2)]
    key = [rows[4 + k : 5 + k] * float(ATOMS) + rows[2 + k : 3 + k] for k in range(2)]
    return first, key


def code(step_x, step_y):
    return (step_x + 1) * 3 + step_y + 1


def hopping(dx, dy, dz, count):
    square = jnp.maximum(dx * dx + dy * dy + dz * dz, 0.5)
    inverse = lax.rsqrt(square)
    cosines = [d * inverse for d in (dx, dy, dz)]
    ratio = BOND_LENGTH * inverse
    radial = ratio * ratio * jnp.exp(1.0 - square * inverse * (1.0 / BOND_LENGTH))

    def final(value):
        return (value.astype(BF16).astype(F32) * count).astype(BF16)

    grid = [[None] * 4 for _ in range(4)]
    grid[0][0] = final(HOP_SS * radial)
    for a in range(3):
        across = final(HOP_SP * radial * cosines[a])
        grid[0][1 + a] = across
        grid[1 + a][0] = -across
        for b in range(a, 3):
            entry = (HOP_PPS - HOP_PPP) * cosines[a] * cosines[b]
            if a == b:
                entry = entry + HOP_PPP
            grid[1 + a][1 + b] = grid[1 + b][1 + a] = final(entry * radial)
    return grid


def planes_of(wave, block):
    n = block.shape[0]
    wide = block.astype(F32).reshape(n // 2, 2, 4, NV)
    wide = jnp.concatenate([wide[:, 0], wide[:, 1]], axis=1).reshape(4 * n, NV)
    for h in range(2):
        wave[h, : 4 * n] = wide[:, h * LANES : (h + 1) * LANES]
    halves = [[wave[h, pl.ds(b, n, stride=4), :] for h in range(2)] for b in range(4)]
    return [jnp.concatenate(pair, axis=1) for pair in halves]


def applied(grid, planes):
    total = None
    for b in range(4):
        stacked = jnp.concatenate([grid[a][b] for a in range(4)], axis=0)
        part = dot(stacked, planes[b].astype(BF16))
        total = part if total is None else total + part
    return total


def atoms_of(planes, wave):
    n = planes[0].shape[0]
    for a in range(4):
        for h in range(2):
            wave[h, pl.ds(a, n, stride=4), :] = planes[a][:, h * LANES : (h + 1) * LANES]
    wide = jnp.concatenate([wave[h, : 4 * n] for h in range(2)], axis=1)
    wide = wide.reshape(n // 2, 8, NV)
    return jnp.stack([wide[:, :4], wide[:, 4:]], axis=1).reshape(n, 4, NV)


def turned(points):
    n = points.shape[1]
    return jnp.concatenate([points, jnp.zeros((5, n), F32)], axis=0).T


def picked_rows(pick, points):
    total = None
    for _ in range(3):
        piece = points.astype(BF16)
        part = dot(pick, piece)
        total = part if total is None else total + part
        points = points - piece.astype(F32)
    return total


def z_shift(zi, zj):
    step = zj - zi
    period = LATTICE_STEP * DEPTH
    return jnp.where(step > 1.5, -period, jnp.where(step < -1.5, period, 0.0))


def wrap(place, across, side, period):
    high = jnp.where((side > 0) & (place == across - 1), period, 0.0)
    return jnp.where((side < 0) & (place == 0), -period, high)


def place_of(sizes):
    return lax.axis_index("gx"), lax.axis_index("gy"), *sizes


def side_of(place):
    first = 1 - 2 * (place & 1)
    return first, -first


def faces_of(side):
    mine = jnp.where(side > 0, SIDE - 1, 0)
    return mine, SIDE - 1 - mine


def sum_of(*readers):
    def read(at):
        total = None
        for reader in readers:
            value = reader(at)
            total = value if total is None else total + value
        return total

    return read


def reader_of(message, first=0):
    return lambda at: message[pl.ds(first + at[0], at[1])].astype(F32)


def aux_of(read, first):
    sites = read((first, AUX))
    return jnp.concatenate([sites[k] for k in range(AUX)], axis=0)


def points_of(rows):
    return rows[0:3] + rows[3:6] + rows[6:9]


def pack_x(sizes, trial, positions, atoms, owner, count, one, two, aux, pos, pairs, owners, sem):
    at_x, at_y, across_x, across_y = place_of(sizes)
    copies = [
        pltpu.make_async_copy(a, b, sem.at[k])
        for k, (a, b) in enumerate(((positions, pos), (atoms, pairs), (owner, owners)))
    ]
    for side, out in zip(side_of(at_x), (one, two)):
        face, _ = faces_of(side)
        for y in range(SIDE):
            begin = (face * SIDE + y) * DEPTH
            part = out.at[pl.ds(PLACE[y], DEPTH)]
            copies.append(
                pltpu.make_async_copy(trial.at[pl.ds(begin, DEPTH)], part, sem.at[len(copies)])
            )
    for copy in copies:
        copy.start()
    rows = 3 * SIDE * SIDE
    tile = (iota((DEPTH, ATOMS), 1) & (DEPTH - 1)) == iota((DEPTH, ATOMS), 0)
    tile = jnp.where(tile, 1.0, 0.0).astype(BF16)
    row = iota((3 * rows, ATOMS), 0)
    keep = (row & (SIDE * SIDE - 1)) == (iota((3 * rows, ATOMS), 1) >> 3)
    gather = (iota((16, 3 * rows), 1) >> 4) == iota((16, 3 * rows), 0)
    gather = jnp.where(gather, 1.0, 0.0).astype(BF16)
    aux[:, ATOMS:] = jnp.zeros((4 * AUX, NV - ATOMS), F32)
    for copy in copies[:3]:
        copy.wait()
    rest = pos[...]
    parts = []
    for _ in range(3):
        piece = rest.astype(BF16)
        parts.append(piece)
        rest = rest - piece.astype(F32)
    spread = dot(jnp.concatenate(parts, axis=0), tile)
    aux[:, :ATOMS] = dot(gather, jnp.where(keep, spread, 0.0).astype(BF16))
    whose = owners[...]
    step = jnp.zeros(whose.shape, F32)
    for x, y in STEPS:
        name = lax.rem(at_x + x + across_x, across_x) * across_y
        name = name + lax.rem(at_y + y + across_y, across_y)
        step = jnp.where(whose == name, float(code(x, y)), step)
    live = iota(whose.shape, 1) < count[0, 0]
    first = jnp.where(live, pairs[0:1], -1).astype(F32)
    second = pairs[1:2].astype(F32)
    for k, values in enumerate((first, second, step)):
        for h in range(2):
            at = POS_ROWS + 2 * k + h
            aux[at : at + 1] = values[:, h * NV : (h + 1) * NV]
    for k in range(AUX):
        site = aux[4 * k : 4 * k + 4].astype(BF16)
        for out in (one, two):
            out[X_AUX + k] = site
    for copy in copies[3:]:
        copy.wait()


def own(sizes, trial, aux, acc, low, two, top, wave):
    first, second = side_of(place_of(sizes)[1])
    for side, outs in ((first, (low, top)), (second, (two,))):
        face, _ = faces_of(side)
        for out in outs:
            for x in range(SIDE):
                begin = (x * SIDE + face) * DEPTH
                out[x * DEPTH : (x + 1) * DEPTH] = trial[pl.ds(begin, DEPTH)]
            for k in range(AUX):
                out[FACE + k] = aux[4 * k : 4 * k + 4].astype(BF16)
    rows = aux[...]
    first, key = list_of(rows[POS_ROWS : POS_ROWS + LIST_ROWS])
    atom = iota((ATOMS, 1), 0)
    is_first = onehot(first, atom.astype(F32))
    is_second = onehot(key, (atom + code(0, 0) * ATOMS).astype(F32))
    count = dot_nt(is_first, is_second) + dot_nt(is_second, is_first)
    pos = points_of(rows)[:, :ATOMS]
    pos_t = turned(pos)
    zi = (atom & (DEPTH - 1)).astype(F32)
    zj = (iota((1, ATOMS), 1) & (DEPTH - 1)).astype(F32)
    dx, dy = (pos[a : a + 1] - pos_t[:, a : a + 1] for a in range(2))
    dz = (pos[2:3] + z_shift(zi, zj)) - pos_t[:, 2:3]
    grid = hopping(dx, dy, dz, count)
    planes = planes_of(wave, trial[...])
    matrix = jnp.concatenate([jnp.concatenate(line, axis=1) for line in grid], axis=0)
    part = dot(matrix, jnp.concatenate(planes, axis=0).astype(BF16))
    for a in range(4):
        onsite = ONSITE_P if a else ONSITE_S
        rows = slice(a * ATOMS, (a + 1) * ATOMS)
        acc[rows] = onsite * planes[a] + part[rows]


def corners(sizes, x_two, x_one, low_in, two_in, top_in, low, two, top, sem):
    del low_in, two_in, top_in
    first, second = side_of(place_of(sizes)[1])
    copies = []
    for side, out in ((first, low), (second, two), (first, top)):
        face, _ = faces_of(side)
        begin = jnp.where(face == 0, PLACE[0], X_AUX)
        for n, message in enumerate((x_one, x_two)):
            part = out.at[pl.ds(Y_BLOCK[n], BLOCK)]
            copies.append(
                pltpu.make_async_copy(message.at[pl.ds(begin, BLOCK)], part, sem.at[len(copies)])
            )
            copies[-1].start()
    for copy in copies:
        copy.wait()


def own_of(aux):
    rows = aux[...]
    return *list_of(rows[POS_ROWS : POS_ROWS + LIST_ROWS]), turned(points_of(rows)[:, :ATOMS])


def pick_rows(atom, pos_t):
    return picked_rows(jnp.where(iota((FACE, ATOMS), 1) == atom, 1.0, 0.0).astype(BF16), pos_t)


def x_part(period, sizes, side, read, own_first, own_key, pos_t, wave):
    at_x, _, across_x, _ = place_of(sizes)
    mine, theirs = faces_of(side)
    k = iota((FACE, 1), 0)
    my_atom = mine * FACE + k
    their_atom = theirs * FACE + (k ^ DEPTH)
    rows = aux_of(read, X_AUX)
    first, key = list_of(rows[POS_ROWS : POS_ROWS + LIST_ROWS])
    left = [
        onehot(own_first, my_atom.astype(F32)),
        onehot(key, (my_atom + ((1 - side) * 3 + 1) * ATOMS).astype(F32)),
    ]
    right = [
        onehot(own_key, (their_atom + ((side + 1) * 3 + 1) * ATOMS).astype(F32)),
        onehot(first, their_atom.astype(F32)),
    ]
    count = dot_nt(jnp.concatenate(left, axis=1), jnp.concatenate(right, axis=1))
    lane = theirs * FACE + (iota((ATOMS, FACE), 1) ^ DEPTH)
    pick = jnp.where(iota((ATOMS, FACE), 0) == lane, 1.0, 0.0).astype(BF16)
    points = points_of(dot(rows[:, :ATOMS].astype(BF16), pick))
    mine_t = pick_rows(my_atom, pos_t)
    zi = (k & (DEPTH - 1)).astype(F32)
    zj = (iota((1, FACE), 1) & (DEPTH - 1)).astype(F32)
    dx = (points[0:1] + wrap(at_x, across_x, side, period)) - mine_t[:, 0:1]
    dy = points[1:2] - mine_t[:, 1:2]
    dz = (points[2:3] + z_shift(zi, zj)) - mine_t[:, 2:3]
    grid = hopping(dx, dy, dz, count)
    half = 2 * DEPTH
    block = jnp.concatenate([read((0, half)), read((half + AUX, half))], axis=0)
    return applied(grid, planes_of(wave, block))


def ghost(theirs, x_sides, shape, axis):
    at = iota(shape, axis)
    part = jnp.where(at < FACE, 0, jnp.where(at < FACE + DEPTH, 1, 2))
    step = jnp.where(part == 0, 0, jnp.where(part == 1, x_sides[0], x_sides[1]))
    layer = jnp.where(part == 0, at >> 3, jnp.where(step > 0, 0, SIDE - 1))
    return layer * FACE + theirs * DEPTH + (at & (DEPTH - 1)), step, part


def y_atoms(side):
    mine, _ = faces_of(side)
    k = iota((FACE, 1), 0)
    return (k >> 3) * FACE + mine * DEPTH + (k & (DEPTH - 1))


def first_half(periods, sizes, aux, x_two, x_one, acc_in, acc, forward, mine_y, wave, other_wave):
    at_x, at_y, _, _ = place_of(sizes)
    own_first, own_key, pos_t = own_of(aux)
    x_sides = side_of(at_x)
    parts = [
        x_part(periods[0], sizes, side, reader_of(message), own_first, own_key, pos_t, scratch)
        for side, message, scratch in zip(x_sides, (x_one, x_two), (wave, other_wave))
    ]
    for n, side in enumerate(side_of(at_y)):
        _, theirs = faces_of(side)
        my_atom = y_atoms(side)
        their_atom, step, _ = ghost(theirs, x_sides, (WIDE, 1), 0)
        target = their_atom + ((step + 1) * 3 + side + 1) * ATOMS
        left = onehot(own_first, my_atom.astype(F32))
        forward[n] = dot_nt(left, onehot(own_key, target.astype(F32)))
        mine_y[n] = pick_rows(my_atom, pos_t)
    acc[...] = acc_in[...]
    for side, part in zip(x_sides, parts):
        mine, _ = faces_of(side)
        for a in range(4):
            at = pl.multiple_of(a * ATOMS + mine * FACE, FACE)
            acc[pl.ds(at, FACE)] += part[a * FACE : (a + 1) * FACE]


def y_part(periods, sizes, side, read, forward, mine_t, wave):
    at_x, at_y, across_x, across_y = place_of(sizes)
    _, theirs = faces_of(side)
    x_sides = side_of(at_x)
    corner_at = jnp.where(theirs == 0, 0, AUX)
    aux_at = jnp.where(theirs == 0, DEPTH, 0)
    my_atom = y_atoms(side)
    their_atom, _, part = ghost(theirs, x_sides, (WIDE, 1), 0)
    lane_atom, _, lane_part = ghost(theirs, x_sides, (ATOMS, WIDE), 1)
    left, right, picks, placed = [], [], [], []
    for m, x in enumerate((0, *x_sides)):
        rows = aux_of(read, Y_BLOCK[m - 1] + aux_at if m else FACE)
        listed, key = list_of(rows[POS_ROWS : POS_ROWS + LIST_ROWS])
        wanted = my_atom + ((1 - x) * 3 + 1 - side) * ATOMS
        left.append(onehot(key, wanted.astype(F32)))
        right.append(onehot(listed, jnp.where(part == m, their_atom, -2).astype(F32)))
        pick = (iota((ATOMS, WIDE), 0) == lane_atom) & (lane_part == m)
        picks.append(jnp.where(pick, 1.0, 0.0).astype(BF16))
        placed.append(rows[:, :ATOMS].astype(BF16))
    count = forward + dot_nt(jnp.concatenate(left, axis=1), jnp.concatenate(right, axis=1))
    points = points_of(dot(jnp.concatenate(placed, axis=1), jnp.concatenate(picks, axis=0)))
    lane = iota((1, WIDE), 1)
    zi = (iota((FACE, 1), 0) & (DEPTH - 1)).astype(F32)
    zj = (lane & (DEPTH - 1)).astype(F32)
    shifts = [wrap(at_x, across_x, x, periods[0]) for x in x_sides]
    shift_x = jnp.where(lane < FACE, 0.0, jnp.where(lane < FACE + DEPTH, *shifts))
    dx = (points[0:1] + shift_x) - mine_t[:, 0:1]
    dy = (points[1:2] + wrap(at_y, across_y, side, periods[1])) - mine_t[:, 1:2]
    dz = (points[2:3] + z_shift(zi, zj)) - mine_t[:, 2:3]
    grid = hopping(dx, dy, dz, count)
    block = [read((0, FACE))] + [read((Y_BLOCK[m] + corner_at, DEPTH)) for m in range(2)]
    return applied(grid, planes_of(wave, jnp.concatenate(block, axis=0)))


def y_rows(side):
    mine, _ = faces_of(side)
    return [(x * SIDE + mine) * DEPTH for x in range(SIDE)]


def second_half(periods, sizes, forward, mine_y, acc, low, faces, done, sums, wave, store):
    sides = side_of(place_of(sizes)[1])
    part = y_part(periods, sizes, sides[0], reader_of(low), forward[0], mine_y[0], wave)
    sums[...] = acc[...]
    for a in range(4):
        for x, row in enumerate(y_rows(sides[0])):
            at = pl.multiple_of(a * ATOMS + row, DEPTH)
            begin = a * FACE + x * DEPTH
            sums[pl.ds(at, DEPTH)] += part[begin : begin + DEPTH]
    done[...] = atoms_of([sums[a * ATOMS : (a + 1) * ATOMS] for a in range(4)], store)
    for n, side in enumerate(sides):
        for a in range(4):
            for x, row in enumerate(y_rows(side)):
                at = pl.multiple_of(a * ATOMS + row, DEPTH)
                begin = a * FACE + x * DEPTH
                faces[n, begin : begin + DEPTH] = sums[pl.ds(at, DEPTH)]


def last_face(periods, sizes, forward, mine_y, faces, done, two, top, out, results, wave, store, sem):
    _, at_y, _, across_y = place_of(sizes)
    lower = at_y < across_y // 4 * 2
    sides = side_of(at_y)
    copies = []

    def copy_of(source, begin, row, count):
        return pltpu.make_async_copy(
            source.at[pl.ds(begin, count)], out.at[pl.ds(row, count)], sem.at[len(copies)]
        )

    def total_of(n, message, scratch):
        read = reader_of(message)
        part = faces[n] + y_part(periods, sizes, sides[n], read, forward[n], mine_y[n], scratch)
        return atoms_of([part[a * FACE : (a + 1) * FACE] for a in range(4)], scratch)

    for x in range(SIDE):
        row = x * FACE + DEPTH
        copies.append(copy_of(done, row, row, FACE - 2 * DEPTH))
        copies[-1].start()
    for row in y_rows(sides[0]):
        copies.append(copy_of(done, row, row, DEPTH))
    firsts = copies[SIDE:]

    @pl.when(lower)
    def _():
        for copy in firsts:
            copy.start()

    results[1] = total_of(1, two, wave)
    for x, row in enumerate(y_rows(sides[1])):
        copies.append(copy_of(results.at[1], x * DEPTH, row, DEPTH))
        copies[-1].start()

    @pl.when(jnp.logical_not(lower))
    def _():
        results[0] = total_of(0, top, store)
        for x, row in enumerate(y_rows(sides[0])):
            pltpu.make_async_copy(
                results.at[0, pl.ds(x * DEPTH, DEPTH)],
                out.at[pl.ds(row, DEPTH)],
                sem.at[SIDE + x],
            ).start()

    for copy in copies:
        copy.wait()


def swap(count, begin):
    pairs = []
    for i in range(begin, count + begin, 2):
        a, b = i % count, (i + 1) % count
        pairs += [(a, b), (b, a)]
    return pairs


def exchange_x(one, two):
    count = lax.axis_size("gx")
    two = lax.ppermute(two, "gx", swap(count, 1))
    one = lax.ppermute(one, "gx", swap(count, 0))
    return one, two


def exchange_y(low, two, top):
    count = lax.axis_size("gy")
    pairs = swap(count, 0)
    begin = count // 4 * 2
    low = lax.ppermute(low, "gy", pairs[:begin])
    two = lax.ppermute(two, "gy", swap(count, 1))
    top = lax.ppermute(top, "gy", pairs[begin:])
    return low, two, top


VMEM = pl.BlockSpec(memory_space=pltpu.VMEM)
SMEM = pl.BlockSpec(memory_space=pltpu.SMEM)
HBM = pl.BlockSpec(memory_space=pltpu.HBM)
ANY = pl.BlockSpec(memory_space=pl.ANY)


def call(kernel, inputs, outputs, in_space=VMEM, out_space=VMEM, **options):
    return pl.pallas_call(
        kernel,
        out_shape=outputs,
        in_specs=in_space if isinstance(in_space, list) else [in_space] * len(inputs),
        out_specs=[out_space] * len(outputs),
        compiler_params=pltpu.CompilerParams(vmem_limit_bytes=16 * 1024 * 1024),
        **options,
    )(*inputs)


def shards(trial, positions, pair_atoms, pair_owner, pair_image, pair_count):
    sizes = across_x, across_y = lax.axis_size("gx"), lax.axis_size("gy")
    periods = tuple(LATTICE_STEP * (SIDE * count) for count in sizes)
    mine = trial.reshape(ATOMS, 4, NV)
    slots = pair_owner.shape[2]

    def message(sites):
        return jax.ShapeDtypeStruct((sites, 4, NV), BF16)

    def floats(*shape):
        return jax.ShapeDtypeStruct(shape, F32)

    def wave(rows):
        return pltpu.VMEM((2, rows, LANES), F32)

    *x_out, aux = call(
        functools.partial(pack_x, sizes),
        tuple(
            pltpu.with_memory_space_constraint(array, pltpu.HBM)
            for array in (
                mine,
                positions.reshape(3 * SIDE * SIDE, DEPTH),
                pair_atoms.reshape(2, slots),
                pair_owner.reshape(1, slots),
            )
        )
        + (pair_count,),
        [message(X_SITES)] * 2 + [floats(4 * AUX, NV)],
        in_space=[HBM] * 4 + [SMEM],
        scratch_shapes=[
            pltpu.VMEM((3 * SIDE * SIDE, DEPTH), F32),
            pltpu.VMEM((2, slots), jnp.int32),
            pltpu.VMEM((1, slots), jnp.int32),
            pltpu.SemaphoreType.DMA((3 + 2 * SIDE,)),
        ],
    )
    x_one, x_two = exchange_x(*x_out)
    acc, *y_out = call(
        functools.partial(own, sizes),
        (mine, aux),
        [floats(4 * ATOMS, NV)] + [message(Y_SITES)] * 3,
        scratch_shapes=[wave(4 * ATOMS)],
    )
    y_out = call(
        functools.partial(corners, sizes),
        (x_two, x_one, *y_out),
        [message(Y_SITES)] * 3,
        in_space=ANY,
        out_space=ANY,
        input_output_aliases={2: 0, 3: 1, 4: 2},
        scratch_shapes=[pltpu.SemaphoreType.DMA((6,))],
    )
    low, two, top = exchange_y(*y_out)
    acc, forward, mine_y = call(
        functools.partial(first_half, periods, sizes),
        (aux, x_two, x_one, acc),
        [floats(4 * ATOMS, NV), floats(2, FACE, WIDE), floats(2, FACE, 8)],
        scratch_shapes=[wave(4 * FACE)] * 2,
    )
    faces, done = call(
        functools.partial(second_half, periods, sizes),
        (forward, mine_y, acc, low),
        [floats(2, 4 * FACE, NV), floats(ATOMS, 4, NV)],
        scratch_shapes=[
            pltpu.VMEM((4 * ATOMS, NV), F32),
            wave(4 * WIDE),
            wave(4 * ATOMS),
        ],
    )
    (product,) = call(
        functools.partial(last_face, periods, sizes),
        (forward, mine_y, faces, done, two, top),
        [floats(ATOMS, 4, NV)],
        out_space=HBM,
        scratch_shapes=[
            pltpu.VMEM((2, FACE, 4, NV), F32),
            wave(4 * WIDE),
            wave(4 * WIDE),
            pltpu.SemaphoreType.DMA((3 * SIDE,)),
        ],
    )
    return product.reshape(trial.shape)


def solution(mesh):
    in_specs = (
        P("gx", "gy", None, None, None),
        P(None, "gx", "gy", None),
        P("gx", "gy", None, None),
        P("gx", "gy", None),
        P("gx", "gy", None, None),
        P("gx", "gy"),
    )
    out_specs = P("gx", "gy", None, None, None)
    return jax.shard_map(shards, mesh=mesh, in_specs=in_specs, out_specs=out_specs, check_vma=False)
```

```python
import functools

import jax
import jax.numpy as jnp
from jax import lax
from jax.experimental import pallas as pl
from jax.experimental.pallas import tpu as pltpu
from jax.sharding import PartitionSpec as P

ONSITE_S = -0.22
ONSITE_P = 0.27
HOP_SS = -0.37
HOP_SP = 0.35
HOP_PPS = 0.4
HOP_PPP = -0.114
BOND_LENGTH = 1.536
LATTICE_STEP = 1.6

SIDE = 4
DEPTH = 8
ATOMS = SIDE * SIDE * DEPTH
FACE = SIDE * DEPTH
WIDE = FACE + 2 * DEPTH
NV = 256
LANES = NV // 2
POS_ROWS = 9
LIST_ROWS = 6
AUX = 4
Y_PLACE = (DEPTH, 0, 3 * DEPTH + AUX, 2 * DEPTH + AUX)
Y_AUX = 2 * DEPTH
Y_SITES = FACE + AUX
BLOCK = DEPTH + AUX
X_BLOCK = (FACE + AUX, FACE + AUX + BLOCK)
X_SITES = WIDE + 3 * AUX
STEPS = [(x, y) for x in (-1, 0, 1) for y in (-1, 0, 1)]
F32 = jnp.float32
BF16 = jnp.bfloat16


def iota(shape, axis):
    return lax.broadcasted_iota(jnp.int32, shape, axis)


def onehot(values, expected):
    wide = [jnp.where(row == expected, 1.0, 0.0).astype(BF16) for row in values]
    return wide[0] if len(wide) == 1 else jnp.concatenate(wide, axis=1)


def dot_nt(a, b):
    return lax.dot_general(a, b, (((1,), (1,)), ((), ())), preferred_element_type=F32)


def dot(a, b):
    return jnp.dot(a, b, preferred_element_type=F32)


def list_of(rows):
    first = [rows[k : k + 1] for k in range(2)]
    key = [rows[4 + k : 5 + k] * float(ATOMS) + rows[2 + k : 3 + k] for k in range(2)]
    return first, key


def code(step_x, step_y):
    return (step_x + 1) * 3 + step_y + 1


def hopping(dx, dy, dz, count):
    square = jnp.maximum(dx * dx + dy * dy + dz * dz, 0.5)
    inverse = lax.rsqrt(square)
    cosines = [d * inverse for d in (dx, dy, dz)]
    ratio = BOND_LENGTH * inverse
    radial = ratio * ratio * jnp.exp(1.0 - square * inverse * (1.0 / BOND_LENGTH))

    def final(value):
        return (value.astype(BF16).astype(F32) * count).astype(BF16)

    grid = [[None] * 4 for _ in range(4)]
    grid[0][0] = final(HOP_SS * radial)
    for a in range(3):
        across = final(HOP_SP * radial * cosines[a])
        grid[0][1 + a] = across
        grid[1 + a][0] = -across
        for b in range(a, 3):
            entry = (HOP_PPS - HOP_PPP) * cosines[a] * cosines[b]
            if a == b:
                entry = entry + HOP_PPP
            grid[1 + a][1 + b] = grid[1 + b][1 + a] = final(entry * radial)
    return grid


def planes_of(wave, block):
    n = block.shape[0]
    wide = block.astype(F32).reshape(n // 2, 2, 4, NV)
    wide = jnp.concatenate([wide[:, 0], wide[:, 1]], axis=1).reshape(4 * n, NV)
    for h in range(2):
        wave[h, : 4 * n] = wide[:, h * LANES : (h + 1) * LANES]
    halves = [[wave[h, pl.ds(b, n, stride=4), :] for h in range(2)] for b in range(4)]
    return [jnp.concatenate(pair, axis=1) for pair in halves]


def applied(grid, planes):
    total = None
    for b in range(4):
        stacked = jnp.concatenate([grid[a][b] for a in range(4)], axis=0)
        part = dot(stacked, planes[b].astype(BF16))
        total = part if total is None else total + part
    return total


def atoms_of(planes, wave):
    n = planes[0].shape[0]
    for a in range(4):
        for h in range(2):
            wave[h, pl.ds(a, n, stride=4), :] = planes[a][:, h * LANES : (h + 1) * LANES]
    wide = jnp.concatenate([wave[h, : 4 * n] for h in range(2)], axis=1)
    wide = wide.reshape(n // 2, 8, NV)
    return jnp.stack([wide[:, :4], wide[:, 4:]], axis=1).reshape(n, 4, NV)


def turned(points):
    n = points.shape[1]
    return jnp.concatenate([points, jnp.zeros((5, n), F32)], axis=0).T


def picked_rows(pick, points):
    total = None
    for _ in range(3):
        piece = points.astype(BF16)
        part = dot(pick, piece)
        total = part if total is None else total + part
        points = points - piece.astype(F32)
    return total


def z_shift(zi, zj):
    step = zj - zi
    period = LATTICE_STEP * DEPTH
    return jnp.where(step > 1.5, -period, jnp.where(step < -1.5, period, 0.0))


def wrap(place, across, side, period):
    high = jnp.where((side > 0) & (place == across - 1), period, 0.0)
    return jnp.where((side < 0) & (place == 0), -period, high)


def place_of(sizes):
    return lax.axis_index("gx"), lax.axis_index("gy"), *sizes


def side_of(place):
    first = 1 - 2 * (place & 1)
    return first, -first


def faces_of(side):
    mine = jnp.where(side > 0, SIDE - 1, 0)
    return mine, SIDE - 1 - mine


def sum_of(*readers):
    def read(at):
        total = None
        for reader in readers:
            value = reader(at)
            total = value if total is None else total + value
        return total

    return read


def reader_of(message, first=0):
    return lambda at: message[pl.ds(first + at[0], at[1])].astype(F32)


def aux_of(read, first):
    sites = read((first, AUX))
    return jnp.concatenate([sites[k] for k in range(AUX)], axis=0)


def points_of(rows):
    return rows[0:3] + rows[3:6] + rows[6:9]


def pack_y(sizes, trial, positions, atoms, owner, count, *refs):
    low, two, top, over, over_up, over_down, aux, pos, pairs, owners, sem = refs
    at_x, at_y, across_x, across_y = place_of(sizes)
    copies = [
        pltpu.make_async_copy(a, b, sem.at[k])
        for k, (a, b) in enumerate(((positions, pos), (atoms, pairs), (owner, owners)))
    ]
    faces = [faces_of(side)[0] for side in side_of(at_y)]
    moves = [
        (x, faces[n], out.at[pl.ds(begin + Y_PLACE[x], DEPTH)])
        for n, out, begin in (
            (0, low, 0),
            (1, two, 0),
            (0, top, 0),
            (1, over, 0),
        )
        for x in range(SIDE)
    ]
    moves.append((SIDE - 1, faces[1], over_up.at[pl.ds(AUX, DEPTH)]))
    moves.append((0, faces[1], over_down.at[pl.ds(0, DEPTH)]))
    for x, face, out in moves:
        begin = (x * SIDE + face) * DEPTH
        copies.append(
            pltpu.make_async_copy(trial.at[pl.ds(begin, DEPTH)], out, sem.at[len(copies)])
        )
    for copy in copies:
        copy.start()
    rows = 3 * SIDE * SIDE
    tile = (iota((DEPTH, ATOMS), 1) & (DEPTH - 1)) == iota((DEPTH, ATOMS), 0)
    tile = jnp.where(tile, 1.0, 0.0).astype(BF16)
    row = iota((3 * rows, ATOMS), 0)
    keep = (row & (SIDE * SIDE - 1)) == (iota((3 * rows, ATOMS), 1) >> 3)
    gather = (iota((16, 3 * rows), 1) >> 4) == iota((16, 3 * rows), 0)
    gather = jnp.where(gather, 1.0, 0.0).astype(BF16)
    aux[:, ATOMS:] = jnp.zeros((4 * AUX, NV - ATOMS), F32)
    for copy in copies[:3]:
        copy.wait()
    rest = pos[...]
    parts = []
    for _ in range(3):
        piece = rest.astype(BF16)
        parts.append(piece)
        rest = rest - piece.astype(F32)
    spread = dot(jnp.concatenate(parts, axis=0), tile)
    aux[:, :ATOMS] = dot(gather, jnp.where(keep, spread, 0.0).astype(BF16))
    whose = owners[...]
    step = jnp.zeros(whose.shape, F32)
    for x, y in STEPS:
        name = lax.rem(at_x + x + across_x, across_x) * across_y
        name = name + lax.rem(at_y + y + across_y, across_y)
        step = jnp.where(whose == name, float(code(x, y)), step)
    live = iota(whose.shape, 1) < count[0, 0]
    first = jnp.where(live, pairs[0:1], -1).astype(F32)
    second = pairs[1:2].astype(F32)
    for k, values in enumerate((first, second, step)):
        for h in range(2):
            at = POS_ROWS + 2 * k + h
            aux[at : at + 1] = values[:, h * NV : (h + 1) * NV]
    places = [(out, Y_AUX) for out in (low, two, top, over)]
    places += [(over_up, 0), (over_down, DEPTH)]
    for k in range(AUX):
        site = aux[4 * k : 4 * k + 4].astype(BF16)
        for out, at in places:
            out[at + k] = site
    for copy in copies[3:]:
        copy.wait()


def own(trial, aux, acc, wave):
    rows = aux[...]
    first, key = list_of(rows[POS_ROWS : POS_ROWS + LIST_ROWS])
    atom = iota((ATOMS, 1), 0)
    is_first = onehot(first, atom.astype(F32))
    is_second = onehot(key, (atom + code(0, 0) * ATOMS).astype(F32))
    count = dot_nt(is_first, is_second) + dot_nt(is_second, is_first)
    pos = points_of(rows)[:, :ATOMS]
    pos_t = turned(pos)
    zi = (atom & (DEPTH - 1)).astype(F32)
    zj = (iota((1, ATOMS), 1) & (DEPTH - 1)).astype(F32)
    dx, dy = (pos[a : a + 1] - pos_t[:, a : a + 1] for a in range(2))
    dz = (pos[2:3] + z_shift(zi, zj)) - pos_t[:, 2:3]
    grid = hopping(dx, dy, dz, count)
    planes = planes_of(wave, trial[...])
    matrix = jnp.concatenate([jnp.concatenate(line, axis=1) for line in grid], axis=0)
    part = dot(matrix, jnp.concatenate(planes, axis=0).astype(BF16))
    for a in range(4):
        onsite = ONSITE_P if a else ONSITE_S
        rows = slice(a * ATOMS, (a + 1) * ATOMS)
        acc[rows] = onsite * planes[a] + part[rows]


def corners(sizes, late, *refs):
    _, *inputs, one, two, sem = refs
    if late:
        over, y_one, y_two, trial, message = inputs
    else:
        y_two, y_one, trial, message = inputs
    at_x, at_y, _, across_y = place_of(sizes)
    copies = []

    def copy_of(source, begin, count, out, at):
        return pltpu.make_async_copy(
            source.at[pl.ds(begin, count)], out.at[pl.ds(at, count)], sem.at[len(copies)]
        )

    for side, out in zip(side_of(at_x), (one, two)):
        face, _ = faces_of(side)
        begin = jnp.where(face == 0, Y_PLACE[0], Y_AUX)
        for given in (
            (trial, face * FACE, FACE, out, 0),
            (message, Y_AUX, AUX, out, FACE),
            (y_one, begin, BLOCK, out, X_BLOCK[0]),
        ):
            copies.append(copy_of(*given))
            copies[-1].start()
        plain = copy_of(y_two, begin, BLOCK, out, X_BLOCK[1])
        if late:
            other = copy_of(over, begin, BLOCK, out, X_BLOCK[1])

            @pl.when(at_y == across_y - 1)
            def _():
                other.start()

            @pl.when(at_y != across_y - 1)
            def _():
                plain.start()
        else:
            plain.start()
        copies.append(plain)
    for copy in copies:
        copy.wait()


def crossed(sizes, over, up, down, one, two, sem):
    del over
    copies = []
    for n, (side, out) in enumerate(zip(side_of(place_of(sizes)[0]), (one, two))):
        low, high = (pltpu.make_async_copy(source.at[pl.ds(0, BLOCK)], out, sem.at[n]) for source in (up, down))

        @pl.when(side < 0)
        def _():
            low.start()

        @pl.when(side > 0)
        def _():
            high.start()

        copies.append(low)
    for copy in copies:
        copy.wait()


def hand_on(after, over, top, back, top_out, sem):
    del after
    copies = [
        pltpu.make_async_copy(over, back, sem.at[0]),
        pltpu.make_async_copy(top, top_out, sem.at[1]),
    ]
    for copy in copies:
        copy.start()
    for copy in copies:
        copy.wait()


def settle(y_two, y_low, out):
    del y_two, y_low
    out[...] = jnp.zeros_like(out)


def blank(*_):
    pass


def own_of(aux):
    rows = aux[...]
    return *list_of(rows[POS_ROWS : POS_ROWS + LIST_ROWS]), turned(points_of(rows)[:, :ATOMS])


def y_atoms(side):
    mine, theirs = faces_of(side)
    k = iota((FACE, 1), 0)
    z = k & (DEPTH - 1)
    line = (k >> 3) * (SIDE * DEPTH) + z
    crossed = ((k >> 3) ^ 1) * (SIDE * DEPTH) + z
    return line + mine * DEPTH, crossed + theirs * DEPTH


def y_ahead(side, own_first, own_key, pos_t):
    my_atom, their_atom = y_atoms(side)
    left = onehot(own_first, my_atom.astype(F32))
    right = onehot(own_key, (their_atom + (4 + side) * ATOMS).astype(F32))
    pick = jnp.where(iota((FACE, ATOMS), 1) == my_atom, 1.0, 0.0).astype(BF16)
    return dot_nt(left, right), picked_rows(pick, pos_t)


def y_part(period, sizes, side, read, forward, mine_t, wave):
    _, at_y, _, across_y = place_of(sizes)
    _, theirs = faces_of(side)
    my_atom, their_atom = y_atoms(side)
    rows = aux_of(read, Y_AUX)
    first, key = list_of(rows[POS_ROWS : POS_ROWS + LIST_ROWS])
    left = onehot(key, (my_atom + (4 - side) * ATOMS).astype(F32))
    count = forward + dot_nt(left, onehot(first, their_atom.astype(F32)))
    lane = iota((ATOMS, FACE), 1)
    lane = ((lane >> 3) ^ 1) * (SIDE * DEPTH) + (lane & (DEPTH - 1)) + theirs * DEPTH
    pick = jnp.where(iota((ATOMS, FACE), 0) == lane, 1.0, 0.0).astype(BF16)
    points = points_of(dot(rows[:, :ATOMS].astype(BF16), pick))
    zi = (iota((FACE, 1), 0) & (DEPTH - 1)).astype(F32)
    zj = (iota((1, FACE), 1) & (DEPTH - 1)).astype(F32)
    dx = points[0:1] - mine_t[:, 0:1]
    dy = (points[1:2] + wrap(at_y, across_y, side, period)) - mine_t[:, 1:2]
    dz = (points[2:3] + z_shift(zi, zj)) - mine_t[:, 2:3]
    grid = hopping(dx, dy, dz, count)
    half = 2 * DEPTH
    block = jnp.concatenate([read((0, half)), read((half + AUX, half))], axis=0)
    return applied(grid, planes_of(wave, block))


def y_add(acc, side, part):
    mine, _ = faces_of(side)
    for a in range(4):
        for x in range(SIDE):
            at = pl.multiple_of(a * ATOMS + (x * SIDE + mine) * DEPTH, DEPTH)
            begin = a * FACE + x * DEPTH
            acc[pl.ds(at, DEPTH)] += part[begin : begin + DEPTH]


def ghost(theirs, y_sides, shape, axis):
    at = iota(shape, axis)
    part = jnp.where(at < FACE, 0, jnp.where(at < FACE + DEPTH, 1, 2))
    step = jnp.where(part == 0, 0, jnp.where(part == 1, y_sides[0], y_sides[1]))
    row = jnp.where(step > 0, 0, (SIDE - 1) * DEPTH)
    atom = theirs * FACE + jnp.where(part == 0, at, row + (at & (DEPTH - 1)))
    return atom, step, part


def first_half(periods, sizes, aux, message, acc_in, acc, wave):
    side = side_of(place_of(sizes)[1])[0]
    forward, mine_t = y_ahead(side, *own_of(aux))
    acc[...] = acc_in[...]
    y_add(acc, side, y_part(periods[1], sizes, side, reader_of(message), forward, mine_t, wave))


def second_half(periods, sizes, late, *refs):
    _, at_y, _, across_y = place_of(sizes)
    mine = at_y < across_y // 4 * 2
    if late:
        _, *refs = refs
        mine = jnp.logical_not(mine)

    @pl.when(mine)
    def _():
        finish(periods, sizes, late, *refs)


def finish(periods, sizes, late, aux, y_two, other, *refs):
    beside, given, acc_in = refs[:2], refs[2:4], refs[4]
    out, acc, wave, one_wave, two_wave, result, x_messages, sem, x_sem = refs[5:]
    at_x, at_y, across_x, across_y = place_of(sizes)
    arrivals = []
    if late:
        x_messages = given[1], given[0]
    else:
        x_messages = x_messages.at[0], x_messages.at[1]
        arrivals = [
            pltpu.make_async_copy(source, target, x_sem.at[n])
            for n, (source, target) in enumerate(zip(given, x_messages[::-1]))
        ]
    for arrival in arrivals:
        arrival.start()
    acc[...] = acc_in[...]
    own_first, own_key, pos_t = own_of(aux)
    y_sides = side_of(at_y)
    x_sides = side_of(at_x)

    read = sum_of(reader_of(y_two), reader_of(other))
    forward_y, mine_y = y_ahead(y_sides[1], own_first, own_key, pos_t)
    added = y_part(periods[1], sizes, y_sides[1], read, forward_y, mine_y, wave)
    k = iota((FACE, 1), 0)
    zi = (k & (DEPTH - 1)).astype(F32)
    lane = iota((1, WIDE), 1)
    zj = (lane & (DEPTH - 1)).astype(F32)
    shifts = [wrap(at_y, across_y, y, periods[1]) for y in y_sides]
    shift_y = jnp.where(lane < FACE, 0.0, jnp.where(lane < FACE + DEPTH, *shifts))
    parts = []
    for arrival in arrivals:
        arrival.wait()
    for n, side in enumerate(x_sides):
        mine, theirs = faces_of(side)
        corner_at = jnp.where(theirs == 0, 0, AUX)
        aux_at = jnp.where(theirs == 0, DEPTH, 0)
        plain = reader_of(x_messages[n])

        def second(at, plain=plain, other=reader_of(beside[n])):
            return plain((X_BLOCK[1] + at[0], at[1])) + other(at)

        def first(at, plain=plain):
            return plain((X_BLOCK[0] + at[0], at[1]))

        my_atom = k + mine * FACE
        their_atom, step, part = ghost(theirs, y_sides, (WIDE, 1), 0)
        target = their_atom + ((side + 1) * 3 + step + 1) * ATOMS
        lane_atom, _, lane_part = ghost(theirs, y_sides, (ATOMS, WIDE), 1)
        left = [onehot(own_first, my_atom.astype(F32))]
        right = [onehot(own_key, target.astype(F32))]
        picks, placed = [], []
        for m, y in enumerate((0, *y_sides)):
            rows = aux_of((plain, first, second)[m], aux_at if m else FACE)
            listed, key = list_of(rows[POS_ROWS : POS_ROWS + LIST_ROWS])
            wanted = my_atom + ((1 - side) * 3 + 1 - y) * ATOMS
            left.append(onehot(key, wanted.astype(F32)))
            right.append(onehot(listed, jnp.where(part == m, their_atom, -2).astype(F32)))
            pick = (iota((ATOMS, WIDE), 0) == lane_atom) & (lane_part == m)
            picks.append(jnp.where(pick, 1.0, 0.0).astype(BF16))
            placed.append(rows[:, :ATOMS].astype(BF16))
        count = dot_nt(jnp.concatenate(left, axis=1), jnp.concatenate(right, axis=1))
        points = dot(jnp.concatenate(placed, axis=1), jnp.concatenate(picks, axis=0))
        points = points_of(points)
        pick = jnp.where(iota((FACE, ATOMS), 1) == my_atom, 1.0, 0.0).astype(BF16)
        mine_t = picked_rows(pick, pos_t)
        dx = (points[0:1] + wrap(at_x, across_x, side, periods[0])) - mine_t[:, 0:1]
        dy = (points[1:2] + shift_y) - mine_t[:, 1:2]
        dz = (points[2:3] + z_shift(zi, zj)) - mine_t[:, 2:3]
        grid = hopping(dx, dy, dz, count)
        block = [plain((0, FACE)), first((corner_at, DEPTH)), second((corner_at, DEPTH))]
        planes = planes_of((one_wave, two_wave)[n], jnp.concatenate(block, axis=0))
        parts.append(applied(grid, planes))
    y_add(acc, y_sides[1], added)
    planes = [acc[a * ATOMS + FACE : a * ATOMS + 3 * FACE] for a in range(4)]
    result[FACE : 3 * FACE] = atoms_of(planes, wave)
    middle = pl.ds(FACE, 2 * FACE)
    copies = [pltpu.make_async_copy(result.at[middle], out.at[middle], sem.at[2])]
    copies[0].start()
    for n, side in enumerate(x_sides):
        mine, _ = faces_of(side)
        planes = []
        for a in range(4):
            at = pl.multiple_of(a * ATOMS + mine * FACE, FACE)
            planes.append(acc[pl.ds(at, FACE)] + parts[n][a * FACE : (a + 1) * FACE])
        face = pl.ds(mine * FACE, FACE)
        result[face] = atoms_of(planes, (one_wave, two_wave)[n])
        copies.append(pltpu.make_async_copy(result.at[face], out.at[face], sem.at[n]))
        copies[-1].start()
    for copy in copies:
        copy.wait()


def swap(count, begin):
    pairs = []
    for i in range(begin, count + begin, 2):
        a, b = i % count, (i + 1) % count
        pairs += [(a, b), (b, a)]
    return pairs


def exchange_x(one, two, rows):
    count, across_y = lax.axis_size("gx"), lax.axis_size("gy")

    def pairs(begin):
        return [
            (a * across_y + y, b * across_y + y) for y in rows for a, b in swap(count, begin)
        ]

    two = lax.ppermute(two, ("gx", "gy"), pairs(1))
    one = lax.ppermute(one, ("gx", "gy"), pairs(0))
    return two, one


def over_wrap(message, step):
    count, across_y = lax.axis_size("gx"), lax.axis_size("gy")
    pairs = [
        (x * across_y + across_y - 1, (x + step) % count * across_y) for x in range(count)
    ]
    return lax.ppermute(message, ("gx", "gy"), pairs)


VMEM = pl.BlockSpec(memory_space=pltpu.VMEM)
SMEM = pl.BlockSpec(memory_space=pltpu.SMEM)
HBM = pl.BlockSpec(memory_space=pltpu.HBM)
ANY = pl.BlockSpec(memory_space=pl.ANY)


def call(kernel, inputs, outputs, in_space=VMEM, out_space=VMEM, **options):
    return pl.pallas_call(
        kernel,
        out_shape=outputs,
        in_specs=in_space if isinstance(in_space, list) else [in_space] * len(inputs),
        out_specs=[out_space] * len(outputs),
        compiler_params=pltpu.CompilerParams(vmem_limit_bytes=16 * 1024 * 1024),
        **options,
    )(*inputs)


def shards(trial, positions, pair_atoms, pair_owner, pair_image, pair_count):
    sizes = across_x, across_y = lax.axis_size("gx"), lax.axis_size("gy")
    periods = tuple(LATTICE_STEP * (SIDE * count) for count in sizes)
    mine = trial.reshape(ATOMS, 4, NV)
    slots = pair_owner.shape[2]

    def message(sites):
        return jax.ShapeDtypeStruct((sites, 4, NV), BF16)

    def floats(*shape):
        return jax.ShapeDtypeStruct(shape, F32)

    def wave(rows):
        return pltpu.VMEM((2, rows, LANES), F32)

    low, two, top, over, over_up, over_down, aux = call(
        functools.partial(pack_y, sizes),
        tuple(
            pltpu.with_memory_space_constraint(array, pltpu.HBM)
            for array in (
                mine,
                positions.reshape(3 * SIDE * SIDE, DEPTH),
                pair_atoms.reshape(2, slots),
                pair_owner.reshape(1, slots),
            )
        )
        + (pair_count,),
        [message(Y_SITES)] * 4
        + [message(Y_SITES)] * 2
        + [floats(4 * AUX, NV)],
        in_space=[HBM] * 4 + [SMEM],
        scratch_shapes=[
            pltpu.VMEM((3 * SIDE * SIDE, DEPTH), F32),
            pltpu.VMEM((2, slots), jnp.int32),
            pltpu.VMEM((1, slots), jnp.int32),
            pltpu.SemaphoreType.DMA((3 + 4 * SIDE + 2,)),
        ],
    )
    half = across_y // 4 * 2
    pairs = swap(across_y, 0)
    early = lax.axis_index("gy") < half
    y_two = lax.ppermute(two, "gy", swap(across_y, 1)[:-2])
    y_low = lax.ppermute(low, "gy", pairs[:half])
    over_in = over_wrap(over, 0)
    over_up = over_wrap(over_up, 1)
    over_down = over_wrap(over_down, -1)
    (settled,) = call(settle, (y_two, y_low), [floats(8, LANES)], in_space=ANY)

    def x_messages(late, *given):
        return call(
            functools.partial(corners, sizes, late),
            given,
            [message(X_SITES)] * 2,
            in_space=ANY,
            out_space=ANY,
            scratch_shapes=[pltpu.SemaphoreType.DMA((8,))],
        )

    def own_atoms(y_message):
        (acc,) = call(own, (mine, aux), [floats(4 * ATOMS, NV)], scratch_shapes=[wave(4 * ATOMS)])
        return call(
            functools.partial(first_half, periods, sizes),
            (aux, y_message, acc),
            [floats(4 * ATOMS, NV)],
            scratch_shapes=[wave(4 * FACE)],
        )

    def nothing():
        kinds = [message(X_SITES)] * 2 + [floats(4 * ATOMS, NV)]
        return tuple(call(blank, (), kinds, out_space=ANY))

    def early_ones():
        messages = x_messages(False, settled, y_two, y_low, mine, low)
        return (*exchange_x(*messages, range(half)), *own_atoms(y_low))

    def late_ones():
        messages = x_messages(True, beside[0], back, y_top, y_two, mine, low)
        return (*exchange_x(*messages, range(half, across_y)), *own_atoms(y_top))

    from_early = lax.cond(early, early_ones, nothing)
    back, top = call(
        hand_on,
        (from_early[0], over, top),
        [message(Y_SITES)] * 2,
        in_space=ANY,
        out_space=ANY,
        scratch_shapes=[pltpu.SemaphoreType.DMA((2,))],
    )
    back = lax.ppermute(back, "gy", [(0, across_y - 1)])
    (y_top,) = lax.cond(
        early,
        lambda: tuple(call(blank, (), [message(Y_SITES)], out_space=ANY)),
        lambda: (lax.ppermute(top, "gy", pairs[half:]),),
    )
    beside = call(
        functools.partial(crossed, sizes),
        (over_in, over_up, over_down),
        [message(BLOCK)] * 2,
        in_space=ANY,
        out_space=ANY,
        scratch_shapes=[pltpu.SemaphoreType.DMA((2,))],
    )
    def result(late, inputs, spaces, **options):
        (product,) = call(
            functools.partial(second_half, periods, sizes, late),
            inputs,
            [floats(ATOMS, 4, NV)],
            in_space=spaces + [VMEM] * 5 + [VMEM if late else ANY] * 2 + [VMEM],
            out_space=HBM,
            scratch_shapes=[
                pltpu.VMEM((4 * ATOMS, NV), F32),
                wave(2 * ATOMS),
                wave(4 * WIDE),
                wave(4 * WIDE),
                pltpu.VMEM((ATOMS, 4, NV), F32),
                pltpu.VMEM((2, X_SITES, 4, NV), BF16),
                pltpu.SemaphoreType.DMA((3,)),
                pltpu.SemaphoreType.DMA((2,)),
            ],
            **options,
        )
        return product

    product = result(False, (aux, y_two, over_in, *beside, *from_early), [])
    from_late = lax.cond(early, nothing, late_ones)
    product = result(
        True,
        (product, aux, y_two, back, *beside, *from_late),
        [HBM],
        input_output_aliases={0: 0},
    )
    return product.reshape(trial.shape)


def solution(mesh):
    in_specs = (
        P("gx", "gy", None, None, None),
        P(None, "gx", "gy", None),
        P("gx", "gy", None, None),
        P("gx", "gy", None),
        P("gx", "gy", None, None),
        P("gx", "gy"),
    )
    out_specs = P("gx", "gy", None, None, None)
    return jax.shard_map(shards, mesh=mesh, in_specs=in_specs, out_specs=out_specs, check_vma=False)
```

```python
import functools

import jax
import jax.numpy as jnp
from jax import lax
from jax.experimental import pallas as pl
from jax.experimental.pallas import tpu as pltpu
from jax.sharding import PartitionSpec as P

ONSITE_S = -0.22
ONSITE_P = 0.27
HOP_SS = -0.37
HOP_SP = 0.35
HOP_PPS = 0.4
HOP_PPP = -0.114
BOND_LENGTH = 1.536
LATTICE_STEP = 1.6

SIDE = 4
DEPTH = 8
ATOMS = SIDE * SIDE * DEPTH
FACE = SIDE * DEPTH
WIDE = FACE + 2 * DEPTH
NV = 256
LANES = NV // 2
POS_ROWS = 9
LIST_ROWS = 6
AUX = 4
Y_PLACE = (DEPTH, 0, 3 * DEPTH + AUX, 2 * DEPTH + AUX)
Y_AUX = 2 * DEPTH
Y_SITES = FACE + AUX
BLOCK = DEPTH + AUX
X_BLOCK = (FACE + AUX, FACE + AUX + BLOCK)
X_SITES = WIDE + 3 * AUX
STEPS = [(x, y) for x in (-1, 0, 1) for y in (-1, 0, 1)]
F32 = jnp.float32
BF16 = jnp.bfloat16


def iota(shape, axis):
    return lax.broadcasted_iota(jnp.int32, shape, axis)


def onehot(values, expected):
    wide = [jnp.where(row == expected, 1.0, 0.0).astype(BF16) for row in values]
    return wide[0] if len(wide) == 1 else jnp.concatenate(wide, axis=1)


def dot_nt(a, b):
    return lax.dot_general(a, b, (((1,), (1,)), ((), ())), preferred_element_type=F32)


def dot(a, b):
    return jnp.dot(a, b, preferred_element_type=F32)


def list_of(rows):
    first = [rows[k : k + 1] for k in range(2)]
    key = [rows[4 + k : 5 + k] * float(ATOMS) + rows[2 + k : 3 + k] for k in range(2)]
    return first, key


def code(step_x, step_y):
    return (step_x + 1) * 3 + step_y + 1


def hopping(dx, dy, dz, count):
    square = jnp.maximum(dx * dx + dy * dy + dz * dz, 0.5)
    inverse = lax.rsqrt(square)
    cosines = [d * inverse for d in (dx, dy, dz)]
    ratio = BOND_LENGTH * inverse
    radial = ratio * ratio * jnp.exp(1.0 - square * inverse * (1.0 / BOND_LENGTH))

    def final(value):
        return (value.astype(BF16).astype(F32) * count).astype(BF16)

    grid = [[None] * 4 for _ in range(4)]
    grid[0][0] = final(HOP_SS * radial)
    for a in range(3):
        across = final(HOP_SP * radial * cosines[a])
        grid[0][1 + a] = across
        grid[1 + a][0] = -across
        for b in range(a, 3):
            entry = (HOP_PPS - HOP_PPP) * cosines[a] * cosines[b]
            if a == b:
                entry = entry + HOP_PPP
            grid[1 + a][1 + b] = grid[1 + b][1 + a] = final(entry * radial)
    return grid


def planes_of(wave, block):
    n = block.shape[0]
    wide = block.astype(F32).reshape(n // 2, 2, 4, NV)
    wide = jnp.concatenate([wide[:, 0], wide[:, 1]], axis=1).reshape(4 * n, NV)
    for h in range(2):
        wave[h, : 4 * n] = wide[:, h * LANES : (h + 1) * LANES]
    halves = [[wave[h, pl.ds(b, n, stride=4), :] for h in range(2)] for b in range(4)]
    return [jnp.concatenate(pair, axis=1) for pair in halves]


def applied(grid, planes):
    total = None
    for b in range(4):
        stacked = jnp.concatenate([grid[a][b] for a in range(4)], axis=0)
        part = dot(stacked, planes[b].astype(BF16))
        total = part if total is None else total + part
    return total


def atoms_of(planes, wave):
    n = planes[0].shape[0]
    for a in range(4):
        for h in range(2):
            wave[h, pl.ds(a, n, stride=4), :] = planes[a][:, h * LANES : (h + 1) * LANES]
    wide = jnp.concatenate([wave[h, : 4 * n] for h in range(2)], axis=1)
    wide = wide.reshape(n // 2, 8, NV)
    return jnp.stack([wide[:, :4], wide[:, 4:]], axis=1).reshape(n, 4, NV)


def turned(points):
    n = points.shape[1]
    return jnp.concatenate([points, jnp.zeros((5, n), F32)], axis=0).T


def picked_rows(pick, points):
    total = None
    for _ in range(3):
        piece = points.astype(BF16)
        part = dot(pick, piece)
        total = part if total is None else total + part
        points = points - piece.astype(F32)
    return total


def z_shift(zi, zj):
    step = zj - zi
    period = LATTICE_STEP * DEPTH
    return jnp.where(step > 1.5, -period, jnp.where(step < -1.5, period, 0.0))


def wrap(place, across, side, period):
    high = jnp.where((side > 0) & (place == across - 1), period, 0.0)
    return jnp.where((side < 0) & (place == 0), -period, high)


def place_of(sizes):
    return lax.axis_index("gx"), lax.axis_index("gy"), *sizes


def side_of(place):
    first = 1 - 2 * (place & 1)
    return first, -first


def faces_of(side):
    mine = jnp.where(side > 0, SIDE - 1, 0)
    return mine, SIDE - 1 - mine


def sum_of(*readers):
    def read(at):
        total = None
        for reader in readers:
            value = reader(at)
            total = value if total is None else total + value
        return total

    return read


def reader_of(message, first=0):
    return lambda at: message[pl.ds(first + at[0], at[1])].astype(F32)


def aux_of(read, first):
    sites = read((first, AUX))
    return jnp.concatenate([sites[k] for k in range(AUX)], axis=0)


def points_of(rows):
    return rows[0:3] + rows[3:6] + rows[6:9]


def pack_y(sizes, trial, positions, atoms, owner, count, *refs):
    low, two, top, over, back, over_up, over_down, aux, pos, pairs, owners, sem = refs
    at_x, at_y, across_x, across_y = place_of(sizes)
    copies = [
        pltpu.make_async_copy(a, b, sem.at[k])
        for k, (a, b) in enumerate(((positions, pos), (atoms, pairs), (owner, owners)))
    ]
    faces = [faces_of(side)[0] for side in side_of(at_y)]
    moves = [
        (x, faces[n], out.at[pl.ds(begin + Y_PLACE[x], DEPTH)])
        for n, out, begin in (
            (0, low, 0),
            (1, two, 0),
            (0, top, 0),
            (1, over, 0),
            (1, back, 0),
        )
        for x in range(SIDE)
    ]
    moves.append((SIDE - 1, faces[1], over_up.at[pl.ds(AUX, DEPTH)]))
    moves.append((0, faces[1], over_down.at[pl.ds(0, DEPTH)]))
    for x, face, out in moves:
        begin = (x * SIDE + face) * DEPTH
        copies.append(
            pltpu.make_async_copy(trial.at[pl.ds(begin, DEPTH)], out, sem.at[len(copies)])
        )
    for copy in copies:
        copy.start()
    rows = 3 * SIDE * SIDE
    tile = (iota((DEPTH, ATOMS), 1) & (DEPTH - 1)) == iota((DEPTH, ATOMS), 0)
    tile = jnp.where(tile, 1.0, 0.0).astype(BF16)
    row = iota((3 * rows, ATOMS), 0)
    keep = (row & (SIDE * SIDE - 1)) == (iota((3 * rows, ATOMS), 1) >> 3)
    gather = (iota((16, 3 * rows), 1) >> 4) == iota((16, 3 * rows), 0)
    gather = jnp.where(gather, 1.0, 0.0).astype(BF16)
    aux[:, ATOMS:] = jnp.zeros((4 * AUX, NV - ATOMS), F32)
    for copy in copies[:3]:
        copy.wait()
    rest = pos[...]
    parts = []
    for _ in range(3):
        piece = rest.astype(BF16)
        parts.append(piece)
        rest = rest - piece.astype(F32)
    spread = dot(jnp.concatenate(parts, axis=0), tile)
    aux[:, :ATOMS] = dot(gather, jnp.where(keep, spread, 0.0).astype(BF16))
    whose = owners[...]
    step = jnp.zeros(whose.shape, F32)
    for x, y in STEPS:
        name = lax.rem(at_x + x + across_x, across_x) * across_y
        name = name + lax.rem(at_y + y + across_y, across_y)
        step = jnp.where(whose == name, float(code(x, y)), step)
    live = iota(whose.shape, 1) < count[0, 0]
    first = jnp.where(live, pairs[0:1], -1).astype(F32)
    second = pairs[1:2].astype(F32)
    for k, values in enumerate((first, second, step)):
        for h in range(2):
            at = POS_ROWS + 2 * k + h
            aux[at : at + 1] = values[:, h * NV : (h + 1) * NV]
    places = [(out, Y_AUX) for out in (low, two, top, over, back)]
    places += [(over_up, 0), (over_down, DEPTH)]
    for k in range(AUX):
        site = aux[4 * k : 4 * k + 4].astype(BF16)
        for out, at in places:
            out[at + k] = site
    for copy in copies[3:]:
        copy.wait()


def own(trial, aux, acc, wave):
    rows = aux[...]
    first, key = list_of(rows[POS_ROWS : POS_ROWS + LIST_ROWS])
    atom = iota((ATOMS, 1), 0)
    is_first = onehot(first, atom.astype(F32))
    is_second = onehot(key, (atom + code(0, 0) * ATOMS).astype(F32))
    count = dot_nt(is_first, is_second) + dot_nt(is_second, is_first)
    pos = points_of(rows)[:, :ATOMS]
    pos_t = turned(pos)
    zi = (atom & (DEPTH - 1)).astype(F32)
    zj = (iota((1, ATOMS), 1) & (DEPTH - 1)).astype(F32)
    dx, dy = (pos[a : a + 1] - pos_t[:, a : a + 1] for a in range(2))
    dz = (pos[2:3] + z_shift(zi, zj)) - pos_t[:, 2:3]
    grid = hopping(dx, dy, dz, count)
    planes = planes_of(wave, trial[...])
    matrix = jnp.concatenate([jnp.concatenate(line, axis=1) for line in grid], axis=0)
    part = dot(matrix, jnp.concatenate(planes, axis=0).astype(BF16))
    for a in range(4):
        onsite = ONSITE_P if a else ONSITE_S
        rows = slice(a * ATOMS, (a + 1) * ATOMS)
        acc[rows] = onsite * planes[a] + part[rows]


def corners(sizes, late, *refs):
    _, *inputs, one, two, sem = refs
    if late:
        over, y_one, y_two, trial, message = inputs
    else:
        y_two, y_one, trial, message = inputs
    at_x, at_y, _, across_y = place_of(sizes)
    copies = []

    def copy_of(source, begin, count, out, at):
        return pltpu.make_async_copy(
            source.at[pl.ds(begin, count)], out.at[pl.ds(at, count)], sem.at[len(copies)]
        )

    for side, out in zip(side_of(at_x), (one, two)):
        face, _ = faces_of(side)
        begin = jnp.where(face == 0, Y_PLACE[0], Y_AUX)
        for given in (
            (trial, face * FACE, FACE, out, 0),
            (message, Y_AUX, AUX, out, FACE),
            (y_one, begin, BLOCK, out, X_BLOCK[0]),
        ):
            copies.append(copy_of(*given))
            copies[-1].start()
        plain = copy_of(y_two, begin, BLOCK, out, X_BLOCK[1])
        if late:
            other = copy_of(over, begin, BLOCK, out, X_BLOCK[1])

            @pl.when(at_y == across_y - 1)
            def _():
                other.start()

            @pl.when(at_y != across_y - 1)
            def _():
                plain.start()
        else:
            plain.start()
        copies.append(plain)
    for copy in copies:
        copy.wait()


def crossed(sizes, over, up, down, one, two, sem):
    del over
    copies = []
    for n, (side, out) in enumerate(zip(side_of(place_of(sizes)[0]), (one, two))):
        low, high = (pltpu.make_async_copy(source.at[pl.ds(0, BLOCK)], out, sem.at[n]) for source in (up, down))

        @pl.when(side < 0)
        def _():
            low.start()

        @pl.when(side > 0)
        def _():
            high.start()

        copies.append(low)
    for copy in copies:
        copy.wait()


def hand_on(*_):
    pass


def settle(y_two, y_low, out):
    del y_two, y_low
    out[...] = jnp.zeros_like(out)


def blank(*_):
    pass


def own_of(aux):
    rows = aux[...]
    return *list_of(rows[POS_ROWS : POS_ROWS + LIST_ROWS]), turned(points_of(rows)[:, :ATOMS])


def y_atoms(side):
    mine, theirs = faces_of(side)
    k = iota((FACE, 1), 0)
    z = k & (DEPTH - 1)
    line = (k >> 3) * (SIDE * DEPTH) + z
    crossed = ((k >> 3) ^ 1) * (SIDE * DEPTH) + z
    return line + mine * DEPTH, crossed + theirs * DEPTH


def y_ahead(side, own_first, own_key, pos_t):
    my_atom, their_atom = y_atoms(side)
    left = onehot(own_first, my_atom.astype(F32))
    right = onehot(own_key, (their_atom + (4 + side) * ATOMS).astype(F32))
    pick = jnp.where(iota((FACE, ATOMS), 1) == my_atom, 1.0, 0.0).astype(BF16)
    return dot_nt(left, right), picked_rows(pick, pos_t)


def y_part(period, sizes, side, read, forward, mine_t, wave):
    _, at_y, _, across_y = place_of(sizes)
    _, theirs = faces_of(side)
    my_atom, their_atom = y_atoms(side)
    rows = aux_of(read, Y_AUX)
    first, key = list_of(rows[POS_ROWS : POS_ROWS + LIST_ROWS])
    left = onehot(key, (my_atom + (4 - side) * ATOMS).astype(F32))
    count = forward + dot_nt(left, onehot(first, their_atom.astype(F32)))
    lane = iota((ATOMS, FACE), 1)
    lane = ((lane >> 3) ^ 1) * (SIDE * DEPTH) + (lane & (DEPTH - 1)) + theirs * DEPTH
    pick = jnp.where(iota((ATOMS, FACE), 0) == lane, 1.0, 0.0).astype(BF16)
    points = points_of(dot(rows[:, :ATOMS].astype(BF16), pick))
    zi = (iota((FACE, 1), 0) & (DEPTH - 1)).astype(F32)
    zj = (iota((1, FACE), 1) & (DEPTH - 1)).astype(F32)
    dx = points[0:1] - mine_t[:, 0:1]
    dy = (points[1:2] + wrap(at_y, across_y, side, period)) - mine_t[:, 1:2]
    dz = (points[2:3] + z_shift(zi, zj)) - mine_t[:, 2:3]
    grid = hopping(dx, dy, dz, count)
    half = 2 * DEPTH
    block = jnp.concatenate([read((0, half)), read((half + AUX, half))], axis=0)
    return applied(grid, planes_of(wave, block))


def y_add(acc, side, part):
    mine, _ = faces_of(side)
    for a in range(4):
        for x in range(SIDE):
            at = pl.multiple_of(a * ATOMS + (x * SIDE + mine) * DEPTH, DEPTH)
            begin = a * FACE + x * DEPTH
            acc[pl.ds(at, DEPTH)] += part[begin : begin + DEPTH]


def ghost(theirs, y_sides, shape, axis):
    at = iota(shape, axis)
    part = jnp.where(at < FACE, 0, jnp.where(at < FACE + DEPTH, 1, 2))
    step = jnp.where(part == 0, 0, jnp.where(part == 1, y_sides[0], y_sides[1]))
    row = jnp.where(step > 0, 0, (SIDE - 1) * DEPTH)
    atom = theirs * FACE + jnp.where(part == 0, at, row + (at & (DEPTH - 1)))
    return atom, step, part


def first_half(periods, sizes, aux, message, acc_in, acc, forward_y, mine_y, forward_x, mine_x, wave):
    at_x, at_y, _, _ = place_of(sizes)
    y_sides = side_of(at_y)
    own_first, own_key, pos_t = own_of(aux)
    forward_y[...], mine_y[...] = y_ahead(y_sides[1], own_first, own_key, pos_t)
    for n, side in enumerate(side_of(at_x)):
        mine, theirs = faces_of(side)
        my_atom = iota((FACE, 1), 0) + mine * FACE
        their_atom, step, _ = ghost(theirs, y_sides, (WIDE, 1), 0)
        target = their_atom + ((side + 1) * 3 + step + 1) * ATOMS
        left = onehot(own_first, my_atom.astype(F32))
        forward_x[n] = dot_nt(left, onehot(own_key, target.astype(F32)))
        pick = jnp.where(iota((FACE, ATOMS), 1) == my_atom, 1.0, 0.0).astype(BF16)
        mine_x[n] = picked_rows(pick, pos_t)
    forward, mine_t = y_ahead(y_sides[0], own_first, own_key, pos_t)
    acc[...] = acc_in[...]
    part = y_part(periods[1], sizes, y_sides[0], reader_of(message), forward, mine_t, wave)
    y_add(acc, y_sides[0], part)


def second_half(periods, sizes, late, *refs):
    _, at_y, _, across_y = place_of(sizes)
    mine = at_y < across_y // 4 * 2
    if late:
        _, *refs = refs
        mine = jnp.logical_not(mine)

    @pl.when(mine)
    def _():
        finish(periods, sizes, late, *refs)


def finish(periods, sizes, late, y_two, other, *refs):
    beside, given = refs[:2], refs[2:4]
    acc_in, forward_y, mine_y, forward_x, mine_x = refs[4:9]
    out, acc, wave, one_wave, two_wave, result, x_messages, sem, x_sem = refs[9:]
    at_x, at_y, across_x, across_y = place_of(sizes)
    arrivals = []
    if late:
        x_messages = given[1], given[0]
    else:
        x_messages = x_messages.at[0], x_messages.at[1]
        arrivals = [
            pltpu.make_async_copy(source, target, x_sem.at[n])
            for n, (source, target) in enumerate(zip(given, x_messages[::-1]))
        ]
    for arrival in arrivals:
        arrival.start()
    acc[...] = acc_in[...]
    y_sides = side_of(at_y)
    x_sides = side_of(at_x)

    read = sum_of(reader_of(y_two), reader_of(other))
    added = y_part(periods[1], sizes, y_sides[1], read, forward_y[...], mine_y[...], wave)
    k = iota((FACE, 1), 0)
    zi = (k & (DEPTH - 1)).astype(F32)
    lane = iota((1, WIDE), 1)
    zj = (lane & (DEPTH - 1)).astype(F32)
    shifts = [wrap(at_y, across_y, y, periods[1]) for y in y_sides]
    shift_y = jnp.where(lane < FACE, 0.0, jnp.where(lane < FACE + DEPTH, *shifts))
    parts = []
    for arrival in arrivals:
        arrival.wait()
    for n, side in enumerate(x_sides):
        mine, theirs = faces_of(side)
        corner_at = jnp.where(theirs == 0, 0, AUX)
        aux_at = jnp.where(theirs == 0, DEPTH, 0)
        plain = reader_of(x_messages[n])

        def second(at, plain=plain, other=reader_of(beside[n])):
            return plain((X_BLOCK[1] + at[0], at[1])) + other(at)

        def first(at, plain=plain):
            return plain((X_BLOCK[0] + at[0], at[1]))

        my_atom = k + mine * FACE
        their_atom, _, part = ghost(theirs, y_sides, (WIDE, 1), 0)
        lane_atom, _, lane_part = ghost(theirs, y_sides, (ATOMS, WIDE), 1)
        left, right, picks, placed = [], [], [], []
        for m, y in enumerate((0, *y_sides)):
            rows = aux_of((plain, first, second)[m], aux_at if m else FACE)
            listed, key = list_of(rows[POS_ROWS : POS_ROWS + LIST_ROWS])
            wanted = my_atom + ((1 - side) * 3 + 1 - y) * ATOMS
            left.append(onehot(key, wanted.astype(F32)))
            right.append(onehot(listed, jnp.where(part == m, their_atom, -2).astype(F32)))
            pick = (iota((ATOMS, WIDE), 0) == lane_atom) & (lane_part == m)
            picks.append(jnp.where(pick, 1.0, 0.0).astype(BF16))
            placed.append(rows[:, :ATOMS].astype(BF16))
        count = forward_x[n] + dot_nt(
            jnp.concatenate(left, axis=1), jnp.concatenate(right, axis=1)
        )
        points = dot(jnp.concatenate(placed, axis=1), jnp.concatenate(picks, axis=0))
        points = points_of(points)
        mine_t = mine_x[n]
        dx = (points[0:1] + wrap(at_x, across_x, side, periods[0])) - mine_t[:, 0:1]
        dy = (points[1:2] + shift_y) - mine_t[:, 1:2]
        dz = (points[2:3] + z_shift(zi, zj)) - mine_t[:, 2:3]
        grid = hopping(dx, dy, dz, count)
        block = [plain((0, FACE)), first((corner_at, DEPTH)), second((corner_at, DEPTH))]
        planes = planes_of((one_wave, two_wave)[n], jnp.concatenate(block, axis=0))
        parts.append(applied(grid, planes))
    y_add(acc, y_sides[1], added)
    planes = [acc[a * ATOMS + FACE : a * ATOMS + 3 * FACE] for a in range(4)]
    result[FACE : 3 * FACE] = atoms_of(planes, wave)
    middle = pl.ds(FACE, 2 * FACE)
    copies = [pltpu.make_async_copy(result.at[middle], out.at[middle], sem.at[2])]
    copies[0].start()
    for n, side in enumerate(x_sides):
        mine, _ = faces_of(side)
        planes = []
        for a in range(4):
            at = pl.multiple_of(a * ATOMS + mine * FACE, FACE)
            planes.append(acc[pl.ds(at, FACE)] + parts[n][a * FACE : (a + 1) * FACE])
        face = pl.ds(mine * FACE, FACE)
        result[face] = atoms_of(planes, (one_wave, two_wave)[n])
        copies.append(pltpu.make_async_copy(result.at[face], out.at[face], sem.at[n]))
        copies[-1].start()
    for copy in copies:
        copy.wait()


def swap(count, begin):
    pairs = []
    for i in range(begin, count + begin, 2):
        a, b = i % count, (i + 1) % count
        pairs += [(a, b), (b, a)]
    return pairs


def exchange_x(one, two, rows):
    count, across_y = lax.axis_size("gx"), lax.axis_size("gy")

    def pairs(begin):
        return [
            (a * across_y + y, b * across_y + y) for y in rows for a, b in swap(count, begin)
        ]

    two = lax.ppermute(two, ("gx", "gy"), pairs(1))
    one = lax.ppermute(one, ("gx", "gy"), pairs(0))
    return two, one


def over_wrap(message, step):
    count, across_y = lax.axis_size("gx"), lax.axis_size("gy")
    pairs = [
        (x * across_y + across_y - 1, (x + step) % count * across_y) for x in range(count)
    ]
    return lax.ppermute(message, ("gx", "gy"), pairs)


VMEM = pl.BlockSpec(memory_space=pltpu.VMEM)
SMEM = pl.BlockSpec(memory_space=pltpu.SMEM)
HBM = pl.BlockSpec(memory_space=pltpu.HBM)
ANY = pl.BlockSpec(memory_space=pl.ANY)


def call(kernel, inputs, outputs, in_space=VMEM, out_space=VMEM, **options):
    return pl.pallas_call(
        kernel,
        out_shape=outputs,
        in_specs=in_space if isinstance(in_space, list) else [in_space] * len(inputs),
        out_specs=[out_space] * len(outputs),
        compiler_params=pltpu.CompilerParams(vmem_limit_bytes=16 * 1024 * 1024),
        **options,
    )(*inputs)


def shards(trial, positions, pair_atoms, pair_owner, pair_image, pair_count):
    sizes = across_x, across_y = lax.axis_size("gx"), lax.axis_size("gy")
    periods = tuple(LATTICE_STEP * (SIDE * count) for count in sizes)
    mine = trial.reshape(ATOMS, 4, NV)
    slots = pair_owner.shape[2]

    def message(sites):
        return jax.ShapeDtypeStruct((sites, 4, NV), BF16)

    def floats(*shape):
        return jax.ShapeDtypeStruct(shape, F32)

    def wave(rows):
        return pltpu.VMEM((2, rows, LANES), F32)

    low, two, top, over, back, over_up, over_down, aux = call(
        functools.partial(pack_y, sizes),
        tuple(
            pltpu.with_memory_space_constraint(array, pltpu.HBM)
            for array in (
                mine,
                positions.reshape(3 * SIDE * SIDE, DEPTH),
                pair_atoms.reshape(2, slots),
                pair_owner.reshape(1, slots),
            )
        )
        + (pair_count,),
        [message(Y_SITES)] * 5
        + [message(Y_SITES)] * 2
        + [floats(4 * AUX, NV)],
        in_space=[HBM] * 4 + [SMEM],
        scratch_shapes=[
            pltpu.VMEM((3 * SIDE * SIDE, DEPTH), F32),
            pltpu.VMEM((2, slots), jnp.int32),
            pltpu.VMEM((1, slots), jnp.int32),
            pltpu.SemaphoreType.DMA((3 + 5 * SIDE + 2,)),
        ],
    )
    half = across_y // 4 * 2
    pairs = swap(across_y, 0)
    early = lax.axis_index("gy") < half
    y_two = lax.ppermute(two, "gy", swap(across_y, 1)[:-2])
    y_low = lax.ppermute(low, "gy", pairs[:half])
    over_in = over_wrap(over, 0)
    over_up = over_wrap(over_up, 1)
    over_down = over_wrap(over_down, -1)
    (settled,) = call(settle, (y_two, y_low), [floats(8, LANES)], in_space=ANY)

    def x_messages(late, *given):
        return call(
            functools.partial(corners, sizes, late),
            given,
            [message(X_SITES)] * 2,
            in_space=ANY,
            out_space=ANY,
            scratch_shapes=[pltpu.SemaphoreType.DMA((8,))],
        )

    own_kinds = [
        floats(4 * ATOMS, NV),
        floats(FACE, FACE),
        floats(FACE, 8),
        floats(2, FACE, WIDE),
        floats(2, FACE, 8),
    ]

    def own_atoms(y_message):
        (acc,) = call(own, (mine, aux), [floats(4 * ATOMS, NV)], scratch_shapes=[wave(4 * ATOMS)])
        return call(
            functools.partial(first_half, periods, sizes),
            (aux, y_message, acc),
            own_kinds,
            scratch_shapes=[wave(4 * FACE)],
        )

    def nothing():
        kinds = [message(X_SITES)] * 2 + own_kinds
        return tuple(call(blank, (), kinds, out_space=ANY))

    def early_ones():
        messages = x_messages(False, settled, y_two, y_low, mine, low)
        return (*exchange_x(*messages, range(half)), *own_atoms(y_low))

    def late_ones():
        messages = x_messages(True, beside[0], back, y_top, y_two, mine, low)
        return (*exchange_x(*messages, range(half, across_y)), *own_atoms(y_top))

    from_early = lax.cond(early, early_ones, nothing)
    back, top = call(
        hand_on,
        (from_early[0], back, top),
        [message(Y_SITES)] * 2,
        in_space=ANY,
        out_space=ANY,
        input_output_aliases={1: 0, 2: 1},
    )
    back = lax.ppermute(back, "gy", [(0, across_y - 1)])
    (y_top,) = lax.cond(
        early,
        lambda: tuple(call(blank, (), [message(Y_SITES)], out_space=ANY)),
        lambda: (lax.ppermute(top, "gy", pairs[half:]),),
    )
    beside = call(
        functools.partial(crossed, sizes),
        (over_in, over_up, over_down),
        [message(BLOCK)] * 2,
        in_space=ANY,
        out_space=ANY,
        scratch_shapes=[pltpu.SemaphoreType.DMA((2,))],
    )
    def result(late, inputs, spaces, **options):
        (product,) = call(
            functools.partial(second_half, periods, sizes, late),
            inputs,
            [floats(ATOMS, 4, NV)],
            in_space=spaces + [VMEM] * 4 + [VMEM if late else ANY] * 2 + [VMEM] * 5,
            out_space=HBM,
            scratch_shapes=[
                pltpu.VMEM((4 * ATOMS, NV), F32),
                wave(2 * ATOMS),
                wave(4 * WIDE),
                wave(4 * WIDE),
                pltpu.VMEM((ATOMS, 4, NV), F32),
                pltpu.VMEM((2, X_SITES, 4, NV), BF16),
                pltpu.SemaphoreType.DMA((3,)),
                pltpu.SemaphoreType.DMA((2,)),
            ],
            **options,
        )
        return product

    product = result(False, (y_two, over_in, *beside, *from_early), [])
    from_late = lax.cond(early, nothing, late_ones)
    product = result(
        True,
        (product, y_two, back, *beside, *from_late),
        [HBM],
        input_output_aliases={0: 0},
    )
    return product.reshape(trial.shape)


def solution(mesh):
    in_specs = (
        P("gx", "gy", None, None, None),
        P(None, "gx", "gy", None),
        P("gx", "gy", None, None),
        P("gx", "gy", None),
        P("gx", "gy", None, None),
        P("gx", "gy"),
    )
    out_specs = P("gx", "gy", None, None, None)
    return jax.shard_map(shards, mesh=mesh, in_specs=in_specs, out_specs=out_specs, check_vma=False)
```

```python
import functools

import jax
import jax.numpy as jnp
from jax import lax
from jax.experimental import pallas as pl
from jax.experimental.pallas import tpu as pltpu
from jax.sharding import PartitionSpec as P

ONSITE_S = -0.22
ONSITE_P = 0.27
HOP_SS = -0.37
HOP_SP = 0.35
HOP_PPS = 0.4
HOP_PPP = -0.114
BOND_LENGTH = 1.536
LATTICE_STEP = 1.6

SIDE = 4
DEPTH = 8
ATOMS = SIDE * SIDE * DEPTH
FACE = SIDE * DEPTH
WIDE = FACE + 2 * DEPTH
NV = 256
LANES = NV // 2
POS_ROWS = 9
LIST_ROWS = 6
AUX = 4
Y_PLACE = (DEPTH, 0, 3 * DEPTH + AUX, 2 * DEPTH + AUX)
Y_AUX = 2 * DEPTH
Y_SITES = FACE + AUX
BLOCK = DEPTH + AUX
X_BLOCK = (FACE + AUX, FACE + AUX + BLOCK)
X_SITES = WIDE + 3 * AUX
STEPS = [(x, y) for x in (-1, 0, 1) for y in (-1, 0, 1)]
F32 = jnp.float32
BF16 = jnp.bfloat16


def iota(shape, axis):
    return lax.broadcasted_iota(jnp.int32, shape, axis)


def onehot(values, expected):
    wide = [jnp.where(row == expected, 1.0, 0.0).astype(BF16) for row in values]
    return wide[0] if len(wide) == 1 else jnp.concatenate(wide, axis=1)


def dot_nt(a, b):
    return lax.dot_general(a, b, (((1,), (1,)), ((), ())), preferred_element_type=F32)


def dot(a, b):
    return jnp.dot(a, b, preferred_element_type=F32)


def list_of(rows):
    first = [rows[k : k + 1] for k in range(2)]
    key = [rows[4 + k : 5 + k] * float(ATOMS) + rows[2 + k : 3 + k] for k in range(2)]
    return first, key


def code(step_x, step_y):
    return (step_x + 1) * 3 + step_y + 1


def hopping(dx, dy, dz, count):
    square = jnp.maximum(dx * dx + dy * dy + dz * dz, 0.5)
    inverse = lax.rsqrt(square)
    cosines = [d * inverse for d in (dx, dy, dz)]
    ratio = BOND_LENGTH * inverse
    radial = ratio * ratio * jnp.exp(1.0 - square * inverse * (1.0 / BOND_LENGTH))

    def final(value):
        return (value.astype(BF16).astype(F32) * count).astype(BF16)

    grid = [[None] * 4 for _ in range(4)]
    grid[0][0] = final(HOP_SS * radial)
    for a in range(3):
        across = final(HOP_SP * radial * cosines[a])
        grid[0][1 + a] = across
        grid[1 + a][0] = -across
        for b in range(a, 3):
            entry = (HOP_PPS - HOP_PPP) * cosines[a] * cosines[b]
            if a == b:
                entry = entry + HOP_PPP
            grid[1 + a][1 + b] = grid[1 + b][1 + a] = final(entry * radial)
    return grid


def planes_of(wave, block):
    n = block.shape[0]
    wide = block.astype(F32).reshape(n // 2, 2, 4, NV)
    wide = jnp.concatenate([wide[:, 0], wide[:, 1]], axis=1).reshape(4 * n, NV)
    for h in range(2):
        wave[h, : 4 * n] = wide[:, h * LANES : (h + 1) * LANES]
    halves = [[wave[h, pl.ds(b, n, stride=4), :] for h in range(2)] for b in range(4)]
    return [jnp.concatenate(pair, axis=1) for pair in halves]


def applied(grid, planes):
    total = None
    for b in range(4):
        stacked = jnp.concatenate([grid[a][b] for a in range(4)], axis=0)
        part = dot(stacked, planes[b].astype(BF16))
        total = part if total is None else total + part
    return total


def atoms_of(planes, wave):
    n = planes[0].shape[0]
    for a in range(4):
        for h in range(2):
            wave[h, pl.ds(a, n, stride=4), :] = planes[a][:, h * LANES : (h + 1) * LANES]
    wide = jnp.concatenate([wave[h, : 4 * n] for h in range(2)], axis=1)
    wide = wide.reshape(n // 2, 8, NV)
    return jnp.stack([wide[:, :4], wide[:, 4:]], axis=1).reshape(n, 4, NV)


def turned(points):
    n = points.shape[1]
    return jnp.concatenate([points, jnp.zeros((5, n), F32)], axis=0).T


def picked_rows(pick, points):
    total = None
    for _ in range(3):
        piece = points.astype(BF16)
        part = dot(pick, piece)
        total = part if total is None else total + part
        points = points - piece.astype(F32)
    return total


def z_shift(zi, zj):
    step = zj - zi
    period = LATTICE_STEP * DEPTH
    return jnp.where(step > 1.5, -period, jnp.where(step < -1.5, period, 0.0))


def wrap(place, across, side, period):
    high = jnp.where((side > 0) & (place == across - 1), period, 0.0)
    return jnp.where((side < 0) & (place == 0), -period, high)


def place_of(sizes):
    return lax.axis_index("gx"), lax.axis_index("gy"), *sizes


def side_of(place):
    first = 1 - 2 * (place & 1)
    return first, -first


def faces_of(side):
    mine = jnp.where(side > 0, SIDE - 1, 0)
    return mine, SIDE - 1 - mine


def sum_of(*readers):
    def read(at):
        total = None
        for reader in readers:
            value = reader(at)
            total = value if total is None else total + value
        return total

    return read


def reader_of(message, first=0):
    return lambda at: message[pl.ds(first + at[0], at[1])].astype(F32)


def aux_of(read, first):
    sites = read((first, AUX))
    return jnp.concatenate([sites[k] for k in range(AUX)], axis=0)


def points_of(rows):
    return rows[0:3] + rows[3:6] + rows[6:9]


def pack_y(sizes, trial, positions, atoms, owner, count, *refs):
    low, two, top, over, back, over_up, over_down, aux, pos, pairs, owners, sem = refs
    at_x, at_y, across_x, across_y = place_of(sizes)
    copies = [
        pltpu.make_async_copy(a, b, sem.at[k])
        for k, (a, b) in enumerate(((positions, pos), (atoms, pairs), (owner, owners)))
    ]
    faces = [faces_of(side)[0] for side in side_of(at_y)]
    moves = [
        (x, faces[n], out.at[pl.ds(begin + Y_PLACE[x], DEPTH)])
        for n, out, begin in (
            (0, low, 0),
            (1, two, 0),
            (0, top, 0),
            (1, over, 0),
            (1, back, 0),
        )
        for x in range(SIDE)
    ]
    moves.append((SIDE - 1, faces[1], over_up.at[pl.ds(AUX, DEPTH)]))
    moves.append((0, faces[1], over_down.at[pl.ds(0, DEPTH)]))
    for x, face, out in moves:
        begin = (x * SIDE + face) * DEPTH
        copies.append(
            pltpu.make_async_copy(trial.at[pl.ds(begin, DEPTH)], out, sem.at[len(copies)])
        )
    for copy in copies:
        copy.start()
    rows = 3 * SIDE * SIDE
    tile = (iota((DEPTH, ATOMS), 1) & (DEPTH - 1)) == iota((DEPTH, ATOMS), 0)
    tile = jnp.where(tile, 1.0, 0.0).astype(BF16)
    row = iota((3 * rows, ATOMS), 0)
    keep = (row & (SIDE * SIDE - 1)) == (iota((3 * rows, ATOMS), 1) >> 3)
    gather = (iota((16, 3 * rows), 1) >> 4) == iota((16, 3 * rows), 0)
    gather = jnp.where(gather, 1.0, 0.0).astype(BF16)
    aux[:, ATOMS:] = jnp.zeros((4 * AUX, NV - ATOMS), F32)
    for copy in copies[:3]:
        copy.wait()
    rest = pos[...]
    parts = []
    for _ in range(3):
        piece = rest.astype(BF16)
        parts.append(piece)
        rest = rest - piece.astype(F32)
    spread = dot(jnp.concatenate(parts, axis=0), tile)
    aux[:, :ATOMS] = dot(gather, jnp.where(keep, spread, 0.0).astype(BF16))
    whose = owners[...]
    step = jnp.zeros(whose.shape, F32)
    for x, y in STEPS:
        name = lax.rem(at_x + x + across_x, across_x) * across_y
        name = name + lax.rem(at_y + y + across_y, across_y)
        step = jnp.where(whose == name, float(code(x, y)), step)
    live = iota(whose.shape, 1) < count[0, 0]
    first = jnp.where(live, pairs[0:1], -1).astype(F32)
    second = pairs[1:2].astype(F32)
    for k, values in enumerate((first, second, step)):
        for h in range(2):
            at = POS_ROWS + 2 * k + h
            aux[at : at + 1] = values[:, h * NV : (h + 1) * NV]
    places = [(out, Y_AUX) for out in (low, two, top, over, back)]
    places += [(over_up, 0), (over_down, DEPTH)]
    for k in range(AUX):
        site = aux[4 * k : 4 * k + 4].astype(BF16)
        for out, at in places:
            out[at + k] = site
    for copy in copies[3:]:
        copy.wait()


def own(trial, aux, acc, wave):
    rows = aux[...]
    first, key = list_of(rows[POS_ROWS : POS_ROWS + LIST_ROWS])
    atom = iota((ATOMS, 1), 0)
    is_first = onehot(first, atom.astype(F32))
    is_second = onehot(key, (atom + code(0, 0) * ATOMS).astype(F32))
    count = dot_nt(is_first, is_second) + dot_nt(is_second, is_first)
    pos = points_of(rows)[:, :ATOMS]
    pos_t = turned(pos)
    zi = (atom & (DEPTH - 1)).astype(F32)
    zj = (iota((1, ATOMS), 1) & (DEPTH - 1)).astype(F32)
    dx, dy = (pos[a : a + 1] - pos_t[:, a : a + 1] for a in range(2))
    dz = (pos[2:3] + z_shift(zi, zj)) - pos_t[:, 2:3]
    grid = hopping(dx, dy, dz, count)
    planes = planes_of(wave, trial[...])
    matrix = jnp.concatenate([jnp.concatenate(line, axis=1) for line in grid], axis=0)
    part = dot(matrix, jnp.concatenate(planes, axis=0).astype(BF16))
    for a in range(4):
        onsite = ONSITE_P if a else ONSITE_S
        rows = slice(a * ATOMS, (a + 1) * ATOMS)
        acc[rows] = onsite * planes[a] + part[rows]


def corners(sizes, late, *refs):
    _, *inputs, one, two, sem = refs
    if late:
        over, y_one, y_two, trial, message = inputs
    else:
        y_two, y_one, trial, message = inputs
    at_x, at_y, _, across_y = place_of(sizes)
    copies = []

    def copy_of(source, begin, count, out, at):
        return pltpu.make_async_copy(
            source.at[pl.ds(begin, count)], out.at[pl.ds(at, count)], sem.at[len(copies)]
        )

    for side, out in zip(side_of(at_x), (one, two)):
        face, _ = faces_of(side)
        begin = jnp.where(face == 0, Y_PLACE[0], Y_AUX)
        for given in (
            (trial, face * FACE, FACE, out, 0),
            (message, Y_AUX, AUX, out, FACE),
            (y_one, begin, BLOCK, out, X_BLOCK[0]),
        ):
            copies.append(copy_of(*given))
            copies[-1].start()
        plain = copy_of(y_two, begin, BLOCK, out, X_BLOCK[1])
        if late:
            other = copy_of(over, begin, BLOCK, out, X_BLOCK[1])

            @pl.when(at_y == across_y - 1)
            def _():
                other.start()

            @pl.when(at_y != across_y - 1)
            def _():
                plain.start()
        else:
            plain.start()
        copies.append(plain)
    for copy in copies:
        copy.wait()


def crossed(sizes, over, up, down, one, two, sem):
    del over
    copies = []
    for n, (side, out) in enumerate(zip(side_of(place_of(sizes)[0]), (one, two))):
        low, high = (pltpu.make_async_copy(source.at[pl.ds(0, BLOCK)], out, sem.at[n]) for source in (up, down))

        @pl.when(side < 0)
        def _():
            low.start()

        @pl.when(side > 0)
        def _():
            high.start()

        copies.append(low)
    for copy in copies:
        copy.wait()


def hand_on(*_):
    pass


def settle(y_two, y_low, out):
    del y_two, y_low
    out[...] = jnp.zeros_like(out)


def blank(*_):
    pass


def own_of(aux):
    rows = aux[...]
    return *list_of(rows[POS_ROWS : POS_ROWS + LIST_ROWS]), turned(points_of(rows)[:, :ATOMS])


def y_atoms(side):
    mine, theirs = faces_of(side)
    k = iota((FACE, 1), 0)
    z = k & (DEPTH - 1)
    line = (k >> 3) * (SIDE * DEPTH) + z
    crossed = ((k >> 3) ^ 1) * (SIDE * DEPTH) + z
    return line + mine * DEPTH, crossed + theirs * DEPTH


def y_ahead(side, own_first, own_key, pos_t):
    my_atom, their_atom = y_atoms(side)
    left = onehot(own_first, my_atom.astype(F32))
    right = onehot(own_key, (their_atom + (4 + side) * ATOMS).astype(F32))
    pick = jnp.where(iota((FACE, ATOMS), 1) == my_atom, 1.0, 0.0).astype(BF16)
    return dot_nt(left, right), picked_rows(pick, pos_t)


def y_part(period, sizes, side, read, forward, mine_t, wave):
    _, at_y, _, across_y = place_of(sizes)
    _, theirs = faces_of(side)
    my_atom, their_atom = y_atoms(side)
    rows = aux_of(read, Y_AUX)
    first, key = list_of(rows[POS_ROWS : POS_ROWS + LIST_ROWS])
    left = onehot(key, (my_atom + (4 - side) * ATOMS).astype(F32))
    count = forward + dot_nt(left, onehot(first, their_atom.astype(F32)))
    lane = iota((ATOMS, FACE), 1)
    lane = ((lane >> 3) ^ 1) * (SIDE * DEPTH) + (lane & (DEPTH - 1)) + theirs * DEPTH
    pick = jnp.where(iota((ATOMS, FACE), 0) == lane, 1.0, 0.0).astype(BF16)
    points = points_of(dot(rows[:, :ATOMS].astype(BF16), pick))
    zi = (iota((FACE, 1), 0) & (DEPTH - 1)).astype(F32)
    zj = (iota((1, FACE), 1) & (DEPTH - 1)).astype(F32)
    dx = points[0:1] - mine_t[:, 0:1]
    dy = (points[1:2] + wrap(at_y, across_y, side, period)) - mine_t[:, 1:2]
    dz = (points[2:3] + z_shift(zi, zj)) - mine_t[:, 2:3]
    grid = hopping(dx, dy, dz, count)
    half = 2 * DEPTH
    block = jnp.concatenate([read((0, half)), read((half + AUX, half))], axis=0)
    return applied(grid, planes_of(wave, block))


def y_add(acc, side, part):
    mine, _ = faces_of(side)
    for a in range(4):
        for x in range(SIDE):
            at = pl.multiple_of(a * ATOMS + (x * SIDE + mine) * DEPTH, DEPTH)
            begin = a * FACE + x * DEPTH
            acc[pl.ds(at, DEPTH)] += part[begin : begin + DEPTH]


def ghost(theirs, y_sides, shape, axis):
    at = iota(shape, axis)
    part = jnp.where(at < FACE, 0, jnp.where(at < FACE + DEPTH, 1, 2))
    step = jnp.where(part == 0, 0, jnp.where(part == 1, y_sides[0], y_sides[1]))
    row = jnp.where(step > 0, 0, (SIDE - 1) * DEPTH)
    atom = theirs * FACE + jnp.where(part == 0, at, row + (at & (DEPTH - 1)))
    return atom, step, part


def first_half(periods, sizes, aux, message, acc_in, acc, forward_y, mine_y, forward_x, mine_x, wave):
    at_x, at_y, _, _ = place_of(sizes)
    y_sides = side_of(at_y)
    own_first, own_key, pos_t = own_of(aux)
    forward_y[...], mine_y[...] = y_ahead(y_sides[1], own_first, own_key, pos_t)
    for n, side in enumerate(side_of(at_x)):
        mine, theirs = faces_of(side)
        my_atom = iota((FACE, 1), 0) + mine * FACE
        their_atom, step, _ = ghost(theirs, y_sides, (WIDE, 1), 0)
        target = their_atom + ((side + 1) * 3 + step + 1) * ATOMS
        left = onehot(own_first, my_atom.astype(F32))
        forward_x[n] = dot_nt(left, onehot(own_key, target.astype(F32)))
        pick = jnp.where(iota((FACE, ATOMS), 1) == my_atom, 1.0, 0.0).astype(BF16)
        mine_x[n] = picked_rows(pick, pos_t)
    forward, mine_t = y_ahead(y_sides[0], own_first, own_key, pos_t)
    acc[...] = acc_in[...]
    part = y_part(periods[1], sizes, y_sides[0], reader_of(message), forward, mine_t, wave)
    y_add(acc, y_sides[0], part)


def second_half(periods, sizes, late, *refs):
    _, at_y, _, across_y = place_of(sizes)
    mine = at_y < across_y // 4 * 2
    if late:
        _, *refs = refs
        mine = jnp.logical_not(mine)

    @pl.when(mine)
    def _():
        finish(periods, sizes, late, *refs)


def finish(periods, sizes, late, y_two, other, *refs):
    beside, given = refs[:2], refs[2:4]
    acc_in, forward_y, mine_y, forward_x, mine_x = refs[4:9]
    out, acc, wave, one_wave, two_wave, result, x_messages, sem, x_sem = refs[9:]
    at_x, at_y, across_x, across_y = place_of(sizes)
    arrivals = []
    if late:
        x_messages = given[1], given[0]
    else:
        x_messages = x_messages.at[0], x_messages.at[1]
        arrivals = [
            pltpu.make_async_copy(source, target, x_sem.at[n])
            for n, (source, target) in enumerate(zip(given, x_messages[::-1]))
        ]
    for arrival in arrivals:
        arrival.start()
    acc[...] = acc_in[...]
    y_sides = side_of(at_y)
    x_sides = side_of(at_x)

    read = sum_of(reader_of(y_two), reader_of(other))
    added = y_part(periods[1], sizes, y_sides[1], read, forward_y[...], mine_y[...], wave)
    y_add(acc, y_sides[1], added)
    planes = [acc[a * ATOMS + FACE : a * ATOMS + 3 * FACE] for a in range(4)]
    result[FACE : 3 * FACE] = atoms_of(planes, wave)
    middle = pl.ds(FACE, 2 * FACE)
    copies = [pltpu.make_async_copy(result.at[middle], out.at[middle], sem.at[2])]
    copies[0].start()
    k = iota((FACE, 1), 0)
    zi = (k & (DEPTH - 1)).astype(F32)
    lane = iota((1, WIDE), 1)
    zj = (lane & (DEPTH - 1)).astype(F32)
    shifts = [wrap(at_y, across_y, y, periods[1]) for y in y_sides]
    shift_y = jnp.where(lane < FACE, 0.0, jnp.where(lane < FACE + DEPTH, *shifts))
    parts = []
    for arrival in arrivals:
        arrival.wait()
    for n, side in enumerate(x_sides):
        mine, theirs = faces_of(side)
        corner_at = jnp.where(theirs == 0, 0, AUX)
        aux_at = jnp.where(theirs == 0, DEPTH, 0)
        plain = reader_of(x_messages[n])

        def second(at, plain=plain, other=reader_of(beside[n])):
            return plain((X_BLOCK[1] + at[0], at[1])) + other(at)

        def first(at, plain=plain):
            return plain((X_BLOCK[0] + at[0], at[1]))

        my_atom = k + mine * FACE
        their_atom, _, part = ghost(theirs, y_sides, (WIDE, 1), 0)
        lane_atom, _, lane_part = ghost(theirs, y_sides, (ATOMS, WIDE), 1)
        left, right, picks, placed = [], [], [], []
        for m, y in enumerate((0, *y_sides)):
            rows = aux_of((plain, first, second)[m], aux_at if m else FACE)
            listed, key = list_of(rows[POS_ROWS : POS_ROWS + LIST_ROWS])
            wanted = my_atom + ((1 - side) * 3 + 1 - y) * ATOMS
            left.append(onehot(key, wanted.astype(F32)))
            right.append(onehot(listed, jnp.where(part == m, their_atom, -2).astype(F32)))
            pick = (iota((ATOMS, WIDE), 0) == lane_atom) & (lane_part == m)
            picks.append(jnp.where(pick, 1.0, 0.0).astype(BF16))
            placed.append(rows[:, :ATOMS].astype(BF16))
        count = forward_x[n] + dot_nt(
            jnp.concatenate(left, axis=1), jnp.concatenate(right, axis=1)
        )
        points = dot(jnp.concatenate(placed, axis=1), jnp.concatenate(picks, axis=0))
        points = points_of(points)
        mine_t = mine_x[n]
        dx = (points[0:1] + wrap(at_x, across_x, side, periods[0])) - mine_t[:, 0:1]
        dy = (points[1:2] + shift_y) - mine_t[:, 1:2]
        dz = (points[2:3] + z_shift(zi, zj)) - mine_t[:, 2:3]
        grid = hopping(dx, dy, dz, count)
        block = [plain((0, FACE)), first((corner_at, DEPTH)), second((corner_at, DEPTH))]
        planes = planes_of((one_wave, two_wave)[n], jnp.concatenate(block, axis=0))
        parts.append(applied(grid, planes))
    for n, side in enumerate(x_sides):
        mine, _ = faces_of(side)
        planes = []
        for a in range(4):
            at = pl.multiple_of(a * ATOMS + mine * FACE, FACE)
            planes.append(acc[pl.ds(at, FACE)] + parts[n][a * FACE : (a + 1) * FACE])
        face = pl.ds(mine * FACE, FACE)
        result[face] = atoms_of(planes, (one_wave, two_wave)[n])
        copies.append(pltpu.make_async_copy(result.at[face], out.at[face], sem.at[n]))
        copies[-1].start()
    for copy in copies:
        copy.wait()


def swap(count, begin):
    pairs = []
    for i in range(begin, count + begin, 2):
        a, b = i % count, (i + 1) % count
        pairs += [(a, b), (b, a)]
    return pairs


def exchange_x(one, two, rows):
    count, across_y = lax.axis_size("gx"), lax.axis_size("gy")

    def pairs(begin):
        return [
            (a * across_y + y, b * across_y + y) for y in rows for a, b in swap(count, begin)
        ]

    two = lax.ppermute(two, ("gx", "gy"), pairs(1))
    one = lax.ppermute(one, ("gx", "gy"), pairs(0))
    return two, one


def over_wrap(message, step):
    count, across_y = lax.axis_size("gx"), lax.axis_size("gy")
    pairs = [
        (x * across_y + across_y - 1, (x + step) % count * across_y) for x in range(count)
    ]
    return lax.ppermute(message, ("gx", "gy"), pairs)


VMEM = pl.BlockSpec(memory_space=pltpu.VMEM)
SMEM = pl.BlockSpec(memory_space=pltpu.SMEM)
HBM = pl.BlockSpec(memory_space=pltpu.HBM)
ANY = pl.BlockSpec(memory_space=pl.ANY)


def call(kernel, inputs, outputs, in_space=VMEM, out_space=VMEM, **options):
    return pl.pallas_call(
        kernel,
        out_shape=outputs,
        in_specs=in_space if isinstance(in_space, list) else [in_space] * len(inputs),
        out_specs=[out_space] * len(outputs),
        compiler_params=pltpu.CompilerParams(vmem_limit_bytes=16 * 1024 * 1024),
        **options,
    )(*inputs)


def shards(trial, positions, pair_atoms, pair_owner, pair_image, pair_count):
    sizes = across_x, across_y = lax.axis_size("gx"), lax.axis_size("gy")
    periods = tuple(LATTICE_STEP * (SIDE * count) for count in sizes)
    mine = trial.reshape(ATOMS, 4, NV)
    slots = pair_owner.shape[2]

    def message(sites):
        return jax.ShapeDtypeStruct((sites, 4, NV), BF16)

    def floats(*shape):
        return jax.ShapeDtypeStruct(shape, F32)

    def wave(rows):
        return pltpu.VMEM((2, rows, LANES), F32)

    low, two, top, over, back, over_up, over_down, aux = call(
        functools.partial(pack_y, sizes),
        tuple(
            pltpu.with_memory_space_constraint(array, pltpu.HBM)
            for array in (
                mine,
                positions.reshape(3 * SIDE * SIDE, DEPTH),
                pair_atoms.reshape(2, slots),
                pair_owner.reshape(1, slots),
            )
        )
        + (pair_count,),
        [message(Y_SITES)] * 5
        + [message(Y_SITES)] * 2
        + [floats(4 * AUX, NV)],
        in_space=[HBM] * 4 + [SMEM],
        scratch_shapes=[
            pltpu.VMEM((3 * SIDE * SIDE, DEPTH), F32),
            pltpu.VMEM((2, slots), jnp.int32),
            pltpu.VMEM((1, slots), jnp.int32),
            pltpu.SemaphoreType.DMA((3 + 5 * SIDE + 2,)),
        ],
    )
    half = across_y // 4 * 2
    pairs = swap(across_y, 0)
    early = lax.axis_index("gy") < half
    y_two = lax.ppermute(two, "gy", swap(across_y, 1)[:-2])
    y_low = lax.ppermute(low, "gy", pairs[:half])
    over_in = over_wrap(over, 0)
    over_up = over_wrap(over_up, 1)
    over_down = over_wrap(over_down, -1)
    (settled,) = call(settle, (y_two, y_low), [floats(8, LANES)], in_space=ANY)

    def x_messages(late, *given):
        return call(
            functools.partial(corners, sizes, late),
            given,
            [message(X_SITES)] * 2,
            in_space=ANY,
            out_space=ANY,
            scratch_shapes=[pltpu.SemaphoreType.DMA((8,))],
        )

    own_kinds = [
        floats(4 * ATOMS, NV),
        floats(FACE, FACE),
        floats(FACE, 8),
        floats(2, FACE, WIDE),
        floats(2, FACE, 8),
    ]

    def own_atoms(y_message):
        (acc,) = call(own, (mine, aux), [floats(4 * ATOMS, NV)], scratch_shapes=[wave(4 * ATOMS)])
        return call(
            functools.partial(first_half, periods, sizes),
            (aux, y_message, acc),
            own_kinds,
            scratch_shapes=[wave(4 * FACE)],
        )

    def nothing():
        kinds = [message(X_SITES)] * 2 + own_kinds
        return tuple(call(blank, (), kinds, out_space=ANY))

    def early_ones():
        messages = x_messages(False, settled, y_two, y_low, mine, low)
        return (*exchange_x(*messages, range(half)), *own_atoms(y_low))

    def late_ones():
        messages = x_messages(True, beside[0], back, y_top, y_two, mine, low)
        return (*exchange_x(*messages, range(half, across_y)), *own_atoms(y_top))

    from_early = lax.cond(early, early_ones, nothing)
    back, top = call(
        hand_on,
        (from_early[0], back, top),
        [message(Y_SITES)] * 2,
        in_space=ANY,
        out_space=ANY,
        input_output_aliases={1: 0, 2: 1},
    )
    back = lax.ppermute(back, "gy", [(0, across_y - 1)])
    (y_top,) = lax.cond(
        early,
        lambda: tuple(call(blank, (), [message(Y_SITES)], out_space=ANY)),
        lambda: (lax.ppermute(top, "gy", pairs[half:]),),
    )
    beside = call(
        functools.partial(crossed, sizes),
        (over_in, over_up, over_down),
        [message(BLOCK)] * 2,
        in_space=ANY,
        out_space=ANY,
        scratch_shapes=[pltpu.SemaphoreType.DMA((2,))],
    )
    def result(late, inputs, spaces, **options):
        (product,) = call(
            functools.partial(second_half, periods, sizes, late),
            inputs,
            [floats(ATOMS, 4, NV)],
            in_space=spaces + [VMEM] * 4 + [VMEM if late else ANY] * 2 + [VMEM] * 5,
            out_space=HBM,
            scratch_shapes=[
                pltpu.VMEM((4 * ATOMS, NV), F32),
                wave(2 * ATOMS),
                wave(4 * WIDE),
                wave(4 * WIDE),
                pltpu.VMEM((ATOMS, 4, NV), F32),
                pltpu.VMEM((2, X_SITES, 4, NV), BF16),
                pltpu.SemaphoreType.DMA((3,)),
                pltpu.SemaphoreType.DMA((2,)),
            ],
            **options,
        )
        return product

    product = result(False, (y_two, over_in, *beside, *from_early), [])
    from_late = lax.cond(early, nothing, late_ones)
    product = result(
        True,
        (product, y_two, back, *beside, *from_late),
        [HBM],
        input_output_aliases={0: 0},
    )
    return product.reshape(trial.shape)


def solution(mesh):
    in_specs = (
        P("gx", "gy", None, None, None),
        P(None, "gx", "gy", None),
        P("gx", "gy", None, None),
        P("gx", "gy", None),
        P("gx", "gy", None, None),
        P("gx", "gy"),
    )
    out_specs = P("gx", "gy", None, None, None)
    return jax.shard_map(shards, mesh=mesh, in_specs=in_specs, out_specs=out_specs, check_vma=False)
```

```python
import functools

import jax
import jax.numpy as jnp
from jax import lax
from jax.experimental import pallas as pl
from jax.experimental.pallas import tpu as pltpu
from jax.sharding import PartitionSpec as P

ONSITE_S = -0.22
ONSITE_P = 0.27
HOP_SS = -0.37
HOP_SP = 0.35
HOP_PPS = 0.4
HOP_PPP = -0.114
BOND_LENGTH = 1.536
LATTICE_STEP = 1.6

SIDE = 4
DEPTH = 8
ATOMS = SIDE * SIDE * DEPTH
FACE = SIDE * DEPTH
WIDE = FACE + 2 * DEPTH
NV = 256
LANES = NV // 2
POS_ROWS = 9
LIST_ROWS = 6
AUX = 4
Y_PLACE = (DEPTH, 0, 3 * DEPTH + AUX, 2 * DEPTH + AUX)
Y_AUX = 2 * DEPTH
Y_SITES = FACE + AUX
BLOCK = DEPTH + AUX
X_BLOCK = (FACE + AUX, FACE + AUX + BLOCK)
X_SITES = WIDE + 3 * AUX
STEPS = [(x, y) for x in (-1, 0, 1) for y in (-1, 0, 1)]
F32 = jnp.float32
BF16 = jnp.bfloat16


def iota(shape, axis):
    return lax.broadcasted_iota(jnp.int32, shape, axis)


def onehot(values, expected):
    wide = [jnp.where(row == expected, 1.0, 0.0).astype(BF16) for row in values]
    return wide[0] if len(wide) == 1 else jnp.concatenate(wide, axis=1)


def dot_nt(a, b):
    return lax.dot_general(a, b, (((1,), (1,)), ((), ())), preferred_element_type=F32)


def dot(a, b):
    return jnp.dot(a, b, preferred_element_type=F32)


def list_of(rows):
    first = [rows[k : k + 1] for k in range(2)]
    key = [rows[4 + k : 5 + k] * float(ATOMS) + rows[2 + k : 3 + k] for k in range(2)]
    return first, key


def code(step_x, step_y):
    return (step_x + 1) * 3 + step_y + 1


def hopping(dx, dy, dz, count):
    square = jnp.maximum(dx * dx + dy * dy + dz * dz, 0.5)
    inverse = lax.rsqrt(square)
    cosines = [d * inverse for d in (dx, dy, dz)]
    ratio = BOND_LENGTH * inverse
    radial = ratio * ratio * jnp.exp(1.0 - square * inverse * (1.0 / BOND_LENGTH))

    def final(value):
        return (value.astype(BF16).astype(F32) * count).astype(BF16)

    grid = [[None] * 4 for _ in range(4)]
    grid[0][0] = final(HOP_SS * radial)
    for a in range(3):
        across = final(HOP_SP * radial * cosines[a])
        grid[0][1 + a] = across
        grid[1 + a][0] = -across
        for b in range(a, 3):
            entry = (HOP_PPS - HOP_PPP) * cosines[a] * cosines[b]
            if a == b:
                entry = entry + HOP_PPP
            grid[1 + a][1 + b] = grid[1 + b][1 + a] = final(entry * radial)
    return grid


def planes_of(wave, block):
    n = block.shape[0]
    wide = block.astype(F32).reshape(n // 2, 2, 4, NV)
    wide = jnp.concatenate([wide[:, 0], wide[:, 1]], axis=1).reshape(4 * n, NV)
    for h in range(2):
        wave[h, : 4 * n] = wide[:, h * LANES : (h + 1) * LANES]
    halves = [[wave[h, pl.ds(b, n, stride=4), :] for h in range(2)] for b in range(4)]
    return [jnp.concatenate(pair, axis=1) for pair in halves]


def applied(grid, planes):
    total = None
    for b in range(4):
        stacked = jnp.concatenate([grid[a][b] for a in range(4)], axis=0)
        part = dot(stacked, planes[b].astype(BF16))
        total = part if total is None else total + part
    return total


def atoms_of(planes, wave):
    n = planes[0].shape[0]
    for a in range(4):
        for h in range(2):
            wave[h, pl.ds(a, n, stride=4), :] = planes[a][:, h * LANES : (h + 1) * LANES]
    wide = jnp.concatenate([wave[h, : 4 * n] for h in range(2)], axis=1)
    wide = wide.reshape(n // 2, 8, NV)
    return jnp.stack([wide[:, :4], wide[:, 4:]], axis=1).reshape(n, 4, NV)


def turned(points):
    n = points.shape[1]
    return jnp.concatenate([points, jnp.zeros((5, n), F32)], axis=0).T


def picked_rows(pick, points):
    total = None
    for _ in range(3):
        piece = points.astype(BF16)
        part = dot(pick, piece)
        total = part if total is None else total + part
        points = points - piece.astype(F32)
    return total


def z_shift(zi, zj):
    step = zj - zi
    period = LATTICE_STEP * DEPTH
    return jnp.where(step > 1.5, -period, jnp.where(step < -1.5, period, 0.0))


def wrap(place, across, side, period):
    high = jnp.where((side > 0) & (place == across - 1), period, 0.0)
    return jnp.where((side < 0) & (place == 0), -period, high)


def place_of(sizes):
    return lax.axis_index("gx"), lax.axis_index("gy"), *sizes


def side_of(place):
    first = 1 - 2 * (place & 1)
    return first, -first


def faces_of(side):
    mine = jnp.where(side > 0, SIDE - 1, 0)
    return mine, SIDE - 1 - mine


def sum_of(*readers):
    def read(at):
        total = None
        for reader in readers:
            value = reader(at)
            total = value if total is None else total + value
        return total

    return read


def reader_of(message, first=0):
    return lambda at: message[pl.ds(first + at[0], at[1])].astype(F32)


def aux_of(read, first):
    sites = read((first, AUX))
    return jnp.concatenate([sites[k] for k in range(AUX)], axis=0)


def points_of(rows):
    return rows[0:3] + rows[3:6] + rows[6:9]


def pack_y(sizes, trial, positions, atoms, owner, count, *refs):
    low, two, top, over, back, over_up, over_down, aux, pos, pairs, owners, sem = refs
    at_x, at_y, across_x, across_y = place_of(sizes)
    copies = [
        pltpu.make_async_copy(a, b, sem.at[k])
        for k, (a, b) in enumerate(((positions, pos), (atoms, pairs), (owner, owners)))
    ]
    faces = [faces_of(side)[0] for side in side_of(at_y)]
    moves = [
        (x, faces[n], out.at[pl.ds(begin + Y_PLACE[x], DEPTH)])
        for n, out, begin in (
            (0, low, 0),
            (1, two, 0),
            (0, top, 0),
            (1, over, 0),
            (1, back, 0),
        )
        for x in range(SIDE)
    ]
    moves.append((SIDE - 1, faces[1], over_up.at[pl.ds(AUX, DEPTH)]))
    moves.append((0, faces[1], over_down.at[pl.ds(0, DEPTH)]))
    for x, face, out in moves:
        begin = (x * SIDE + face) * DEPTH
        copies.append(
            pltpu.make_async_copy(trial.at[pl.ds(begin, DEPTH)], out, sem.at[len(copies)])
        )
    for copy in copies:
        copy.start()
    rows = 3 * SIDE * SIDE
    tile = (iota((DEPTH, ATOMS), 1) & (DEPTH - 1)) == iota((DEPTH, ATOMS), 0)
    tile = jnp.where(tile, 1.0, 0.0).astype(BF16)
    row = iota((3 * rows, ATOMS), 0)
    keep = (row & (SIDE * SIDE - 1)) == (iota((3 * rows, ATOMS), 1) >> 3)
    gather = (iota((16, 3 * rows), 1) >> 4) == iota((16, 3 * rows), 0)
    gather = jnp.where(gather, 1.0, 0.0).astype(BF16)
    aux[:, ATOMS:] = jnp.zeros((4 * AUX, NV - ATOMS), F32)
    for copy in copies[:3]:
        copy.wait()
    rest = pos[...]
    parts = []
    for _ in range(3):
        piece = rest.astype(BF16)
        parts.append(piece)
        rest = rest - piece.astype(F32)
    spread = dot(jnp.concatenate(parts, axis=0), tile)
    aux[:, :ATOMS] = dot(gather, jnp.where(keep, spread, 0.0).astype(BF16))
    whose = owners[...]
    step = jnp.zeros(whose.shape, F32)
    for x, y in STEPS:
        name = lax.rem(at_x + x + across_x, across_x) * across_y
        name = name + lax.rem(at_y + y + across_y, across_y)
        step = jnp.where(whose == name, float(code(x, y)), step)
    live = iota(whose.shape, 1) < count[0, 0]
    first = jnp.where(live, pairs[0:1], -1).astype(F32)
    second = pairs[1:2].astype(F32)
    for k, values in enumerate((first, second, step)):
        for h in range(2):
            at = POS_ROWS + 2 * k + h
            aux[at : at + 1] = values[:, h * NV : (h + 1) * NV]
    places = [(out, Y_AUX) for out in (low, two, top, over, back)]
    places += [(over_up, 0), (over_down, DEPTH)]
    for k in range(AUX):
        site = aux[4 * k : 4 * k + 4].astype(BF16)
        for out, at in places:
            out[at + k] = site
    for copy in copies[3:]:
        copy.wait()


def own(trial, aux, acc, wave):
    rows = aux[...]
    first, key = list_of(rows[POS_ROWS : POS_ROWS + LIST_ROWS])
    atom = iota((ATOMS, 1), 0)
    is_first = onehot(first, atom.astype(F32))
    is_second = onehot(key, (atom + code(0, 0) * ATOMS).astype(F32))
    count = dot_nt(is_first, is_second) + dot_nt(is_second, is_first)
    pos = points_of(rows)[:, :ATOMS]
    pos_t = turned(pos)
    zi = (atom & (DEPTH - 1)).astype(F32)
    zj = (iota((1, ATOMS), 1) & (DEPTH - 1)).astype(F32)
    dx, dy = (pos[a : a + 1] - pos_t[:, a : a + 1] for a in range(2))
    dz = (pos[2:3] + z_shift(zi, zj)) - pos_t[:, 2:3]
    grid = hopping(dx, dy, dz, count)
    planes = planes_of(wave, trial[...])
    matrix = jnp.concatenate([jnp.concatenate(line, axis=1) for line in grid], axis=0)
    part = dot(matrix, jnp.concatenate(planes, axis=0).astype(BF16))
    for a in range(4):
        onsite = ONSITE_P if a else ONSITE_S
        rows = slice(a * ATOMS, (a + 1) * ATOMS)
        acc[rows] = onsite * planes[a] + part[rows]


def corners(sizes, late, *refs):
    _, *inputs, one, two, sem = refs
    if late:
        over, y_one, y_two, trial, message = inputs
    else:
        y_two, y_one, trial, message = inputs
    at_x, at_y, _, across_y = place_of(sizes)
    copies = []

    def copy_of(source, begin, count, out, at):
        return pltpu.make_async_copy(
            source.at[pl.ds(begin, count)], out.at[pl.ds(at, count)], sem.at[len(copies)]
        )

    for side, out in zip(side_of(at_x), (one, two)):
        face, _ = faces_of(side)
        begin = jnp.where(face == 0, Y_PLACE[0], Y_AUX)
        for given in (
            (trial, face * FACE, FACE, out, 0),
            (message, Y_AUX, AUX, out, FACE),
            (y_one, begin, BLOCK, out, X_BLOCK[0]),
        ):
            copies.append(copy_of(*given))
            copies[-1].start()
        plain = copy_of(y_two, begin, BLOCK, out, X_BLOCK[1])
        if late:
            other = copy_of(over, begin, BLOCK, out, X_BLOCK[1])

            @pl.when(at_y == across_y - 1)
            def _():
                other.start()

            @pl.when(at_y != across_y - 1)
            def _():
                plain.start()
        else:
            plain.start()
        copies.append(plain)
    for copy in copies:
        copy.wait()


def hand_on(*_):
    pass


def settle(y_two, y_low, out):
    del y_two, y_low
    out[...] = jnp.zeros_like(out)


def blank(*_):
    pass


def own_of(aux):
    rows = aux[...]
    return *list_of(rows[POS_ROWS : POS_ROWS + LIST_ROWS]), turned(points_of(rows)[:, :ATOMS])


def y_atoms(side):
    mine, theirs = faces_of(side)
    k = iota((FACE, 1), 0)
    z = k & (DEPTH - 1)
    line = (k >> 3) * (SIDE * DEPTH) + z
    crossed = ((k >> 3) ^ 1) * (SIDE * DEPTH) + z
    return line + mine * DEPTH, crossed + theirs * DEPTH


def y_ahead(side, own_first, own_key, pos_t):
    my_atom, their_atom = y_atoms(side)
    left = onehot(own_first, my_atom.astype(F32))
    right = onehot(own_key, (their_atom + (4 + side) * ATOMS).astype(F32))
    pick = jnp.where(iota((FACE, ATOMS), 1) == my_atom, 1.0, 0.0).astype(BF16)
    return dot_nt(left, right), picked_rows(pick, pos_t)


def y_part(period, sizes, side, read, forward, mine_t, wave):
    _, at_y, _, across_y = place_of(sizes)
    _, theirs = faces_of(side)
    my_atom, their_atom = y_atoms(side)
    rows = aux_of(read, Y_AUX)
    first, key = list_of(rows[POS_ROWS : POS_ROWS + LIST_ROWS])
    left = onehot(key, (my_atom + (4 - side) * ATOMS).astype(F32))
    count = forward + dot_nt(left, onehot(first, their_atom.astype(F32)))
    lane = iota((ATOMS, FACE), 1)
    lane = ((lane >> 3) ^ 1) * (SIDE * DEPTH) + (lane & (DEPTH - 1)) + theirs * DEPTH
    pick = jnp.where(iota((ATOMS, FACE), 0) == lane, 1.0, 0.0).astype(BF16)
    points = points_of(dot(rows[:, :ATOMS].astype(BF16), pick))
    zi = (iota((FACE, 1), 0) & (DEPTH - 1)).astype(F32)
    zj = (iota((1, FACE), 1) & (DEPTH - 1)).astype(F32)
    dx = points[0:1] - mine_t[:, 0:1]
    dy = (points[1:2] + wrap(at_y, across_y, side, period)) - mine_t[:, 1:2]
    dz = (points[2:3] + z_shift(zi, zj)) - mine_t[:, 2:3]
    grid = hopping(dx, dy, dz, count)
    half = 2 * DEPTH
    block = jnp.concatenate([read((0, half)), read((half + AUX, half))], axis=0)
    return applied(grid, planes_of(wave, block))


def y_add(acc, side, part):
    mine, _ = faces_of(side)
    for a in range(4):
        for x in range(SIDE):
            at = pl.multiple_of(a * ATOMS + (x * SIDE + mine) * DEPTH, DEPTH)
            begin = a * FACE + x * DEPTH
            acc[pl.ds(at, DEPTH)] += part[begin : begin + DEPTH]


def ghost(theirs, y_sides, shape, axis):
    at = iota(shape, axis)
    part = jnp.where(at < FACE, 0, jnp.where(at < FACE + DEPTH, 1, 2))
    step = jnp.where(part == 0, 0, jnp.where(part == 1, y_sides[0], y_sides[1]))
    row = jnp.where(step > 0, 0, (SIDE - 1) * DEPTH)
    atom = theirs * FACE + jnp.where(part == 0, at, row + (at & (DEPTH - 1)))
    return atom, step, part


def first_half(periods, sizes, aux, message, acc_in, acc, forward_y, mine_y, forward_x, mine_x, wave):
    at_x, at_y, _, _ = place_of(sizes)
    y_sides = side_of(at_y)
    own_first, own_key, pos_t = own_of(aux)
    forward_y[...], mine_y[...] = y_ahead(y_sides[1], own_first, own_key, pos_t)
    for n, side in enumerate(side_of(at_x)):
        mine, theirs = faces_of(side)
        my_atom = iota((FACE, 1), 0) + mine * FACE
        their_atom, step, _ = ghost(theirs, y_sides, (WIDE, 1), 0)
        target = their_atom + ((side + 1) * 3 + step + 1) * ATOMS
        left = onehot(own_first, my_atom.astype(F32))
        forward_x[n] = dot_nt(left, onehot(own_key, target.astype(F32)))
        pick = jnp.where(iota((FACE, ATOMS), 1) == my_atom, 1.0, 0.0).astype(BF16)
        mine_x[n] = picked_rows(pick, pos_t)
    forward, mine_t = y_ahead(y_sides[0], own_first, own_key, pos_t)
    acc[...] = acc_in[...]
    part = y_part(periods[1], sizes, y_sides[0], reader_of(message), forward, mine_t, wave)
    y_add(acc, y_sides[0], part)


def second_half(periods, sizes, late, *refs):
    _, at_y, _, across_y = place_of(sizes)
    mine = at_y < across_y // 4 * 2
    if late:
        _, *refs = refs
        mine = jnp.logical_not(mine)

    @pl.when(mine)
    def _():
        finish(periods, sizes, late, *refs)


def finish(periods, sizes, late, y_two, other, *refs):
    beside, given = refs[:2], refs[2:4]
    acc_in, forward_y, mine_y, forward_x, mine_x = refs[4:9]
    out, acc, wave, one_wave, two_wave, result, x_messages, sem, x_sem = refs[9:]
    at_x, at_y, across_x, across_y = place_of(sizes)
    arrivals = []
    if late:
        x_messages = given[1], given[0]
    else:
        x_messages = x_messages.at[0], x_messages.at[1]
        arrivals = [
            pltpu.make_async_copy(source, target, x_sem.at[n])
            for n, (source, target) in enumerate(zip(given, x_messages[::-1]))
        ]
    for arrival in arrivals:
        arrival.start()
    acc[...] = acc_in[...]
    y_sides = side_of(at_y)
    x_sides = side_of(at_x)

    read = sum_of(reader_of(y_two), reader_of(other))
    added = y_part(periods[1], sizes, y_sides[1], read, forward_y[...], mine_y[...], wave)
    k = iota((FACE, 1), 0)
    zi = (k & (DEPTH - 1)).astype(F32)
    lane = iota((1, WIDE), 1)
    zj = (lane & (DEPTH - 1)).astype(F32)
    shifts = [wrap(at_y, across_y, y, periods[1]) for y in y_sides]
    shift_y = jnp.where(lane < FACE, 0.0, jnp.where(lane < FACE + DEPTH, *shifts))
    parts = []
    for arrival in arrivals:
        arrival.wait()
    for n, side in enumerate(x_sides):
        mine, theirs = faces_of(side)
        corner_at = jnp.where(theirs == 0, 0, AUX)
        aux_at = jnp.where(theirs == 0, DEPTH, 0)
        plain = reader_of(x_messages[n])

        def second(at, plain=plain, side=side):
            up, down = (reader_of(message)(at) for message in beside)
            return plain((X_BLOCK[1] + at[0], at[1])) + jnp.where(side < 0, up, down)

        def first(at, plain=plain):
            return plain((X_BLOCK[0] + at[0], at[1]))

        my_atom = k + mine * FACE
        their_atom, _, part = ghost(theirs, y_sides, (WIDE, 1), 0)
        lane_atom, _, lane_part = ghost(theirs, y_sides, (ATOMS, WIDE), 1)
        left, right, picks, placed = [], [], [], []
        for m, y in enumerate((0, *y_sides)):
            rows = aux_of((plain, first, second)[m], aux_at if m else FACE)
            listed, key = list_of(rows[POS_ROWS : POS_ROWS + LIST_ROWS])
            wanted = my_atom + ((1 - side) * 3 + 1 - y) * ATOMS
            left.append(onehot(key, wanted.astype(F32)))
            right.append(onehot(listed, jnp.where(part == m, their_atom, -2).astype(F32)))
            pick = (iota((ATOMS, WIDE), 0) == lane_atom) & (lane_part == m)
            picks.append(jnp.where(pick, 1.0, 0.0).astype(BF16))
            placed.append(rows[:, :ATOMS].astype(BF16))
        count = forward_x[n] + dot_nt(
            jnp.concatenate(left, axis=1), jnp.concatenate(right, axis=1)
        )
        points = dot(jnp.concatenate(placed, axis=1), jnp.concatenate(picks, axis=0))
        points = points_of(points)
        mine_t = mine_x[n]
        dx = (points[0:1] + wrap(at_x, across_x, side, periods[0])) - mine_t[:, 0:1]
        dy = (points[1:2] + shift_y) - mine_t[:, 1:2]
        dz = (points[2:3] + z_shift(zi, zj)) - mine_t[:, 2:3]
        grid = hopping(dx, dy, dz, count)
        block = [plain((0, FACE)), first((corner_at, DEPTH)), second((corner_at, DEPTH))]
        planes = planes_of((one_wave, two_wave)[n], jnp.concatenate(block, axis=0))
        parts.append(applied(grid, planes))
    y_add(acc, y_sides[1], added)
    planes = [acc[a * ATOMS + FACE : a * ATOMS + 3 * FACE] for a in range(4)]
    result[FACE : 3 * FACE] = atoms_of(planes, wave)
    middle = pl.ds(FACE, 2 * FACE)
    copies = [pltpu.make_async_copy(result.at[middle], out.at[middle], sem.at[2])]
    copies[0].start()
    for n, side in enumerate(x_sides):
        mine, _ = faces_of(side)
        planes = []
        for a in range(4):
            at = pl.multiple_of(a * ATOMS + mine * FACE, FACE)
            planes.append(acc[pl.ds(at, FACE)] + parts[n][a * FACE : (a + 1) * FACE])
        face = pl.ds(mine * FACE, FACE)
        result[face] = atoms_of(planes, (one_wave, two_wave)[n])
        copies.append(pltpu.make_async_copy(result.at[face], out.at[face], sem.at[n]))
        copies[-1].start()
    for copy in copies:
        copy.wait()


def swap(count, begin):
    pairs = []
    for i in range(begin, count + begin, 2):
        a, b = i % count, (i + 1) % count
        pairs += [(a, b), (b, a)]
    return pairs


def exchange_x(one, two, rows):
    count, across_y = lax.axis_size("gx"), lax.axis_size("gy")

    def pairs(begin):
        return [
            (a * across_y + y, b * across_y + y) for y in rows for a, b in swap(count, begin)
        ]

    two = lax.ppermute(two, ("gx", "gy"), pairs(1))
    one = lax.ppermute(one, ("gx", "gy"), pairs(0))
    return two, one


def over_wrap(message, step):
    count, across_y = lax.axis_size("gx"), lax.axis_size("gy")
    pairs = [
        (x * across_y + across_y - 1, (x + step) % count * across_y) for x in range(count)
    ]
    return lax.ppermute(message, ("gx", "gy"), pairs)


VMEM = pl.BlockSpec(memory_space=pltpu.VMEM)
SMEM = pl.BlockSpec(memory_space=pltpu.SMEM)
HBM = pl.BlockSpec(memory_space=pltpu.HBM)
ANY = pl.BlockSpec(memory_space=pl.ANY)


def call(kernel, inputs, outputs, in_space=VMEM, out_space=VMEM, **options):
    return pl.pallas_call(
        kernel,
        out_shape=outputs,
        in_specs=in_space if isinstance(in_space, list) else [in_space] * len(inputs),
        out_specs=[out_space] * len(outputs),
        compiler_params=pltpu.CompilerParams(vmem_limit_bytes=16 * 1024 * 1024),
        **options,
    )(*inputs)


def shards(trial, positions, pair_atoms, pair_owner, pair_image, pair_count):
    sizes = across_x, across_y = lax.axis_size("gx"), lax.axis_size("gy")
    periods = tuple(LATTICE_STEP * (SIDE * count) for count in sizes)
    mine = trial.reshape(ATOMS, 4, NV)
    slots = pair_owner.shape[2]

    def message(sites):
        return jax.ShapeDtypeStruct((sites, 4, NV), BF16)

    def floats(*shape):
        return jax.ShapeDtypeStruct(shape, F32)

    def wave(rows):
        return pltpu.VMEM((2, rows, LANES), F32)

    low, two, top, over, back, over_up, over_down, aux = call(
        functools.partial(pack_y, sizes),
        tuple(
            pltpu.with_memory_space_constraint(array, pltpu.HBM)
            for array in (
                mine,
                positions.reshape(3 * SIDE * SIDE, DEPTH),
                pair_atoms.reshape(2, slots),
                pair_owner.reshape(1, slots),
            )
        )
        + (pair_count,),
        [message(Y_SITES)] * 5
        + [message(Y_SITES)] * 2
        + [floats(4 * AUX, NV)],
        in_space=[HBM] * 4 + [SMEM],
        scratch_shapes=[
            pltpu.VMEM((3 * SIDE * SIDE, DEPTH), F32),
            pltpu.VMEM((2, slots), jnp.int32),
            pltpu.VMEM((1, slots), jnp.int32),
            pltpu.SemaphoreType.DMA((3 + 5 * SIDE + 2,)),
        ],
    )
    half = across_y // 4 * 2
    pairs = swap(across_y, 0)
    early = lax.axis_index("gy") < half
    y_two = lax.ppermute(two, "gy", swap(across_y, 1)[:-2])
    y_low = lax.ppermute(low, "gy", pairs[:half])
    over_in = over_wrap(over, 0)
    over_up = over_wrap(over_up, 1)
    over_down = over_wrap(over_down, -1)
    (settled,) = call(settle, (y_two, y_low), [floats(8, LANES)], in_space=ANY)

    def x_messages(late, *given):
        return call(
            functools.partial(corners, sizes, late),
            given,
            [message(X_SITES)] * 2,
            in_space=ANY,
            out_space=ANY,
            scratch_shapes=[pltpu.SemaphoreType.DMA((8,))],
        )

    own_kinds = [
        floats(4 * ATOMS, NV),
        floats(FACE, FACE),
        floats(FACE, 8),
        floats(2, FACE, WIDE),
        floats(2, FACE, 8),
    ]

    def own_atoms(y_message):
        (acc,) = call(own, (mine, aux), [floats(4 * ATOMS, NV)], scratch_shapes=[wave(4 * ATOMS)])
        return call(
            functools.partial(first_half, periods, sizes),
            (aux, y_message, acc),
            own_kinds,
            scratch_shapes=[wave(4 * FACE)],
        )

    def nothing():
        kinds = [message(X_SITES)] * 2 + own_kinds
        return tuple(call(blank, (), kinds, out_space=ANY))

    def early_ones():
        messages = x_messages(False, settled, y_two, y_low, mine, low)
        return (*exchange_x(*messages, range(half)), *own_atoms(y_low))

    def late_ones():
        messages = x_messages(True, product, back, y_top, y_two, mine, low)
        return (*exchange_x(*messages, range(half, across_y)), *own_atoms(y_top))

    from_early = lax.cond(early, early_ones, nothing)
    back, top = call(
        hand_on,
        (from_early[0], back, top),
        [message(Y_SITES)] * 2,
        in_space=ANY,
        out_space=ANY,
        input_output_aliases={1: 0, 2: 1},
    )
    back = lax.ppermute(back, "gy", [(0, across_y - 1)])
    (y_top,) = lax.cond(
        early,
        lambda: tuple(call(blank, (), [message(Y_SITES)], out_space=ANY)),
        lambda: (lax.ppermute(top, "gy", pairs[half:]),),
    )
    def result(late, inputs, spaces, **options):
        (product,) = call(
            functools.partial(second_half, periods, sizes, late),
            inputs,
            [floats(ATOMS, 4, NV)],
            in_space=spaces + [VMEM] * 4 + [VMEM if late else ANY] * 2 + [VMEM] * 5,
            out_space=HBM,
            scratch_shapes=[
                pltpu.VMEM((4 * ATOMS, NV), F32),
                wave(2 * ATOMS),
                wave(4 * WIDE),
                wave(4 * WIDE),
                pltpu.VMEM((ATOMS, 4, NV), F32),
                pltpu.VMEM((2, X_SITES, 4, NV), BF16),
                pltpu.SemaphoreType.DMA((3,)),
                pltpu.SemaphoreType.DMA((2,)),
            ],
            **options,
        )
        return product

    product = result(False, (y_two, over_in, over_up, over_down, *from_early), [])
    from_late = lax.cond(early, nothing, late_ones)
    product = result(
        True,
        (product, y_two, back, over_up, over_down, *from_late),
        [HBM],
        input_output_aliases={0: 0},
    )
    return product.reshape(trial.shape)


def solution(mesh):
    in_specs = (
        P("gx", "gy", None, None, None),
        P(None, "gx", "gy", None),
        P("gx", "gy", None, None),
        P("gx", "gy", None),
        P("gx", "gy", None, None),
        P("gx", "gy"),
    )
    out_specs = P("gx", "gy", None, None, None)
    return jax.shard_map(shards, mesh=mesh, in_specs=in_specs, out_specs=out_specs, check_vma=False)
```
